32 devices in a mesh: dp: 8 (over z, y), mp: 4 (over x, core).
Axes of the slice: x: 2, y: 2, z: 4, core: 2. Of those that a mesh axis runs over, the one named last changes fastest.
Arguments:
- targets: bfloat16 [8, 256, 1024], P('dp'), may hold values from -6 to 6
- labels: int32 [8, 256], replicated, may hold values from 0 to 50175
- passages: bfloat16 [16, 256, 1024], P('dp'), may hold values from -6 to 6
- slot_question: int32 [32], replicated, may hold values from 0 to 7, as said below
- slot_passage: int32 [32], P('dp'), may hold values from 0 to 1, as said below
- score_table: float32 [64], replicated, may hold values from -4 to 4
- score_index: int32 [32], replicated, may hold values from 0 to 63
- query_weight: bfloat16 [1024, 1024], P(None, 'mp'), may hold values from -0.1875 to 0.1875
- query_bias: bfloat16 [1024], P('mp'), may hold values from -1.1953125 to 1.1953125
- key_weight: bfloat16 [1024, 1024], P(None, 'mp'), may hold values from -0.1875 to 0.1875
- value_weight: bfloat16 [1024, 1024], P(None, 'mp'), may hold values from -0.1875 to 0.1875
- value_bias: bfloat16 [1024], P('mp'), may hold values from -1.1953125 to 1.1953125
- output_weight: bfloat16 [1024, 1024], P('mp'), may hold values from -0.75 to 0.75
- output_bias: bfloat16 [1024], replicated, may hold values from -1.1953125 to 1.1953125
- first_gain: bfloat16 [1024], replicated, may hold values from 0.5 to 1.5
- first_shift: bfloat16 [1024], replicated, may hold values from -1.1953125 to 1.1953125
- probe_weight: bfloat16 [1024, 1024], P(None, 'mp'), may hold values from -0.1875 to 0.1875
- probe_bias: bfloat16 [1024], P('mp'), may hold values from -1.1953125 to 1.1953125
- address_weight: bfloat16 [1024, 1024], P(None, 'mp'), may hold values from -0.1875 to 0.1875
- content_weight: bfloat16 [1024, 1024], P(None, 'mp'), may hold values from -0.1875 to 0.1875
- content_bias: bfloat16 [1024], P('mp'), may hold values from -1.1953125 to 1.1953125
- merged_weight: bfloat16 [1024, 1024], P('mp'), may hold values from -0.75 to 0.75
- merged_bias: bfloat16 [1024], replicated, may hold values from -1.1953125 to 1.1953125
- second_gain: bfloat16 [1024], replicated, may hold values from 0.5 to 1.5
- second_shift: bfloat16 [1024], replicated, may hold values from -1.1953125 to 1.1953125
- expand_weight: bfloat16 [1024, 4096], P(None, 'mp'), may hold values from -0.1875 to 0.1875
- expand_bias: bfloat16 [4096], P('mp'), may hold values from -1.1953125 to 1.1953125
- shrink_weight: bfloat16 [4096, 1024], P('mp'), may hold values from -0.09375 to 0.09375
- shrink_bias: bfloat16 [1024], replicated, may hold values from -1.1953125 to 1.1953125
- third_gain: bfloat16 [1024], replicated, may hold values from 0.5 to 1.5
- third_shift: bfloat16 [1024], replicated, may hold values from -1.1953125 to 1.1953125
- embedding: bfloat16 [50176, 1024], P('mp'), may hold values from -0.375 to 0.375
Outputs:
- objective: float32 [], replicated
- targets_slope: float32 [8, 256, 1024], P('dp')
- passages_slope: float32 [16, 256, 1024], P('dp')
- query_slope: float32 [1024, 1024], P('dp', 'mp')
- bias_query: float32 [1024], P(('mp', 'dp'))
- key_slope: float32 [1024, 1024], P('dp', 'mp')
- value_slope: float32 [1024, 1024], P('dp', 'mp')
- bias_value: float32 [1024], P(('mp', 'dp'))
- output_slope: float32 [1024, 1024], P('mp', 'dp')
- bias_output: float32 [1024], P('dp')
- first_gain_slope: float32 [1024], P('dp')
- first_shift_slope: float32 [1024], P('dp')
- probe_slope: float32 [1024, 1024], P('dp', 'mp')
- bias_probe: float32 [1024], P(('mp', 'dp'))
- address_slope: float32 [1024, 1024], P('dp', 'mp')
- content_slope: float32 [1024, 1024], P('dp', 'mp')
- bias_content: float32 [1024], P(('mp', 'dp'))
- merged_slope: float32 [1024, 1024], P('mp', 'dp')
- bias_merged: float32 [1024], P('dp')
- second_gain_slope: float32 [1024], P('dp')
- second_shift_slope: float32 [1024], P('dp')
- expand_slope: float32 [1024, 4096], P('dp', 'mp')
- bias_expand: float32 [4096], P(('mp', 'dp'))
- shrink_slope: float32 [4096, 1024], P('mp', 'dp')
- bias_shrink: float32 [1024], P('dp')
- third_gain_slope: float32 [1024], P('dp')
- third_shift_slope: float32 [1024], P('dp')
- embedding_slope: float32 [50176, 1024], P('mp', 'dp')
The draws below stay inside these ranges and needn't reach their ends.
Inputs may be any that keep to these rules, and one draw needn't show every extreme that they name: `slot_question`: each question is named by exactly 4 slots. `slot_passage`: among the 4 slots of one dp index (aligned blocks), every one of that index's 2 passages is named at least once.
All inputs are finite; a program needn't handle non-finite values.
Results may differ from the reference program's by a relative error of at most 0.03.
Values may be sent and summed in bfloat16 or wider, within the bound.
No kernel may reach another device: no remote copies, remote signals or barrier semaphores. Data moves between devices by JAX's collectives and lax.ppermute only.
A program may use at most 320 MiB of HBM per device.

```python
import math
import jax
import jax.numpy as jnp
import numpy as np
from jax import lax

D = 1024
HEADS = 16
HD = 64
FF = 4096
VOCAB = 50176
LEN = 256
PLEN = 256
SLOTS = 4
TABLE = 64
PAIRS_DEV = 4
PASS_DEV = 2
QUESTIONS = 8
PASSAGES = 16


def draw_slot_question(key, part):
    key = jax.random.fold_in(key, 5)
    owners = jnp.repeat(jnp.arange(QUESTIONS, dtype=jnp.int32), SLOTS)
    return jax.random.permutation(key, owners).astype(jnp.int32)


def draw_slot_passage(key, part):
    key = jax.random.fold_in(key, 9)
    blocks = QUESTIONS * SLOTS // PAIRS_DEV
    position = jnp.arange(PAIRS_DEV, dtype=jnp.int32)[None, :]
    filler = jax.random.randint(key, (blocks, PAIRS_DEV), 0, PASS_DEV).astype(jnp.int32)
    sectioned = jnp.where(position < PASS_DEV, position, filler)
    shuffle_keys = jax.random.split(jax.random.fold_in(key, 1), blocks)
    shuffled = jax.vmap(jax.random.permutation)(shuffle_keys, sectioned)
    return shuffled.reshape(-1).astype(jnp.int32)


def place_ends(drawn, rng, low, top_value):
    dims = drawn.shape
    spot = [jax.random.randint(jax.random.fold_in(rng, axis), (), 0, dims[axis]) for axis in range(len(dims))]
    drawn = drawn.at[tuple(spot)].set(low)
    longest = dims.index(max(dims))
    spot[longest] = (spot[longest] + 1) % dims[longest]
    return drawn.at[tuple(spot)].set(top_value)


def block_scale(rng, extent, pieces, low, top_value):
    level = 1.0
    for dim, parts in pieces:
        heights = jax.random.uniform(jax.random.fold_in(jax.random.fold_in(rng, 6), dim), (parts,), jnp.float32, low / len(pieces), top_value / len(pieces))
        level = level * jnp.repeat(jnp.exp(heights), extent[dim] // parts).reshape((-1,) + (1,) * (len(extent) - 1 - dim))
    return level


def rank_bounds(count, slope):
    portions = [(1 << 20) // math.isqrt(rank ** slope) + 1 for rank in range(1, count + 1)]
    deviation = 1 + sum(portions) // (1 << 30)
    return np.cumsum(np.array([max(1, weight // deviation) for weight in portions]))


def ranked(rng, dims, amount, slope):
    grid = rank_bounds(amount, slope)
    lot = jax.random.randint(jax.random.fold_in(rng, 1), dims, 0, int(grid[amount - 1]))
    rank = jnp.searchsorted(jnp.asarray(grid, jnp.int32), lot, side="right")
    return jax.random.permutation(jax.random.fold_in(rng, 2), amount)[rank].astype(jnp.int32)


def bell_draw(rng, shape, width, bound, shards=(), held_as=jnp.bfloat16):
    loudness = block_scale(rng, shape, shards, -0.22, 0.18) if shards else 1.0
    entries = jax.random.normal(rng, shape, jnp.float32) * width * loudness
    return jnp.minimum(jnp.maximum(entries, -bound), bound).astype(held_as)


def setup_inputs(seed: int = 0) -> dict:
    keys = jax.random.split(jax.random.key(seed), 33)
    return {
        "targets": bell_draw(keys[0], (QUESTIONS, LEN, D), 1.0, 6.0, ((0, 8),)),
        "labels": place_ends(ranked(keys[1], (QUESTIONS, LEN), VOCAB, 2), jax.random.fold_in(keys[1], 3), 0, VOCAB - 1).astype(jnp.int32),
        "passages": bell_draw(keys[2], (PASSAGES, PLEN, D), 1.0, 6.0, ((0, 8),)),
        "slot_question": draw_slot_question(jax.random.fold_in(keys[32], 71), 0),
        "slot_passage": draw_slot_passage(jax.random.fold_in(keys[32], 71), 0),
        "score_table": bell_draw(keys[5], (TABLE,), 1.0, 4.0, (), jnp.float32),
        "score_index": place_ends(jax.random.randint(keys[6], (QUESTIONS * SLOTS,), 0, TABLE), jax.random.fold_in(keys[6], 1), 0, TABLE - 1).astype(jnp.int32),
        "query_weight": bell_draw(keys[7], (D, D), D ** -0.5, 0.1875, ((1, 4),)),
        "query_bias": bell_draw(keys[8], (D,), 0.2, 1.1953125, ((0, 4),)),
        "key_weight": bell_draw(keys[9], (D, D), D ** -0.5, 0.1875, ((1, 4),)),
        "value_weight": bell_draw(keys[10], (D, D), D ** -0.5, 0.1875, ((1, 4),)),
        "value_bias": bell_draw(keys[11], (D,), 0.2, 1.1953125, ((0, 4),)),
        "output_weight": bell_draw(keys[12], (D, D), (D // 16) ** -0.5, 0.75, ((0, 4),)),
        "output_bias": bell_draw(keys[13], (D,), 0.2, 1.1953125),
        "first_gain": jnp.clip(1.0 + 0.1 * jax.random.normal(keys[14], (D,), jnp.float32), 0.5, 1.5).astype(jnp.bfloat16),
        "first_shift": bell_draw(keys[15], (D,), 0.2, 1.1953125),
        "probe_weight": bell_draw(keys[16], (D, D), D ** -0.5, 0.1875, ((1, 4),)),
        "probe_bias": bell_draw(keys[17], (D,), 0.2, 1.1953125, ((0, 4),)),
        "address_weight": bell_draw(keys[18], (D, D), D ** -0.5, 0.1875, ((1, 4),)),
        "content_weight": bell_draw(keys[19], (D, D), D ** -0.5, 0.1875, ((1, 4),)),
        "content_bias": bell_draw(keys[20], (D,), 0.2, 1.1953125, ((0, 4),)),
        "merged_weight": bell_draw(keys[21], (D, D), (D // 16) ** -0.5, 0.75, ((0, 4),)),
        "merged_bias": bell_draw(keys[22], (D,), 0.2, 1.1953125),
        "second_gain": jnp.clip(1.0 + 0.1 * jax.random.normal(keys[23], (D,), jnp.float32), 0.5, 1.5).astype(jnp.bfloat16),
        "second_shift": bell_draw(keys[24], (D,), 0.2, 1.1953125),
        "expand_weight": bell_draw(keys[25], (D, FF), D ** -0.5, 0.1875, ((1, 4),)),
        "expand_bias": bell_draw(keys[26], (FF,), 0.2, 1.1953125, ((0, 4),)),
        "shrink_weight": bell_draw(keys[27], (FF, D), FF ** -0.5, 0.09375, ((0, 4),)),
        "shrink_bias": bell_draw(keys[28], (D,), 0.2, 1.1953125),
        "third_gain": jnp.clip(1.0 + 0.1 * jax.random.normal(keys[29], (D,), jnp.float32), 0.5, 1.5).astype(jnp.bfloat16),
        "third_shift": bell_draw(keys[30], (D,), 0.2, 1.1953125),
        "embedding": bell_draw(keys[31], (VOCAB, D), (D // 4) ** -0.5, 0.375, ((0, 4),)),
    }


HIGHEST = lax.Precision.HIGHEST
EPSILON = 1e-05
ENTROPY_WEIGHT = 0.5

@jax.custom_vjp
def low(v):
    return lax.optimization_barrier(v.astype(jnp.bfloat16)).astype(jnp.float32)

@jax.custom_vjp
def low_back(v):
    return v

def low_keep(v):
    return (low(v), None)

def low_pass(kept, grad):
    return (grad,)

def back_keep(v):
    return (v, None)

def back_low(kept, grad):
    return (low(grad),)
low.defvjp(low_keep, low_pass)
low_back.defvjp(back_keep, back_low)

def rounded(value):
    return low_back(low(value))

def layer_norm(hidden, gain, shift):
    center = hidden - lax.optimization_barrier(jnp.mean(hidden, -1, keepdims=True))
    spread = lax.optimization_barrier(jnp.mean(center * center, -1, keepdims=True))
    return center * lax.rsqrt(spread + EPSILON) * gain + shift

def project(left, right):
    return jnp.dot(left, right, precision=HIGHEST)

def attend(queries, addresses, contents, causal):
    scores = jnp.einsum('blhe,bmhe->bhlm', queries, addresses, precision=HIGHEST) * 0.125
    if causal:
        row_place = lax.broadcasted_iota(jnp.int32, scores.shape, 2)
        col_place = lax.broadcasted_iota(jnp.int32, scores.shape, 3)
        scores = jnp.where(row_place >= col_place, scores, -1000000000.0)
    scores = low_back(scores)
    top = lax.optimization_barrier(jnp.max(scores, -1, keepdims=True))
    expo = jnp.exp(scores - top)
    weights = low(expo / lax.optimization_barrier(jnp.sum(expo, -1, keepdims=True)))
    return jnp.einsum('bhlm,bmhe->blhe', weights, contents, precision=HIGHEST)

def marginal_objective(seq_values, doc_scores, member, length):
    joint = doc_scores + seq_values / length
    masked = jnp.where(member, joint[None, :], -1e+30)
    top = lax.optimization_barrier(jnp.max(masked, 1, keepdims=True))
    unscaled = jnp.where(member, jnp.exp(masked - top), 0.0)
    total = lax.optimization_barrier(jnp.sum(unscaled, 1, keepdims=True))
    marginal = top[:, 0] + jnp.log(total[:, 0])
    posterior = unscaled / total
    entropy = -lax.optimization_barrier(jnp.sum(jnp.where(member, posterior * (joint[None, :] - marginal[:, None]), 0.0), 1))
    return jnp.mean(-marginal + ENTROPY_WEIGHT * entropy)

def forward(targets, passages, weights, labels, slot_question, slot_passage, doc_scores):
    query_weight, query_bias, key_weight, value_weight, value_bias, output_weight, output_bias, first_gain, first_shift, probe_weight, probe_bias, address_weight, content_weight, content_bias, merged_weight, merged_bias, second_gain, second_shift, expand_weight, expand_bias, shrink_weight, shrink_bias, third_gain, third_shift, embedding = weights
    slot_count = slot_question.shape[0]

    def split_heads(flat):
        return flat.reshape(slot_count, -1, HEADS, HD)
    inputs = low_back(targets[slot_question]).reshape(-1, D)
    self_queries = rounded(project(inputs, query_weight) + query_bias)
    self_addresses = rounded(project(inputs, key_weight))
    self_contents = rounded(project(inputs, value_weight) + value_bias)
    self_mixed = rounded(attend(split_heads(self_queries), split_heads(self_addresses), split_heads(self_contents), True).reshape(-1, D))
    branch = low_back(project(self_mixed, output_weight) + output_bias)
    first = layer_norm(inputs + branch, first_gain, first_shift)
    first_low = low(first)
    probes = rounded(project(first_low, probe_weight) + probe_bias)
    passage_rows = passages.reshape(-1, D)
    stored_addresses = rounded(project(passage_rows, address_weight)).reshape(PASSAGES, PLEN, HEADS, HD)
    stored_contents = rounded(project(passage_rows, content_weight) + content_bias).reshape(PASSAGES, PLEN, HEADS, HD)
    chosen = jnp.arange(slot_count, dtype=jnp.int32) // PAIRS_DEV * PASS_DEV + slot_passage
    recall_mixed = rounded(attend(split_heads(probes), stored_addresses[chosen], stored_contents[chosen], False).reshape(-1, D))
    branch = low_back(project(recall_mixed, merged_weight) + merged_bias)
    second = layer_norm(first + branch, second_gain, second_shift)
    second_low = low(second)
    expanded = low_back(project(second_low, expand_weight) + expand_bias)
    activated = low(jax.nn.gelu(expanded, approximate=False))
    branch = low_back(project(activated, shrink_weight) + shrink_bias)
    third = layer_norm(second + branch, third_gain, third_shift)
    third_low = low(third)

    def pair_likelihood(packed):
        states, wanted = packed
        logits = low_back(jnp.dot(states, embedding.T, precision=HIGHEST))
        top = lax.optimization_barrier(jnp.max(logits, -1, keepdims=True))
        log_norm = top[:, 0] + jnp.log(lax.optimization_barrier(jnp.sum(jnp.exp(logits - top), -1)))
        picked = jnp.take_along_axis(logits, wanted[:, None], 1)[:, 0]
        return jnp.sum(picked - log_norm)
    likelihood = lax.map(jax.checkpoint(pair_likelihood), (third_low.reshape(slot_count, LEN, D), labels[slot_question]))
    member = slot_question[None, :] == jnp.arange(QUESTIONS, dtype=jnp.int32)[:, None]
    return marginal_objective(likelihood, doc_scores, member, LEN)

def reference(targets, labels, passages, slot_question, slot_passage, score_table, score_index, query_weight, query_bias, key_weight, value_weight, value_bias, output_weight, output_bias, first_gain, first_shift, probe_weight, probe_bias, address_weight, content_weight, content_bias, merged_weight, merged_bias, second_gain, second_shift, expand_weight, expand_bias, shrink_weight, shrink_bias, third_gain, third_shift, embedding):
    weights = tuple((weight.astype(jnp.float32) for weight in (query_weight, query_bias, key_weight, value_weight, value_bias, output_weight, output_bias, first_gain, first_shift, probe_weight, probe_bias, address_weight, content_weight, content_bias, merged_weight, merged_bias, second_gain, second_shift, expand_weight, expand_bias, shrink_weight, shrink_bias, third_gain, third_shift, embedding)))
    doc_scores = score_table.astype(jnp.float32)[score_index]

    def wrapped(target_values, passage_values, weight_values):
        return forward(target_values, passage_values, weight_values, labels, slot_question, slot_passage, doc_scores)
    objective, pullback = jax.vjp(wrapped, targets.astype(jnp.float32), passages.astype(jnp.float32), weights)
    target_slope, passage_slope, slopes = pullback(jnp.ones_like(objective) * (QUESTIONS * LEN))
    return (objective, target_slope, passage_slope, slopes[0], slopes[1], slopes[2], slopes[3], slopes[4], slopes[5], slopes[6], slopes[7], slopes[8], slopes[9], slopes[10], slopes[11], slopes[12], slopes[13], slopes[14], slopes[15], slopes[16], slopes[17], slopes[18], slopes[19], slopes[20], slopes[21], slopes[22], slopes[23], slopes[24])
```

```python
import functools

import jax
import jax.numpy as jnp
from jax import lax
from jax.sharding import PartitionSpec as P

HD = 64
LANES = 128
EPSILON = 1e-05
ENTROPY_WEIGHT = 0.5
bfloat = jnp.bfloat16
single = jnp.float32


def norm_forward(hidden, gain, shift):
    center = hidden - jnp.mean(hidden, -1, keepdims=True)
    spread = jnp.mean(center * center, -1, keepdims=True)
    return center * lax.rsqrt(spread + EPSILON) * gain + shift


def norm_backward(hidden, gain, upstream):
    center = hidden - jnp.mean(hidden, -1, keepdims=True)
    spread = jnp.mean(center * center, -1, keepdims=True)
    inverse = lax.rsqrt(spread + EPSILON)
    normal = center * inverse
    scaled = upstream * gain
    delta = inverse * (
        scaled
        - jnp.mean(scaled, -1, keepdims=True)
        - normal * jnp.mean(scaled * normal, -1, keepdims=True)
    )
    return delta, jnp.sum(upstream * normal, 0), jnp.sum(upstream, 0)


def exact_gelu(inputs):
    return jax.nn.gelu(inputs, approximate=False)


def gelu_backward(inputs, upstream):
    unused_value, pullback = jax.vjp(exact_gelu, inputs)
    return pullback(upstream)[0]


def matmul(left, right):
    return jnp.dot(left, right, preferred_element_type=single)


def inner_rows(left, right):
    return lax.dot_general(left, right, (((0,), (0,)), ((), ())), preferred_element_type=single)


def outer_rows(left, right):
    return lax.dot_general(left, right, (((1,), (1,)), ((), ())), preferred_element_type=single)


def bits_of(count):
    bits = []
    while (1 << len(bits)) < count:
        bits.append(1 << len(bits))
    return bits


def swap(value, axis, count, bit):
    return lax.ppermute(value, axis, [(i, i ^ bit) for i in range(count)])


def relative_of(order):
    table = [0]
    for bit in order:
        table = table + [r ^ bit for r in table]
    return table


def gather_blocks(own, axis, count, order):
    held = own[None]
    for bit in order:
        held = jnp.concatenate([held, swap(held, axis, count, bit)], 0)
    return held


def scatter_blocks(parts, axis, count, order):
    for bit in reversed(order):
        half = parts.shape[0] // 2
        arrived = swap(parts[half:].astype(bfloat), axis, count, bit)
        parts = parts[:half] + arrived.astype(single)
    return parts[0]


def total_over(value, axis, count, order):
    for bit in order:
        value = value + swap(value, axis, count, bit)
    return value


def xor_take(table, me, array, axis):
    return jnp.take(array, me ^ jnp.asarray(table, jnp.int32), axis=axis, mode="clip")


def places(table):
    inverse = [0] * len(table)
    for position, relative in enumerate(table):
        inverse[relative] = position
    return inverse


def natural_order(table, me, array, axis):
    count = len(table)
    order = jnp.asarray(places(table), jnp.int32)[me ^ jnp.arange(count, dtype=jnp.int32)]
    return jnp.take(array, order, axis=axis, mode="clip")


def score_block(queries, addresses, causal):
    scores = (
        jnp.einsum("plhe,pmhe->phlm", queries, addresses, preferred_element_type=single) * 0.125
    )
    if causal:
        row_place = lax.broadcasted_iota(jnp.int32, scores.shape, 2)
        col_place = lax.broadcasted_iota(jnp.int32, scores.shape, 3)
        scores = jnp.where(row_place >= col_place, scores, -1000000000.0)
    return scores


def attend_forward(queries, addresses, contents, causal):
    scores = score_block(queries, addresses, causal)
    top = jnp.max(scores, -1, keepdims=True)
    expo = jnp.exp(scores - top)
    total = jnp.sum(expo, -1, keepdims=True)
    weights = (expo / total).astype(bfloat)
    mixed = jnp.einsum("phlm,pmhe->plhe", weights, contents, preferred_element_type=single)
    return (mixed.astype(bfloat), top + jnp.log(total))


def attend_backward(queries, addresses, contents, log_total, upstream, causal):
    weights = jnp.exp(score_block(queries, addresses, causal) - log_total)
    weight_delta = jnp.einsum("plhe,pmhe->phlm", upstream, contents, preferred_element_type=single)
    score_delta = (
        weights * (weight_delta - jnp.sum(weights * weight_delta, -1, keepdims=True))
    ).astype(bfloat)
    query_delta = (
        jnp.einsum("phlm,pmhe->plhe", score_delta, addresses, preferred_element_type=single) * 0.125
    )
    address_delta = (
        jnp.einsum("phlm,plhe->pmhe", score_delta, queries, preferred_element_type=single) * 0.125
    )
    content_delta = jnp.einsum(
        "phlm,plhe->pmhe", weights.astype(bfloat), upstream, preferred_element_type=single
    )
    return query_delta, address_delta, content_delta


def marginal_objective(seq_values, doc_scores, member, length):
    joint = doc_scores + seq_values / length
    masked = jnp.where(member, joint[None, :], -1e30)
    top = jnp.max(masked, 1, keepdims=True)
    unscaled = jnp.where(member, jnp.exp(masked - top), 0.0)
    total = jnp.sum(unscaled, 1, keepdims=True)
    marginal = top[:, 0] + jnp.log(total[:, 0])
    posterior = unscaled / total
    entropy = -jnp.sum(jnp.where(member, posterior * (joint[None, :] - marginal[:, None]), 0.0), 1)
    return jnp.mean(-marginal + ENTROPY_WEIGHT * entropy)


def on_device(
    dp,
    mp,
    targets,
    labels,
    passages,
    slot_question,
    slot_passage,
    score_table,
    score_index,
    query_weight,
    query_bias,
    key_weight,
    value_weight,
    value_bias,
    output_weight,
    output_bias,
    first_gain,
    first_shift,
    probe_weight,
    probe_bias,
    address_weight,
    content_weight,
    content_bias,
    merged_weight,
    merged_bias,
    second_gain,
    second_shift,
    expand_weight,
    expand_bias,
    shrink_weight,
    shrink_bias,
    third_gain,
    third_shift,
    embedding,
):
    group = lax.axis_index("dp")
    member_index = lax.axis_index("mp")
    own_questions, length, width = targets.shape
    questions = own_questions * dp
    pair_count = slot_passage.shape[0]
    store_count, passage_length = (passages.shape[0], passages.shape[1])
    vocab_share = embedding.shape[0]
    heads_local = query_weight.shape[1] // HD
    local_width = query_weight.shape[1]
    quarter = length // mp

    mp_order = bits_of(mp)[::-1]
    mp_table = relative_of(mp_order)
    dp_bits = bits_of(dp)
    dp_order = dp_bits[::-1]
    dp_table = relative_of(dp_order)

    def split_heads(flat, count):
        return flat.reshape(count, -1, heads_local, HD)

    def to_own(rows, count):
        natural = rows.reshape((count, mp, quarter) + rows.shape[2:])
        return jnp.moveaxis(xor_take(mp_table, member_index, natural, 1), 1, 0)

    def to_natural(rows, count):
        shaped = rows.reshape((mp, count, quarter) + rows.shape[1:])
        return jnp.moveaxis(natural_order(mp_table, member_index, shaped, 0), 0, 1)

    def mp_scatter(rows, count):
        return scatter_blocks(rows.reshape(mp, count * quarter, width), "mp", mp, mp_order)

    def mp_gather(rows):
        return gather_blocks(rows, "mp", mp, mp_order).reshape((-1,) + rows.shape[1:])

    gains = [value.astype(single) for value in (first_gain, second_gain, third_gain)]
    shifts = [value.astype(single) for value in (first_shift, second_shift, third_shift)]

    inputs = targets.reshape(own_questions * length, width)
    self_queries = (matmul(inputs, query_weight) + query_bias).astype(bfloat)
    self_addresses = matmul(inputs, key_weight).astype(bfloat)
    self_contents = (matmul(inputs, value_weight) + value_bias).astype(bfloat)
    self_mixed, self_total = attend_forward(
        split_heads(self_queries, own_questions),
        split_heads(self_addresses, own_questions),
        split_heads(self_contents, own_questions),
        True,
    )
    self_flat = self_mixed.reshape(own_questions * length, local_width)
    self_own = to_own(self_mixed.reshape(own_questions, length, local_width), own_questions)
    inputs_own = lax.dynamic_slice_in_dim(targets, member_index * quarter, quarter, 1)
    first_in = inputs_own.reshape(-1, width) + (
        mp_scatter(matmul(self_own.reshape(-1, local_width), output_weight), own_questions)
        + output_bias
    )
    first_norm = norm_forward(first_in, gains[0], shifts[0])
    first_low = first_norm.astype(bfloat)
    first_full = mp_gather(first_low)
    probe_own = (matmul(first_full, probe_weight) + probe_bias).astype(bfloat)

    def to_slots(value):
        gathered = gather_blocks(value, "dp", dp, dp_order)
        gathered = jnp.moveaxis(gathered, 2, 1).reshape((questions,) + value.shape[:1] + value.shape[2:])
        where = jnp.asarray(places(dp_table), jnp.int32)[group ^ (my_questions // own_questions)]
        return jnp.take(gathered, where * own_questions + my_questions % own_questions, axis=0, mode="clip")

    my_questions = lax.dynamic_slice_in_dim(slot_question, group * pair_count, pair_count)
    first_slots = to_slots(first_low.reshape(1, own_questions, quarter * width))
    first_slots = first_slots.reshape(pair_count * quarter, width)
    probe_slots = to_slots(probe_own.reshape(mp, own_questions, quarter * local_width))
    probe_slots = probe_slots.reshape(pair_count, length, local_width)

    passage_rows = passages.reshape(-1, width)
    stored_addresses = matmul(passage_rows, address_weight).astype(bfloat)
    stored_contents = (matmul(passage_rows, content_weight) + content_bias).astype(bfloat)

    def select(stored):
        picked = jnp.take(stored.reshape(store_count, -1), slot_passage, axis=0, mode="clip")
        return split_heads(picked, pair_count)

    picked_addresses = select(stored_addresses)
    picked_contents = select(stored_contents)
    cross_mixed, cross_total = attend_forward(
        split_heads(probe_slots, pair_count), picked_addresses, picked_contents, False
    )

    def slots_inside(rows):
        return jnp.moveaxis(rows.reshape(pair_count, mp, quarter, -1), 1, 0).reshape(
            mp * pair_count * quarter, -1
        )

    def slots_outside(rows):
        return jnp.moveaxis(rows.reshape(mp, pair_count, quarter, -1), 0, 1).reshape(
            pair_count, length, -1
        )

    cross_flat = slots_inside(cross_mixed)
    second_in = first_slots + (mp_scatter(matmul(cross_flat, merged_weight), pair_count) + merged_bias)
    second_norm = norm_forward(second_in, gains[1], shifts[1])
    second_low = mp_gather(second_norm.astype(bfloat))
    expanded = matmul(second_low, expand_weight) + expand_bias
    activated = exact_gelu(expanded).astype(bfloat)
    third_in = second_norm + (mp_scatter(matmul(activated, shrink_weight), pair_count) + shrink_bias)
    third_norm = norm_forward(third_in, gains[2], shifts[2])
    third_low = mp_gather(third_norm.astype(bfloat))

    pair_labels = to_own(jnp.take(labels, my_questions, axis=0, mode="clip"), pair_count).reshape(-1)
    local_index = pair_labels - member_index * vocab_share
    inside = (local_index >= 0) & (local_index < vocab_share)
    clipped = jnp.clip(local_index, 0, vocab_share - 1)
    label_rows = jnp.take(embedding, clipped, axis=0, mode="clip")
    logits = outer_rows(third_low, embedding)
    local_top = jnp.max(logits, -1)
    local_total = jnp.sum(jnp.exp(logits - local_top[:, None]), -1)
    local_target = jnp.where(
        inside, jnp.sum(third_low.astype(single) * label_rows.astype(single), -1), 0.0
    )
    top, total, target_logit = local_top, local_total, local_target
    stats = to_natural(jnp.stack([top, total, target_logit], -1), pair_count)
    for bit in mp_order[::-1]:
        other = swap(stats, "mp", mp, bit)
        high = jnp.maximum(stats[..., 0], other[..., 0])
        sums = stats[..., 1] * jnp.exp(stats[..., 0] - high) + other[..., 1] * jnp.exp(
            other[..., 0] - high
        )
        stats = jnp.stack([high, sums, stats[..., 2] + other[..., 2]], -1)
    row_log = stats[..., 0] + jnp.log(stats[..., 1])
    pair_likelihood = jnp.sum((stats[..., 2] - row_log).reshape(pair_count, length), -1)
    every_likelihood = natural_order(
        dp_table, group, gather_blocks(pair_likelihood, "dp", dp, dp_order), 0
    ).reshape(-1)
    log_norm = to_own(row_log.reshape(pair_count, length), pair_count).reshape(-1)
    doc_scores = jnp.take(score_table, score_index)
    member = slot_question[None, :] == jnp.arange(questions, dtype=jnp.int32)[:, None]

    def scored(values_all):
        return marginal_objective(values_all, doc_scores, member, length)

    objective, pullback = jax.vjp(scored, every_likelihood)
    likelihood_delta = pullback(jnp.ones_like(objective) * (questions * length))[0]
    pair_delta = lax.dynamic_slice_in_dim(likelihood_delta, group * pair_count, pair_count)
    row_delta = jnp.broadcast_to(pair_delta[None, :, None], (mp, pair_count, quarter)).reshape(-1)
    columns = lax.broadcasted_iota(jnp.int32, logits.shape, 1)
    hit_table = jnp.where(columns == local_index[:, None], 1.0, 0.0)
    logit_delta = (row_delta[:, None] * (hit_table - jnp.exp(logits - log_norm[:, None]))).astype(
        bfloat
    )

    fast = width % (dp * LANES) == 0

    def permuted(right, order):
        blocks = right.reshape(right.shape[0], dp, width // dp)
        return xor_take(relative_of(order), group, blocks, 1).reshape(right.shape)

    def slope_sum(pairs, order):
        if not fast:
            slope = jnp.concatenate([inner_rows(left, right) for left, right in pairs], 0)
            return lax.psum_scatter(slope, "dp", scatter_dimension=1, tiled=True)
        pairs = [(left, permuted(right, order)) for left, right in pairs]
        held = None
        span = width
        for bit in reversed(order):
            half = span // 2
            sent = [inner_rows(left, right[:, half:span]) for left, right in pairs]
            sent = sent[0] if len(sent) == 1 else jnp.concatenate(sent, 0)
            if held is not None:
                sent = sent + held[:, half:].astype(single)
                held = held[:, :half]
            arrived = swap(sent.astype(bfloat), "dp", dp, bit)
            held = arrived if held is None else held.astype(single) + arrived.astype(single)
            span = half
        kept = [inner_rows(left, right[:, :span]) for left, right in pairs]
        kept = kept[0] if len(kept) == 1 else jnp.concatenate(kept, 0)
        return kept + held.astype(single)

    order_a = dp_bits[::-1]
    order_b = order_a if dp < 4 else [dp_bits[-1], dp_bits[0]] + dp_bits[1:-1]
    unit = vocab_share // 7 if vocab_share % 7 == 0 else vocab_share
    cuts = [0, 2 * unit, 4 * unit, 6 * unit, vocab_share] if unit < vocab_share else [0, unit]
    embedding_parts = []
    for index in range(len(cuts) - 1):
        piece = logit_delta[:, cuts[index] : cuts[index + 1]]
        embedding_parts.append(slope_sum([(piece, third_low)], order_b if index == 1 else order_a))
    embedding_slope = jnp.concatenate(embedding_parts, 0)

    third_delta = mp_scatter(matmul(logit_delta, embedding), pair_count)
    third_back = norm_backward(third_in, gains[2], third_delta)
    feed_low = third_back[0].astype(bfloat)
    feed_delta = mp_gather(feed_low)
    expanded_delta = gelu_backward(expanded, outer_rows(feed_delta, shrink_weight)).astype(bfloat)
    bias_expand = jnp.sum(expanded_delta, 0, dtype=single)
    second_delta = third_back[0] + mp_scatter(outer_rows(expanded_delta, expand_weight), pair_count)
    second_back = norm_backward(second_in, gains[1], second_delta)
    recall_low = second_back[0].astype(bfloat)
    recall_delta = mp_gather(recall_low)
    mixed_delta = outer_rows(recall_delta, merged_weight).astype(bfloat)
    probe_delta, picked_address_delta, picked_content_delta = attend_backward(
        split_heads(probe_slots, pair_count),
        picked_addresses,
        picked_contents,
        cross_total,
        split_heads(slots_outside(mixed_delta), pair_count),
        False,
    )

    def to_questions(value):
        natural = jnp.arange(dp, dtype=jnp.int32)[:, None] * 0 + (
            (group ^ jnp.asarray(dp_table, jnp.int32))[:, None] * own_questions
            + jnp.arange(own_questions, dtype=jnp.int32)[None, :]
        )
        binned = sum(
            jnp.where((natural == my_questions[s])[..., None], value[s][None, None, :], 0.0)
            for s in range(pair_count)
        )
        return scatter_blocks(binned, "dp", dp, dp_order)

    state_delta = to_questions(second_back[0].reshape(pair_count, quarter * width))
    state_delta = state_delta.reshape(own_questions * quarter, width)
    probe_sum = to_questions(probe_delta.reshape(pair_count, length * local_width))
    probe_flat = jnp.moveaxis(
        probe_sum.reshape(own_questions, mp, quarter, local_width), 1, 0
    ).reshape(-1, local_width).astype(bfloat)

    def by_passage(value):
        flat = value.reshape(pair_count, -1)
        return jnp.stack(
            [
                sum(jnp.where(slot_passage[s] == p, flat[s], 0.0) for s in range(pair_count))
                for p in range(store_count)
            ]
        ).astype(bfloat).reshape(store_count * passage_length, local_width)

    address_delta = by_passage(picked_address_delta)
    content_delta = by_passage(picked_content_delta)
    bias_content = jnp.sum(content_delta, 0, dtype=single)
    passages_slope = lax.psum(
        (outer_rows(address_delta, address_weight) + outer_rows(content_delta, content_weight)).astype(bfloat),
        "mp",
    ).astype(single).reshape(passages.shape)

    bias_probe = jnp.sum(probe_flat, 0, dtype=single)
    first_delta = state_delta + mp_scatter(outer_rows(probe_flat, probe_weight), own_questions)
    first_back = norm_backward(first_in, gains[0], first_delta)
    self_low = first_back[0].astype(bfloat)
    self_delta = to_natural(mp_gather(self_low), own_questions).reshape(-1, width)
    self_mixed_delta = outer_rows(self_delta, output_weight).astype(bfloat)
    query_delta, address_raw, content_raw = attend_backward(
        split_heads(self_queries, own_questions),
        split_heads(self_addresses, own_questions),
        split_heads(self_contents, own_questions),
        self_total,
        split_heads(self_mixed_delta, own_questions),
        True,
    )
    query_flat = query_delta.reshape(-1, local_width).astype(bfloat)
    key_flat = address_raw.reshape(-1, local_width).astype(bfloat)
    value_flat = content_raw.reshape(-1, local_width).astype(bfloat)
    bias_query = jnp.sum(query_flat, 0, dtype=single)
    bias_value = jnp.sum(value_flat, 0, dtype=single)
    partial = (
        outer_rows(query_flat, query_weight)
        + outer_rows(key_flat, key_weight)
        + outer_rows(value_flat, value_weight)
    )
    partial_own = to_own(partial.reshape(own_questions, length, width), own_questions)
    input_delta = first_back[0] + mp_scatter(partial_own, own_questions)
    targets_slope = to_natural(mp_gather(input_delta.astype(bfloat)), own_questions)
    targets_slope = targets_slope.reshape(targets.shape).astype(single)

    feed_slopes = slope_sum([(activated, feed_delta), (expanded_delta, second_low)], order_a)
    cross_slopes = slope_sum(
        [
            (cross_flat, recall_delta),
            (address_delta, passage_rows),
            (content_delta, passage_rows),
        ],
        order_a,
    )
    self_slopes = slope_sum(
        [
            (probe_flat, first_full),
            (self_flat, self_delta),
            (query_flat, inputs),
            (key_flat, inputs),
            (value_flat, inputs),
        ],
        order_a,
    )
    hidden = expanded.shape[1]
    shrink_slope = feed_slopes[:hidden]
    expand_slope = feed_slopes[hidden:].T
    merged_slope = cross_slopes[:local_width]
    address_slope = cross_slopes[local_width : 2 * local_width].T
    content_slope = cross_slopes[2 * local_width :].T
    probe_slope = self_slopes[:local_width].T
    output_slope = self_slopes[local_width : 2 * local_width]
    query_slope = self_slopes[2 * local_width : 3 * local_width].T
    key_slope = self_slopes[3 * local_width : 4 * local_width].T
    value_slope = self_slopes[4 * local_width :].T

    shared = total_over(
        jnp.stack(
            [
                jnp.sum(self_low, 0, dtype=single),
                first_back[1],
                first_back[2],
                jnp.sum(recall_low, 0, dtype=single),
                second_back[1],
                second_back[2],
                jnp.sum(feed_low, 0, dtype=single),
                third_back[1],
                third_back[2],
            ]
        ),
        "mp",
        mp,
        mp_order,
    )
    vectors = jnp.concatenate(
        [
            value.reshape(-1, dp, value.shape[-1] // dp).swapaxes(0, 1).reshape(dp, -1)
            for value in (shared, bias_expand, bias_query, bias_value, bias_probe, bias_content)
        ],
        1,
    )
    vectors = scatter_blocks(xor_take(dp_table, group, vectors, 0), "dp", dp, dp_order)
    span = width // dp
    (
        bias_output,
        first_gain_slope,
        first_shift_slope,
        bias_merged,
        second_gain_slope,
        second_shift_slope,
        bias_shrink,
        third_gain_slope,
        third_shift_slope,
    ) = (vectors[i * span : (i + 1) * span] for i in range(9))
    vectors = vectors[9 * span :]
    bias_expand = vectors[: hidden // dp]
    vectors = vectors[hidden // dp :]
    bias_query, bias_value, bias_probe, bias_content = (
        vectors[i * (local_width // dp) : (i + 1) * (local_width // dp)] for i in range(4)
    )
    return (
        objective,
        targets_slope,
        passages_slope,
        query_slope,
        bias_query,
        key_slope,
        value_slope,
        bias_value,
        output_slope,
        bias_output,
        first_gain_slope,
        first_shift_slope,
        probe_slope,
        bias_probe,
        address_slope,
        content_slope,
        bias_content,
        merged_slope,
        bias_merged,
        second_gain_slope,
        second_shift_slope,
        expand_slope,
        bias_expand,
        shrink_slope,
        bias_shrink,
        third_gain_slope,
        third_shift_slope,
        embedding_slope,
    )


def solution(mesh):
    return jax.shard_map(
        functools.partial(on_device, mesh.shape["dp"], mesh.shape["mp"]),
        mesh=mesh,
        in_specs=(
            P("dp", None, None),
            P(),
            P("dp", None, None),
            P(),
            P("dp"),
            P(),
            P(),
            P(None, "mp"),
            P("mp"),
            P(None, "mp"),
            P(None, "mp"),
            P("mp"),
            P("mp", None),
            P(),
            P(),
            P(),
            P(None, "mp"),
            P("mp"),
            P(None, "mp"),
            P(None, "mp"),
            P("mp"),
            P("mp", None),
            P(),
            P(),
            P(),
            P(None, "mp"),
            P("mp"),
            P("mp", None),
            P(),
            P(),
            P(),
            P("mp", None),
        ),
        out_specs=(
            P(),
            P("dp", None, None),
            P("dp", None, None),
            P("dp", "mp"),
            P(("mp", "dp")),
            P("dp", "mp"),
            P("dp", "mp"),
            P(("mp", "dp")),
            P("mp", "dp"),
            P("dp"),
            P("dp"),
            P("dp"),
            P("dp", "mp"),
            P(("mp", "dp")),
            P("dp", "mp"),
            P("dp", "mp"),
            P(("mp", "dp")),
            P("mp", "dp"),
            P("dp"),
            P("dp"),
            P("dp"),
            P("dp", "mp"),
            P(("mp", "dp")),
            P("mp", "dp"),
            P("dp"),
            P("dp"),
            P("dp"),
            P("mp", "dp"),
        ),
        check_vma=False,
    )
```

```python
import functools

import jax
import jax.numpy as jnp
from jax import lax
from jax.experimental import pallas as pl
from jax.experimental.pallas import tpu as pltpu
from jax.sharding import PartitionSpec as P

HD = 64
LANES = 128
EPSILON = 1e-05
ENTROPY_WEIGHT = 0.5
BRIEF = pl.CostEstimate(flops=0, bytes_accessed=0, transcendentals=0)
bfloat = jnp.bfloat16
single = jnp.float32


def matmul(left, right):
    return jnp.dot(left, right, preferred_element_type=single)


def inner_rows(left, right):
    return lax.dot_general(left, right, (((0,), (0,)), ((), ())), preferred_element_type=single)


def outer_rows(left, right):
    return lax.dot_general(left, right, (((1,), (1,)), ((), ())), preferred_element_type=single)


def bits_of(count):
    bits = []
    while (1 << len(bits)) < count:
        bits.append(1 << len(bits))
    return bits


def swap(value, axis, count, bit):
    return lax.ppermute(value, axis, [(i, i ^ bit) for i in range(count)])


def relative_of(order):
    table = [0]
    for bit in order:
        table = table + [r ^ bit for r in table]
    return table


def gather_blocks(own, axis, count, order):
    held = own[None]
    for bit in order:
        held = jnp.concatenate([held, swap(held, axis, count, bit)], 0)
    return held


def scatter_blocks(parts, axis, count, order):
    for bit in reversed(order):
        half = parts.shape[0] // 2
        arrived = swap(parts[half:].astype(bfloat), axis, count, bit)
        parts = parts[:half] + arrived.astype(single)
    return parts[0]


def tie(*values):
    return lax.optimization_barrier(values)


def gather_both(owns, axis, count, orders):
    helds = [own[None] for own in owns]
    for bits in zip(*orders):
        arrived = tie(*(swap(held, axis, count, bit) for held, bit in zip(helds, bits)))
        helds = [jnp.concatenate([held, more], 0) for held, more in zip(helds, arrived)]
    return helds


def scatter_both_steps(values, axis, count, orders, through):
    for bits in zip(*(order[::-1] for order in orders)):
        sent = through(*(value[0] for value in values))
        arrived = [swap(value, axis, count, bit) for value, bit in zip(sent, bits)]
        yield None
        arrived = through(*arrived)
        if bits[0] == orders[0][0]:
            yield [(value[1], more) for value, more in zip(values, arrived)]
        else:
            values = [add_halves(value[1], more) for value, more in zip(values, arrived)]


def total_over(value, axis, count, order):
    for bit in order:
        value = value + swap(value, axis, count, bit)
    return value


def xor_take(table, me, array, axis):
    return jnp.take(array, me ^ jnp.asarray(table, jnp.int32), axis=axis, mode="clip")


def places(table):
    inverse = [0] * len(table)
    for position, relative in enumerate(table):
        inverse[relative] = position
    return inverse


def natural_order(table, me, array, axis):
    count = len(table)
    order = jnp.asarray(places(table), jnp.int32)[me ^ jnp.arange(count, dtype=jnp.int32)]
    return jnp.take(array, order, axis=axis, mode="clip")


VMEM = pl.BlockSpec(memory_space=pltpu.VMEM)


def run_whole(kernel, name, outs, *operands, scratch=()):
    return pl.pallas_call(
        kernel,
        in_specs=[VMEM] * len(operands),
        out_specs=[VMEM] * len(outs),
        out_shape=[jax.ShapeDtypeStruct(shape, dtype) for shape, dtype in outs],
        scratch_shapes=list(scratch),
        compiler_params=pltpu.CompilerParams(vmem_limit_bytes=56 * 1024 * 1024),
        cost_estimate=BRIEF,
        name=name,
    )(*operands)


def row(vector):
    return vector.reshape(1, -1).astype(single)


def norm_forward_kernel(kept_ref, arrived_ref, state_ref, bias_ref, gain_ref, shift_ref, in_ref, out_ref, low_ref):
    hidden = (
        state_ref[...].astype(single)
        + (kept_ref[...].astype(single) + arrived_ref[...].astype(single))
        + bias_ref[...]
    )
    in_ref[...] = hidden
    center = hidden - jnp.mean(hidden, -1, keepdims=True)
    spread = jnp.mean(center * center, -1, keepdims=True)
    normal = center * lax.rsqrt(spread + EPSILON) * gain_ref[...] + shift_ref[...]
    out_ref[...] = normal
    low_ref[...] = normal.astype(bfloat)


def norm_forward(kept, arrived, state, bias, gain, shift):
    shape = state.shape
    return run_whole(
        norm_forward_kernel,
        "norm_forward",
        [(shape, single), (shape, single), (shape, bfloat)],
        kept.reshape(shape),
        arrived.reshape(shape),
        state,
        row(bias),
        row(gain),
        row(shift),
    )


def norm_backward_kernel(count, *refs):
    hidden_ref, gain_ref, out_ref, low_ref, sums_ref = refs[count:]
    upstream = refs[0][...].astype(single)
    for ref in refs[1:count]:
        upstream = upstream + ref[...].astype(single)
    hidden = hidden_ref[...]
    center = hidden - jnp.mean(hidden, -1, keepdims=True)
    spread = jnp.mean(center * center, -1, keepdims=True)
    inverse = lax.rsqrt(spread + EPSILON)
    normal = center * inverse
    scaled = upstream * gain_ref[...]
    delta = inverse * (
        scaled
        - jnp.mean(scaled, -1, keepdims=True)
        - normal * jnp.mean(scaled * normal, -1, keepdims=True)
    )
    low = delta.astype(bfloat)
    out_ref[...] = delta
    low_ref[...] = low
    sums_ref[0:1, :] = jnp.sum(low.astype(single), 0, keepdims=True)
    sums_ref[1:2, :] = jnp.sum(upstream * normal, 0, keepdims=True)
    sums_ref[2:3, :] = jnp.sum(upstream, 0, keepdims=True)


def norm_backward(parts, hidden, gain):
    shape = hidden.shape
    return run_whole(
        functools.partial(norm_backward_kernel, len(parts)),
        "norm_backward",
        [(shape, single), (shape, bfloat), ((3, shape[1]), single)],
        *(part.reshape(shape) for part in parts),
        hidden,
        row(gain),
    )


def erf_gelu(value):
    phi = 0.5 * (1.0 + lax.erf(value * 0.7071067811865476))
    return value * phi, phi


def join(pieces, full_ref):
    rows = pieces[0].shape[0]
    for index, piece in enumerate(pieces):
        full_ref[index * rows : (index + 1) * rows, :] = piece[...]


def feed_forward_kernel(count, *refs):
    expand_ref, bias_ref, shrink_ref, full_ref, hidden_ref, act_ref, sent_ref, kept_ref = refs[count:]
    join(refs[:count], full_ref)
    half = sent_ref.shape[0]
    for index in (1, 0):
        part = slice(index * half, (index + 1) * half)
        hidden = matmul(full_ref[part, :], expand_ref[...]) + bias_ref[...]
        hidden_ref[part, :] = hidden
        act = erf_gelu(hidden)[0].astype(bfloat)
        act_ref[part, :] = act
        out = matmul(act, shrink_ref[...])
        if index == 0:
            kept_ref[...] = out
        else:
            sent_ref[...] = out.astype(bfloat)


def feed_forward(pieces, expand, bias, shrink):
    rows, width = len(pieces) * pieces[0].shape[0], pieces[0].shape[1]
    hidden = expand.shape[1]
    return run_whole(
        functools.partial(feed_forward_kernel, len(pieces)),
        "feed_forward",
        [
            ((rows, width), bfloat),
            ((rows, hidden), single),
            ((rows, hidden), bfloat),
            ((rows // 2, width), bfloat),
            ((rows // 2, width), single),
        ],
        *pieces,
        expand,
        row(bias),
        shrink,
    )


def feed_backward_kernel(count, *refs):
    expand_ref, shrink_ref, hidden_ref, full_ref, delta_ref, sums_ref, sent_ref, kept_ref = refs[count:]
    join(refs[:count], full_ref)
    half = sent_ref.shape[0]
    sums = jnp.zeros(sums_ref.shape, single)
    for index in (1, 0):
        part = slice(index * half, (index + 1) * half)
        upstream = outer_rows(full_ref[part, :], shrink_ref[...])
        hidden = hidden_ref[part, :]
        slope = erf_gelu(hidden)[1] + hidden * jnp.exp(-0.5 * hidden * hidden) * 0.3989422804014327
        delta = (upstream * slope).astype(bfloat)
        delta_ref[part, :] = delta
        sums = sums + jnp.sum(delta.astype(single), 0, keepdims=True)
        out = outer_rows(delta, expand_ref[...])
        if index == 0:
            kept_ref[...] = out
        else:
            sent_ref[...] = out.astype(bfloat)
    sums_ref[...] = sums


def feed_backward(pieces, expand, shrink, hidden):
    rows, width = len(pieces) * pieces[0].shape[0], pieces[0].shape[1]
    return run_whole(
        functools.partial(feed_backward_kernel, len(pieces)),
        "feed_backward",
        [
            ((rows, width), bfloat),
            (hidden.shape, bfloat),
            ((1, hidden.shape[1]), single),
            ((rows // 2, width), bfloat),
            ((rows // 2, width), single),
        ],
        *pieces,
        expand,
        shrink,
        hidden,
    )


def project_kernel(count, transposed, *refs):
    weight_ref, bias_ref, full_ref, out_ref = refs[count:]
    join(refs[:count], full_ref)
    out = (outer_rows if transposed else matmul)(full_ref[...], weight_ref[...])
    out_ref[...] = (out + bias_ref[...]).astype(bfloat)


def project(pieces, weight, bias, transposed=False):
    rows, width = len(pieces) * pieces[0].shape[0], pieces[0].shape[1]
    return run_whole(
        functools.partial(project_kernel, len(pieces), transposed),
        "project",
        [((rows, width), bfloat), ((rows, bias.shape[0]), bfloat)],
        *pieces,
        weight,
        row(bias),
    )


def halves_kernel(count, transposed, *refs):
    lefts, weights, (sent_ref, kept_ref) = refs[:count], refs[count : 2 * count], refs[2 * count :]
    half = sent_ref.shape[0]
    product = outer_rows if transposed else matmul
    for part, out in ((slice(half, 2 * half), sent_ref), (slice(0, half), kept_ref)):
        total = product(lefts[0][part, :], weights[0][...])
        for left, weight in zip(lefts[1:], weights[1:]):
            total = total + product(left[part, :], weight[...])
        out[...] = total.astype(out.dtype)


def product_halves(lefts, weights, transposed=False):
    half = lefts[0].shape[0] // 2
    width = weights[0].shape[0] if transposed else weights[0].shape[1]
    return run_whole(
        functools.partial(halves_kernel, len(lefts), transposed),
        "product_halves",
        [((half, width), bfloat), ((half, width), single)],
        *lefts,
        *weights,
    )


def add_halves_kernel(kept_ref, arrived_ref, sent_ref, left_ref):
    half = kept_ref.shape[0] // 2
    sent_ref[...] = (kept_ref[half:, :].astype(single) + arrived_ref[half:, :].astype(single)).astype(bfloat)
    left_ref[...] = kept_ref[:half, :].astype(single) + arrived_ref[:half, :].astype(single)


def add_halves(kept, arrived):
    half, width = kept.shape[0] // 2, kept.shape[1]
    return run_whole(
        add_halves_kernel,
        "add_halves",
        [((half, width), bfloat), ((half, width), single)],
        kept,
        arrived,
    )


def add_columns_kernel(kept_ref, arrived_ref, sent_ref, left_ref):
    half = sent_ref.shape[1]
    total = kept_ref[...].astype(single) + arrived_ref[...].astype(single)
    sent_ref[...] = total[:, half:].astype(bfloat)
    left_ref[...] = total[:, :half].astype(bfloat)


def add_columns(kept, arrived):
    rows, width = kept.shape
    block = rows
    for count in (8, 7, 6, 5, 4, 3, 2):
        if rows % (16 * count) == 0:
            block = rows // count
            break
    whole = pl.BlockSpec((block, width), lambda i: (i, 0))
    half = pl.BlockSpec((block, width // 2), lambda i: (i, 0))
    return pl.pallas_call(
        add_columns_kernel,
        grid=(rows // block,),
        in_specs=[whole, whole],
        out_specs=[half, half],
        out_shape=[jax.ShapeDtypeStruct((rows, width // 2), bfloat)] * 2,
        cost_estimate=BRIEF,
        name="add_columns",
    )(kept, arrived)


def bin_rows_kernel(bins_ref, value_ref, sent_ref, kept_ref, sums):
    sums[...] = jnp.zeros_like(sums)
    for slot in range(value_ref.shape[0]):
        sums[bins_ref[slot]] += value_ref[slot]
    half = sent_ref.shape[0]
    sent_ref[...] = sums[half:].astype(bfloat)
    kept_ref[...] = sums[:half]


def bin_rows(value, bins, count):
    shape = (count // 2,) + value.shape[1:]
    return pl.pallas_call(
        bin_rows_kernel,
        in_specs=[pl.BlockSpec(memory_space=pltpu.SMEM), VMEM],
        out_specs=[VMEM, VMEM],
        out_shape=[jax.ShapeDtypeStruct(shape, bfloat), jax.ShapeDtypeStruct(shape, single)],
        scratch_shapes=[pltpu.VMEM((count,) + value.shape[1:], single)],
        compiler_params=pltpu.CompilerParams(vmem_limit_bytes=56 * 1024 * 1024),
        cost_estimate=BRIEF,
        name="bin_rows",
    )(bins, value)


def vocab_tile(vocab_share):
    for tile in (1792, 896, 512, 256, 128):
        if vocab_share % tile == 0:
            return tile
    return vocab_share


def vocab_forward_kernel(state_ref, table_ref, label_ref, weight_ref, sum_ref, mixed_ref, tops_ref, top):
    step = pl.program_id(0)
    rows = state_ref.shape[0]
    tile = table_ref.shape[0]
    block = min(rows, 1024)

    @pl.when(step == 0)
    def start():
        top[...] = jnp.full_like(top, -jnp.inf)
        sum_ref[...] = jnp.zeros_like(sum_ref)
        mixed_ref[...] = jnp.zeros_like(mixed_ref)
        tops_ref[...] = jnp.zeros_like(tops_ref)

    repeat = lambda value, count: jnp.concatenate([value] * count, 1) if count > 1 else value
    spans = tile // LANES
    for index in range(rows // block):
        part = pl.ds(index * block, block)
        logits = outer_rows(state_ref[part, :], table_ref[...])
        old = top[part, :]
        new = jnp.maximum(old, jnp.max(logits, -1, keepdims=True))
        lanes = lax.broadcasted_iota(jnp.int32, new.shape, 1)
        offset = label_ref[part, :] - step * tile
        shrink = jnp.exp(old - new)
        top[part, :] = new
        tops_ref[part, :] = jnp.where(lanes == step, new, tops_ref[part, :])
        sums = sum_ref[part, :] * shrink
        low = []
        for span in range(spans):
            weights = jnp.exp(logits[:, span * LANES : (span + 1) * LANES] - new)
            weights = jnp.where(lanes + span * LANES == offset, 0.0, weights)
            sums = sums + weights
            low.append(weights.astype(bfloat))
        sum_ref[part, :] = sums
        low = jnp.concatenate(low, 1)
        weight_ref[part, :] = low
        mixed_ref[part, :] = mixed_ref[part, :] * repeat(shrink, mixed_ref.shape[1] // LANES) + matmul(
            low, table_ref[...]
        )


def vocab_forward(states, table, label):
    rows, width = states.shape
    entries = table.shape[0]
    tile = vocab_tile(entries)
    whole = lambda *shape: pl.BlockSpec(shape, lambda i: (0,) * len(shape))
    return pl.pallas_call(
        vocab_forward_kernel,
        grid=(entries // tile,),
        in_specs=[
            whole(rows, width),
            pl.BlockSpec((tile, width), lambda i: (i, 0)),
            whole(rows, LANES),
        ],
        out_specs=[
            pl.BlockSpec((rows, tile), lambda i: (0, i)),
            whole(rows, LANES),
            whole(rows, width),
            whole(rows, LANES),
        ],
        out_shape=[
            jax.ShapeDtypeStruct((rows, entries), bfloat),
            jax.ShapeDtypeStruct((rows, LANES), single),
            jax.ShapeDtypeStruct((rows, width), single),
            jax.ShapeDtypeStruct((rows, LANES), single),
        ],
        scratch_shapes=[pltpu.VMEM((rows, LANES), single)],
        compiler_params=pltpu.CompilerParams(
            dimension_semantics=("arbitrary",), vmem_limit_bytes=56 * 1024 * 1024
        ),
        cost_estimate=BRIEF,
        name="vocab_forward",
    )(states, table, label)


def vocab_slope_kernel(first, ratio, order_ref, weight_ref, factor_ref, label_ref, patch_ref, state_ref, sent_ref, kept_ref, moved):
    step = pl.program_id(0)
    tile = weight_ref.shape[1]
    width = state_ref.shape[1]
    blocks = order_ref.shape[0]
    span = width // blocks

    @pl.when(step == 0)
    def start():
        for place in range(blocks):
            source = pl.multiple_of(order_ref[place] * span, span)
            moved[:, place * span : (place + 1) * span] = state_ref[:, pl.ds(source, span)]

    here = step + first
    factors = factor_ref[...]
    lanes = lax.broadcasted_iota(jnp.int32, factors.shape, 1)
    factor = jnp.sum(jnp.where(lanes == here // ratio, factors, 0.0), -1, keepdims=True)
    columns = lax.broadcasted_iota(jnp.int32, weight_ref.shape, 1) + here * tile
    delta = jnp.where(
        columns == label_ref[...], patch_ref[...], weight_ref[...].astype(single) * factor
    ).astype(bfloat)
    half = width // 2
    sent_ref[...] = inner_rows(delta, moved[:, half:]).astype(bfloat)
    kept_ref[...] = inner_rows(delta, moved[:, :half]).astype(bfloat)


def vocab_slope(weights, factors, label, patch, states, order, first, count, tile):
    rows, width = states.shape
    whole = lambda *shape: pl.BlockSpec(shape, lambda i, o: (0,) * len(shape))
    half = pl.BlockSpec((tile, width // 2), lambda i, o: (i, 0))
    return pl.pallas_call(
        functools.partial(vocab_slope_kernel, first, vocab_tile(weights.shape[1]) // tile),
        grid_spec=pltpu.PrefetchScalarGridSpec(
            num_scalar_prefetch=1,
            grid=(count,),
            in_specs=[
                pl.BlockSpec((rows, tile), lambda i, o: (0, i + first)),
                whole(rows, LANES),
                whole(rows, 1),
                whole(rows, 1),
                whole(rows, width),
            ],
            out_specs=[half, half],
            scratch_shapes=[pltpu.VMEM((rows, width), bfloat)],
        ),
        out_shape=[jax.ShapeDtypeStruct((count * tile, width // 2), bfloat)] * 2,
        compiler_params=pltpu.CompilerParams(
            dimension_semantics=("arbitrary",), vmem_limit_bytes=56 * 1024 * 1024
        ),
        cost_estimate=BRIEF,
        name="vocab_slope",
    )(order, weights, factors, label, patch, states)


def slope_group_kernel(count, order_ref, *refs):
    lefts, rights = refs[:count], refs[count : 2 * count]
    sent_ref, kept_ref, moved = refs[2 * count :]
    blocks = order_ref.shape[0]
    width = rights[0].shape[1]
    span, half = width // blocks, width // 2
    base = 0
    for index in range(count):
        rows, entries = lefts[index].shape
        if index == 0 or rights[index] is not rights[index - 1]:
            for place in range(blocks):
                source = pl.multiple_of(order_ref[place] * span, span)
                moved[:rows, place * span : (place + 1) * span] = rights[index][:, pl.ds(source, span)]
        right = moved[:rows, :]
        left = lefts[index][...]
        sent_ref[base : base + entries, :] = inner_rows(left, right[:, half:]).astype(bfloat)
        kept_ref[base : base + entries, :] = inner_rows(left, right[:, :half]).astype(bfloat)
        base += entries


def slope_group(pairs, order):
    width = pairs[0][1].shape[1]
    total = sum(left.shape[1] for left, right in pairs)
    rows = max(left.shape[0] for left, right in pairs)
    lefts = [left for left, right in pairs]
    rights = [right for left, right in pairs]
    whole = pl.BlockSpec(memory_space=pltpu.VMEM)
    return pl.pallas_call(
        functools.partial(slope_group_kernel, len(pairs)),
        in_specs=[pl.BlockSpec(memory_space=pltpu.SMEM)] + [whole] * (2 * len(pairs)),
        out_specs=[whole, whole],
        out_shape=[jax.ShapeDtypeStruct((total, width // 2), bfloat)] * 2,
        scratch_shapes=[pltpu.VMEM((rows, width), bfloat)],
        compiler_params=pltpu.CompilerParams(vmem_limit_bytes=56 * 1024 * 1024),
        cost_estimate=BRIEF,
        name="slope_group",
    )(order, *lefts, *rights)


def head_weights(causal, places, query, address, lanes, head):
    own = (lanes // HD) == head
    scores = outer_rows(jnp.where(own, query, jnp.zeros_like(query)), address) * 0.125
    if causal:
        scores = jnp.where(places[0][:, :1] >= places[1][:1, :], scores, -1000000000.0)
    expo = jnp.exp(scores - jnp.max(scores, -1, keepdims=True))
    return own, expo / jnp.sum(expo, -1, keepdims=True)


def attend_forward_kernel(causal, bins_ref, stores_ref, query_ref, address_ref, content_ref, *refs):
    mixed_ref = refs[-1]
    places = [ref[...] for ref in refs[:-1]]
    length, width = query_ref.shape[1:]
    for pair in range(width // LANES):
        part = slice(pair * LANES, (pair + 1) * LANES)
        query, address, content = query_ref[0, :, part], address_ref[0, :, part], content_ref[0, :, part]
        lanes = lax.broadcasted_iota(jnp.int32, query.shape, 1)
        total = jnp.zeros(query.shape, single)
        for head in range(LANES // HD):
            own, weights = head_weights(causal, places, query, address, lanes, head)
            total = jnp.where(own, matmul(weights.astype(bfloat), content), total)
        shape = (mixed_ref.shape[0], mixed_ref.shape[2], LANES)
        mixed_ref[:, 0, :, part] = total.astype(bfloat).reshape(shape)


def attend_forward(queries, addresses, contents, bins, stores, parts, places=()):
    count = bins.shape[0]
    length, width = queries.shape[1:]
    stored = addresses.shape[1]
    return pl.pallas_call(
        functools.partial(attend_forward_kernel, bool(places)),
        grid_spec=pltpu.PrefetchScalarGridSpec(
            num_scalar_prefetch=2,
            grid=(count,),
            in_specs=[
                pl.BlockSpec((1, length, width), lambda i, b, s: (b[i], 0, 0)),
                pl.BlockSpec((1, stored, width), lambda i, b, s: (s[i], 0, 0)),
                pl.BlockSpec((1, stored, width), lambda i, b, s: (s[i], 0, 0)),
            ]
            + [pl.BlockSpec(place.shape, lambda i, b, s: (0, 0)) for place in places],
            out_specs=pl.BlockSpec((parts, 1, length // parts, width), lambda i, b, s: (0, i, 0, 0)),
        ),
        out_shape=jax.ShapeDtypeStruct((parts, count, length // parts, width), bfloat),
        compiler_params=pltpu.CompilerParams(
            dimension_semantics=("arbitrary",), vmem_limit_bytes=32 * 1024 * 1024
        ),
        cost_estimate=BRIEF,
        name="attend_forward",
    )(bins, stores, queries, addresses, contents, *places)


def attend_backward_kernel(
    causal, bins_ref, stores_ref, sums_ref, query_ref, address_ref, content_ref, upstream_ref, *refs
):
    query_out, address_out, content_out, query_sum, address_sum, content_sum = refs[-6:]
    places = [ref[...] for ref in refs[:-6]]
    step = pl.program_id(0)
    length, width = query_ref.shape[1:]

    @pl.when(step == 0)
    def start():
        query_sum[...] = jnp.zeros_like(query_sum)
        address_sum[...] = jnp.zeros_like(address_sum)
        content_sum[...] = jnp.zeros_like(content_sum)

    for pair in range(width // LANES):
        part = slice(pair * LANES, (pair + 1) * LANES)
        query, address, content = query_ref[0, :, part], address_ref[0, :, part], content_ref[0, :, part]
        upstream = upstream_ref[:, 0, :, part].reshape(length, LANES)
        lanes = lax.broadcasted_iota(jnp.int32, query.shape, 1)
        query_delta = jnp.zeros(query.shape, single)
        address_delta = jnp.zeros(address.shape, single)
        content_delta = jnp.zeros(address.shape, single)
        for head in range(LANES // HD):
            own, weights = head_weights(causal, places, query, address, lanes, head)
            weight_delta = outer_rows(jnp.where(own, upstream, jnp.zeros_like(upstream)), content)
            score_delta = (
                weights * (weight_delta - jnp.sum(weights * weight_delta, -1, keepdims=True))
            ).astype(bfloat)
            query_delta = jnp.where(own, matmul(score_delta, address), query_delta)
            address_delta = jnp.where(own, inner_rows(score_delta, query), address_delta)
            content_delta = jnp.where(own, inner_rows(weights.astype(bfloat), upstream), content_delta)
        query_sum[sums_ref[step], :, part] += query_delta * 0.125
        address_sum[stores_ref[step], :, part] += address_delta * 0.125
        content_sum[stores_ref[step], :, part] += content_delta

    @pl.when(step == pl.num_programs(0) - 1)
    def finish():
        query_out[...] = query_sum[...].astype(bfloat)
        address_out[...] = address_sum[...].astype(bfloat)
        content_out[...] = content_sum[...].astype(bfloat)


def attend_backward(queries, addresses, contents, upstream, bins, stores, sums, places=()):
    count = bins.shape[0]
    length, width = queries.shape[1:]
    stored = addresses.shape[1]
    whole = lambda shape: pl.BlockSpec(shape, lambda i, b, s, t: (0,) * len(shape))
    return pl.pallas_call(
        functools.partial(attend_backward_kernel, bool(places)),
        grid_spec=pltpu.PrefetchScalarGridSpec(
            num_scalar_prefetch=3,
            grid=(count,),
            in_specs=[
                pl.BlockSpec((1, length, width), lambda i, b, s, t: (b[i], 0, 0)),
                pl.BlockSpec((1, stored, width), lambda i, b, s, t: (s[i], 0, 0)),
                pl.BlockSpec((1, stored, width), lambda i, b, s, t: (s[i], 0, 0)),
                pl.BlockSpec((upstream.shape[0], 1) + upstream.shape[2:], lambda i, b, s, t: (0, i, 0, 0)),
            ]
            + [whole(place.shape) for place in places],
            out_specs=[whole(queries.shape), whole(addresses.shape), whole(addresses.shape)],
            scratch_shapes=[
                pltpu.VMEM(queries.shape, single),
                pltpu.VMEM(addresses.shape, single),
                pltpu.VMEM(addresses.shape, single),
            ],
        ),
        out_shape=[
            jax.ShapeDtypeStruct(queries.shape, bfloat),
            jax.ShapeDtypeStruct(addresses.shape, bfloat),
            jax.ShapeDtypeStruct(addresses.shape, bfloat),
        ],
        compiler_params=pltpu.CompilerParams(
            dimension_semantics=("arbitrary",), vmem_limit_bytes=56 * 1024 * 1024
        ),
        cost_estimate=BRIEF,
        name="attend_backward",
    )(bins, stores, sums, queries, addresses, contents, upstream, *places)


def pick_kernel(bins_ref, value_ref, out_ref):
    out_ref[...] = value_ref[...]


def pick(value, bins):
    block = (1,) + value.shape[1:]
    return pl.pallas_call(
        pick_kernel,
        grid_spec=pltpu.PrefetchScalarGridSpec(
            num_scalar_prefetch=1,
            grid=(bins.shape[0],),
            in_specs=[pl.BlockSpec(block, lambda i, b: (b[i], 0, 0))],
            out_specs=pl.BlockSpec(block, lambda i, b: (i, 0, 0)),
        ),
        out_shape=jax.ShapeDtypeStruct(bins.shape + value.shape[1:], value.dtype),
        name="pick",
    )(bins, value)


def finish_kernel(count, *refs):
    base = 0
    for index in range(count):
        rows = refs[index].shape[0]
        refs[-1][base : base + rows, :] = refs[index][...].astype(single) + refs[count + index][
            ...
        ].astype(single)
        base += rows


def finish_sums(kept, arrived):
    total = sum(part.shape[0] for part in kept)
    whole = pl.BlockSpec(memory_space=pltpu.VMEM)
    return pl.pallas_call(
        functools.partial(finish_kernel, len(kept)),
        in_specs=[whole] * (2 * len(kept)),
        out_specs=whole,
        out_shape=jax.ShapeDtypeStruct((total, kept[0].shape[1]), single),
        compiler_params=pltpu.CompilerParams(vmem_limit_bytes=40 * 1024 * 1024),
        name="finish_sums",
    )(*kept, *arrived)


def marginal_objective(seq_values, doc_scores, member, length):
    joint = doc_scores + seq_values / length
    masked = jnp.where(member, joint[None, :], -1e30)
    top = jnp.max(masked, 1, keepdims=True)
    unscaled = jnp.where(member, jnp.exp(masked - top), 0.0)
    total = jnp.sum(unscaled, 1, keepdims=True)
    marginal = top[:, 0] + jnp.log(total[:, 0])
    posterior = unscaled / total
    entropy = -jnp.sum(jnp.where(member, posterior * (joint[None, :] - marginal[:, None]), 0.0), 1)
    return jnp.mean(-marginal + ENTROPY_WEIGHT * entropy)


def on_device(
    dp,
    mp,
    targets,
    labels,
    passages,
    slot_question,
    slot_passage,
    score_table,
    score_index,
    query_weight,
    query_bias,
    key_weight,
    value_weight,
    value_bias,
    output_weight,
    output_bias,
    first_gain,
    first_shift,
    probe_weight,
    probe_bias,
    address_weight,
    content_weight,
    content_bias,
    merged_weight,
    merged_bias,
    second_gain,
    second_shift,
    expand_weight,
    expand_bias,
    shrink_weight,
    shrink_bias,
    third_gain,
    third_shift,
    embedding,
):
    group = lax.axis_index("dp")
    member_index = lax.axis_index("mp")
    own_questions, length, width = targets.shape
    questions = own_questions * dp
    pair_count = slot_passage.shape[0]
    store_count, passage_length = (passages.shape[0], passages.shape[1])
    vocab_share = embedding.shape[0]
    local_width = query_weight.shape[1]
    quarter = length // mp
    assert own_questions == 1

    token = [score_table[0]]

    def through(*values):
        values = tie(*values, token[0])
        token[0] = values[-1]
        return values[:-1] if len(values) > 2 else values[0]

    mp_order = bits_of(mp)[::-1]
    mp_table = relative_of(mp_order)
    dp_bits = bits_of(dp)
    dp_order = dp_bits[::-1]
    dp_table = relative_of(dp_order)

    def to_own(rows, count):
        natural = rows.reshape((count, mp, quarter) + rows.shape[2:])
        return jnp.moveaxis(xor_take(mp_table, member_index, natural, 1), 1, 0)

    def to_natural(rows, count):
        shaped = rows.reshape((mp, count, quarter) + rows.shape[1:])
        return jnp.moveaxis(natural_order(mp_table, member_index, shaped, 0), 0, 1)

    def mp_scatter_steps(halves):
        assert len(mp_order) == 2
        sent, kept = through(*halves)
        arrived = swap(sent, "mp", mp, mp_order[1])
        yield None
        sent, kept = through(*add_halves(kept, through(arrived)))
        arrived = swap(sent, "mp", mp, mp_order[0])
        yield None
        yield kept, through(arrived)

    def mp_gather_steps(own):
        own = through(own)
        held = [own, swap(own, "mp", mp, mp_order[0]), swap(own, "mp", mp, mp_order[1])]
        yield None
        held[1] = through(held[1])
        held.append(swap(held[1], "mp", mp, mp_order[1]))
        yield None
        yield through(*held)

    def last(steps):
        for value in steps:
            pass
        return value

    my_questions = lax.dynamic_slice_in_dim(slot_question, group * pair_count, pair_count)
    every = jnp.arange(own_questions, dtype=jnp.int32)
    quarters = member_index ^ jnp.asarray(mp_table, jnp.int32)
    place = (
        quarters[:, None] * quarter + jnp.arange(quarter, dtype=jnp.int32)[None, :]
    ).reshape(length)
    places_of = (
        jnp.broadcast_to(place[:, None], (length, LANES)),
        jnp.broadcast_to(place[None, :], (8, length)),
    )
    inputs = to_own(targets, own_questions)

    def by_question(rows):
        return jnp.moveaxis(rows.reshape(mp, own_questions, quarter, -1), 0, 1).reshape(
            own_questions, length, -1
        )

    inputs = inputs.reshape(-1, width)
    self_queries = by_question((matmul(inputs, query_weight) + query_bias).astype(bfloat))
    self_addresses = by_question(matmul(inputs, key_weight).astype(bfloat))
    self_contents = by_question((matmul(inputs, value_weight) + value_bias).astype(bfloat))
    self_flat = attend_forward(
        self_queries, self_addresses, self_contents, every, every, mp, places_of
    ).reshape(-1, local_width)
    kept, arrived = last(mp_scatter_steps(product_halves([self_flat], [output_weight])))
    first_in, first_norm, first_low = norm_forward(
        kept, arrived, inputs[:quarter], output_bias, first_gain, first_shift
    )
    first_full, probe_own = project(last(mp_gather_steps(first_low)), probe_weight, probe_bias)
    probe_own = by_question(probe_own)

    def where_slots(order):
        spots = jnp.asarray(places(relative_of(order)), jnp.int32)
        return spots[group ^ (my_questions // own_questions)] * own_questions + (
            my_questions % own_questions
        )

    probe_order = dp_bits[::-1]
    first_order = dp_bits[:1] + dp_bits[:0:-1]
    probe_bins = where_slots(probe_order)
    first_bins = where_slots(first_order)
    probe_all, first_all = gather_both(
        (probe_own, first_low.reshape(own_questions, quarter, width)),
        "dp",
        dp,
        (probe_order, first_order),
    )
    probe_all = probe_all.reshape(questions, length, local_width)
    first_all = first_all.reshape(questions, quarter, width)
    passage_rows = passages.reshape(-1, width)
    stored_addresses = matmul(passage_rows, address_weight).astype(bfloat)
    stored_contents = (matmul(passage_rows, content_weight) + content_bias).astype(bfloat)
    stored_addresses = stored_addresses.reshape(store_count, passage_length, local_width)
    stored_contents = stored_contents.reshape(store_count, passage_length, local_width)
    pair_labels = to_own(jnp.take(labels, my_questions, axis=0, mode="clip"), pair_count).reshape(-1)
    local_index = pair_labels - member_index * vocab_share
    inside = (local_index >= 0) & (local_index < vocab_share)
    label_rows = jnp.take(embedding, jnp.clip(local_index, 0, vocab_share - 1), axis=0, mode="clip")
    probe_all, label_rows = lax.optimization_barrier((probe_all, label_rows))

    cross_flat = attend_forward(
        probe_all, stored_addresses, stored_contents, probe_bins, slot_passage, mp
    ).reshape(-1, local_width)
    first_slots = pick(first_all, first_bins).reshape(-1, width)
    kept, arrived = last(mp_scatter_steps(product_halves([cross_flat], [merged_weight])))
    second_in, second_norm, low = norm_forward(
        kept, arrived, first_slots, merged_bias, second_gain, second_shift
    )
    second_low, expanded, activated, sent, kept = feed_forward(
        last(mp_gather_steps(low)), expand_weight, expand_bias, shrink_weight
    )
    kept, arrived = last(mp_scatter_steps((sent, kept)))
    third_in, third_norm, low = norm_forward(
        kept, arrived, second_norm, shrink_bias, third_gain, third_shift
    )
    third_low = jnp.concatenate(last(mp_gather_steps(low)), 0)

    label_lanes = jnp.broadcast_to(local_index[:, None], (local_index.shape[0], LANES))
    entry_weights, entry_sums, entry_mix, entry_tops = vocab_forward(third_low, embedding, label_lanes)
    entry_tile = vocab_tile(vocab_share)
    local_top = entry_tops[:, vocab_share // entry_tile - 1]
    local_target = jnp.where(
        inside, jnp.sum(third_low.astype(single) * label_rows.astype(single), -1), 0.0
    )
    local_total = jnp.sum(entry_sums, -1) + jnp.where(inside, jnp.exp(local_target - local_top), 0.0)
    stats = jnp.stack([local_top, local_total, local_target]).reshape(3, mp, pair_count, quarter)
    for index, bit in reversed(list(enumerate(mp_order))):
        other = swap(stats, "mp", mp, bit)
        other = jnp.flip(
            other.reshape(3, mp >> (index + 1), 2, 1 << index, pair_count, quarter), 2
        ).reshape(stats.shape)
        high = jnp.maximum(stats[0], other[0])
        sums = stats[1] * jnp.exp(stats[0] - high) + other[1] * jnp.exp(other[0] - high)
        stats = jnp.stack([high, sums, stats[2] + other[2]])
    log_norm = (stats[0] + jnp.log(stats[1])).reshape(-1)
    target_logit = stats[2].reshape(-1)
    pair_likelihood = jnp.sum((target_logit - log_norm).reshape(mp, pair_count, quarter), -1)
    while pair_likelihood.shape[0] > 1:
        pair_likelihood = pair_likelihood[0::2] + pair_likelihood[1::2]
    every_likelihood = natural_order(
        dp_table, group, gather_blocks(pair_likelihood[0], "dp", dp, dp_order), 0
    ).reshape(-1)
    doc_scores = jnp.take(score_table, score_index)
    member = slot_question[None, :] == jnp.arange(questions, dtype=jnp.int32)[:, None]

    def scored(values_all):
        return marginal_objective(values_all, doc_scores, member, length)

    objective, pullback = jax.vjp(scored, every_likelihood)
    likelihood_delta = pullback(jnp.ones_like(objective) * (questions * length))[0]
    pair_delta = lax.dynamic_slice_in_dim(likelihood_delta, group * pair_count, pair_count)
    row_delta = jnp.broadcast_to(pair_delta[None, :, None], (mp, pair_count, quarter)).reshape(-1)
    surplus = row_delta * (1.0 - jnp.exp(target_logit - log_norm))
    factors = -row_delta[:, None] * jnp.exp(entry_tops - log_norm[:, None])
    third_part = (
        jnp.where(inside, surplus, 0.0)[:, None] * label_rows.astype(single)
        - (row_delta * jnp.exp(local_top - log_norm))[:, None] * entry_mix
    )

    fast = width % (dp * LANES) == 0

    def order_table(order):
        if not fast:
            return jnp.arange(width // LANES, dtype=jnp.int32)
        return group ^ jnp.asarray(relative_of(order), jnp.int32)

    token[0] = objective

    class ColumnSum:
        def __init__(self, halves, order):
            self.sent, self.kept = through(*halves)
            self.bits = order[::-1]
            self.arrived = None

        def send(self):
            if fast:
                self.sent = through(self.sent)
                self.arrived = swap(self.sent, "dp", dp, self.bits[0])
                self.bits = self.bits[1:]

        def step(self):
            if not fast or not self.bits:
                return
            self.arrived, self.kept = through(self.arrived, self.kept)
            half = self.kept.shape[1] // 2
            total = self.kept.astype(single) + self.arrived.astype(single)
            self.sent, self.kept = total[:, half:].astype(bfloat), total[:, :half].astype(bfloat)
            self.send()

        def wait(self):
            if fast:
                self.arrived = through(self.arrived)

    def finish(parts):
        if not fast:
            slopes = [
                lax.psum_scatter(
                    jnp.concatenate([part.kept, part.sent], 1), "dp", scatter_dimension=1, tiled=True
                )
                for part in parts
            ]
            return jnp.concatenate(slopes, 0).astype(single)
        assert not any(part.bits for part in parts)
        return finish_sums([part.kept for part in parts], [part.arrived for part in parts])

    order_a = dp_bits[::-1]
    order_b = order_a if dp < 4 else [dp_bits[-1], dp_bits[0]] + dp_bits[1:-1]
    slope_tile = entry_tile // 2 if entry_tile % (2 * LANES) == 0 else entry_tile
    tiles = vocab_share // slope_tile
    cuts = [tiles * i // 14 for i in (0, 3, 6, 10, 14)]
    def table_sum(index, order):
        halves = vocab_slope(
            entry_weights,
            through(factors),
            local_index[:, None],
            surplus[:, None],
            third_low,
            order_table(order),
            cuts[index],
            cuts[index + 1] - cuts[index],
            slope_tile,
        )
        return ColumnSum(halves, order)

    def group_sum(pairs, order):
        pairs = [(through(pairs[0][0]), pairs[0][1])] + pairs[1:]
        return ColumnSum(slope_group(pairs, order_table(order)), order)

    half = third_part.shape[0] // 2
    steps = mp_scatter_steps((third_part[half:].astype(bfloat), third_part[:half]))
    next(steps)
    sum_a1 = table_sum(0, order_a)
    sum_a1.send()
    next(steps)
    sum_b = table_sum(1, order_b)
    sum_b.send()
    third_back, feed_low, third_sums = norm_backward(next(steps), third_in, third_gain)
    steps = mp_gather_steps(feed_low)
    next(steps)
    sum_a2 = table_sum(2, order_a)
    sum_a2.send()
    next(steps)
    feed_delta, expanded_delta, bias_expand, sent, kept = feed_backward(
        next(steps), expand_weight, shrink_weight, expanded
    )
    steps = mp_scatter_steps((sent, kept))
    next(steps)
    next(steps)
    sum_a1.step()
    sum_f = group_sum([(activated, feed_delta), (expanded_delta, second_low)], order_b)
    second_back, recall_low, second_sums = norm_backward(
        next(steps) + (third_back,), second_in, second_gain
    )
    steps = mp_gather_steps(recall_low)
    next(steps)
    sum_b.step()
    sum_a3 = table_sum(3, order_a)
    next(steps)
    recall_delta, mixed_delta = project(
        next(steps), merged_weight, jnp.zeros((local_width,), single), True
    )
    probe_binned, address_delta, content_delta = attend_backward(
        probe_all,
        stored_addresses,
        stored_contents,
        mixed_delta.reshape(mp, pair_count, quarter, local_width),
        probe_bins,
        slot_passage,
        probe_bins,
    )
    address_delta = address_delta.reshape(-1, local_width)
    content_delta = content_delta.reshape(-1, local_width)

    half = questions // 2
    steps = scatter_both_steps(
        (
            (
                probe_binned[half:].reshape(-1, local_width),
                probe_binned[:half].reshape(-1, local_width),
            ),
            tuple(
                value.reshape(-1, width)
                for value in bin_rows(
                    second_back.reshape(pair_count, quarter, width), probe_bins, questions
                )
            ),
        ),
        "dp",
        dp,
        (probe_order, probe_order),
        through,
    )
    next(steps)
    sum_a1.step()
    sum_a2.step()
    sum_a3.send()
    sum_x = group_sum(
        [
            (cross_flat, recall_delta),
            (address_delta, passage_rows),
            (content_delta, passage_rows),
        ],
        order_b,
    )
    next(steps)
    sum_f.send()
    sum_b.step()
    sum_a1.wait()
    for unused in range(len(dp_bits) - 2):
        next(steps)
    sum_a2.step()
    sum_x.send()
    probe_parts, state_parts = next(steps)
    probe_flat = (
        probe_parts[0].astype(single) + probe_parts[1].astype(single)
    ).astype(bfloat)

    bias_content = jnp.sum(content_delta, 0, dtype=single)
    passages_slope = lax.psum(
        (outer_rows(address_delta, address_weight) + outer_rows(content_delta, content_weight)).astype(bfloat),
        "mp",
    ).astype(single).reshape(passages.shape)

    bias_probe = jnp.sum(probe_flat, 0, dtype=single)
    steps = mp_scatter_steps(product_halves([probe_flat], [probe_weight], True))
    next(steps)
    next(steps)
    sum_b.wait()
    first_back, self_low, first_sums = norm_backward(
        next(steps) + tuple(state_parts), first_in, first_gain
    )
    steps = mp_gather_steps(self_low)
    next(steps)
    sum_f.step()
    next(steps)
    self_delta, self_mixed_delta = project(
        next(steps), output_weight, jnp.zeros((local_width,), single), True
    )
    self_deltas = attend_backward(
        self_queries,
        self_addresses,
        self_contents,
        self_mixed_delta.reshape(mp, own_questions, quarter, local_width),
        every,
        every,
        every,
        places_of,
    )
    query_flat, key_flat, value_flat = (
        jnp.moveaxis(delta.reshape(own_questions, mp, quarter, local_width), 1, 0).reshape(
            -1, local_width
        )
        for delta in self_deltas
    )
    steps = mp_scatter_steps(
        product_halves(
            [query_flat, key_flat, value_flat], [query_weight, key_weight, value_weight], True
        )
    )
    shared = total_over(
        jnp.concatenate([first_sums, second_sums, third_sums], 0), "mp", mp, mp_order
    )
    bias_query = jnp.sum(query_flat, 0, dtype=single)
    bias_value = jnp.sum(value_flat, 0, dtype=single)
    quads = jnp.stack([bias_query, bias_value, bias_probe, bias_content])
    quads = quads.reshape(4, dp, local_width // dp).swapaxes(0, 1).reshape(1, width)
    vectors = jnp.concatenate([shared, bias_expand, quads, jnp.zeros((5, width), single)], 0)
    next(steps)
    sum_a3.step()
    next(steps)
    sum_s = group_sum(
        [
            (probe_flat, first_full),
            (self_flat, self_delta),
            (query_flat, inputs),
            (key_flat, inputs),
            (value_flat, inputs),
            (jnp.eye(16, dtype=bfloat), vectors.astype(bfloat)),
        ],
        order_a,
    )
    kept, arrived = next(steps)
    input_low = (kept + arrived.astype(single) + first_back).astype(bfloat)
    steps = mp_gather_steps(input_low)
    next(steps)
    sum_s.send()
    next(steps)
    targets_slope = to_natural(jnp.concatenate(next(steps), 0), own_questions)
    targets_slope = targets_slope.reshape(targets.shape).astype(single)

    sum_a2.wait()
    sum_x.step()
    sum_f.step()
    sum_a3.step()
    sum_s.step()
    sum_x.step()
    sum_s.step()
    sum_f.wait()
    sum_a3.wait()
    sum_x.wait()
    sum_s.wait()
    embedding_slope = finish([sum_a1, sum_b, sum_a2, sum_a3])
    feed_slopes = finish([sum_f])
    cross_slopes = finish([sum_x])
    self_slopes = finish([sum_s])
    hidden = expanded.shape[1]
    shrink_slope = feed_slopes[:hidden]
    expand_slope = feed_slopes[hidden:].T
    merged_slope = cross_slopes[:local_width]
    address_slope = cross_slopes[local_width : 2 * local_width].T
    content_slope = cross_slopes[2 * local_width :].T
    probe_slope = self_slopes[:local_width].T
    output_slope = self_slopes[local_width : 2 * local_width]
    query_slope = self_slopes[2 * local_width : 3 * local_width].T
    key_slope = self_slopes[3 * local_width : 4 * local_width].T
    value_slope = self_slopes[4 * local_width : 5 * local_width].T

    vectors = self_slopes[5 * local_width :]
    (
        bias_output,
        first_gain_slope,
        first_shift_slope,
        bias_merged,
        second_gain_slope,
        second_shift_slope,
        bias_shrink,
        third_gain_slope,
        third_shift_slope,
        bias_expand,
    ) = (vectors[i] for i in range(10))
    bias_query, bias_value, bias_probe, bias_content = vectors[10].reshape(4, local_width // dp)
    return (
        token[0],
        targets_slope,
        passages_slope,
        query_slope,
        bias_query,
        key_slope,
        value_slope,
        bias_value,
        output_slope,
        bias_output,
        first_gain_slope,
        first_shift_slope,
        probe_slope,
        bias_probe,
        address_slope,
        content_slope,
        bias_content,
        merged_slope,
        bias_merged,
        second_gain_slope,
        second_shift_slope,
        expand_slope,
        bias_expand,
        shrink_slope,
        bias_shrink,
        third_gain_slope,
        third_shift_slope,
        embedding_slope,
    )


def solution(mesh):
    return jax.shard_map(
        functools.partial(on_device, mesh.shape["dp"], mesh.shape["mp"]),
        mesh=mesh,
        in_specs=(
            P("dp", None, None),
            P(),
            P("dp", None, None),
            P(),
            P("dp"),
            P(),
            P(),
            P(None, "mp"),
            P("mp"),
            P(None, "mp"),
            P(None, "mp"),
            P("mp"),
            P("mp", None),
            P(),
            P(),
            P(),
            P(None, "mp"),
            P("mp"),
            P(None, "mp"),
            P(None, "mp"),
            P("mp"),
            P("mp", None),
            P(),
            P(),
            P(),
            P(None, "mp"),
            P("mp"),
            P("mp", None),
            P(),
            P(),
            P(),
            P("mp", None),
        ),
        out_specs=(
            P(),
            P("dp", None, None),
            P("dp", None, None),
            P("dp", "mp"),
            P(("mp", "dp")),
            P("dp", "mp"),
            P("dp", "mp"),
            P(("mp", "dp")),
            P("mp", "dp"),
            P("dp"),
            P("dp"),
            P("dp"),
            P("dp", "mp"),
            P(("mp", "dp")),
            P("dp", "mp"),
            P("dp", "mp"),
            P(("mp", "dp")),
            P("mp", "dp"),
            P("dp"),
            P("dp"),
            P("dp"),
            P("dp", "mp"),
            P(("mp", "dp")),
            P("mp", "dp"),
            P("dp"),
            P("dp"),
            P("dp"),
            P("mp", "dp"),
        ),
        check_vma=False,
    )
```

```python
import functools

import jax
import jax.numpy as jnp
from jax import lax
from jax.experimental import pallas as pl
from jax.experimental.pallas import tpu as pltpu
from jax.sharding import PartitionSpec as P

HD = 64
LANES = 128
EPSILON = 1e-05
ENTROPY_WEIGHT = 0.5
BRIEF = pl.CostEstimate(flops=0, bytes_accessed=0, transcendentals=0)
bfloat = jnp.bfloat16

CUTS = (0, 2, 4, 7)
ORDERS = {"f": "z", "p": "y", "s": "y"}
PLAN = (
    (),
    (("a", "make"), ("a", "send"),),
    (("b", "make"), ("b", "send"),),
    (),
    (("a", "add"),),
    (("f", "make"), ("f", "send"),),
    (),
    (("c", "make"),),
    (),
    (),
    (("t", "step"), ("b", "add"), ("f", "add"),),
    (("t", "step"),),
    (("a", "send"), ("b", "send"),),
    (("c", "send"), ("t", "step"), ("f", "send"),),
    (),
    (),
    (),
    (),
    (("p", "make"), ("p", "send"), ("a", "add"), ("a", "send"),),
    (("s", "make"), ("s", "send"),),
    (("c", "add"), ("c", "send"), ("b", "add"), ("b", "send"),),
    (),
    (("f", "add"), ("f", "send"), ("p", "add"), ("p", "send"), ("c", "add"), ("c", "send"), ("s", "add"), ("s", "send"), ("a", "wait"), ("b", "wait"), ("p", "add"), ("p", "send"), ("f", "wait"), ("s", "add"), ("s", "send"), ("c", "wait"), ("p", "wait"), ("s", "wait"),),
)
single = jnp.float32


def matmul(left, right):
    return jnp.dot(left, right, preferred_element_type=single)


def inner_rows(left, right):
    return lax.dot_general(left, right, (((0,), (0,)), ((), ())), preferred_element_type=single)


def outer_rows(left, right):
    return lax.dot_general(left, right, (((1,), (1,)), ((), ())), preferred_element_type=single)


def bits_of(count):
    bits = []
    while (1 << len(bits)) < count:
        bits.append(1 << len(bits))
    return bits


def swap(value, axis, count, bit):
    return lax.ppermute(value, axis, [(i, i ^ bit) for i in range(count)])


def relative_of(order):
    table = [0]
    for bit in order:
        table = table + [r ^ bit for r in table]
    return table


def gather_blocks(own, axis, count, order):
    held = own[None]
    for bit in order:
        held = jnp.concatenate([held, swap(held, axis, count, bit)], 0)
    return held


def scatter_blocks(parts, axis, count, order):
    for bit in reversed(order):
        half = parts.shape[0] // 2
        arrived = swap(parts[half:].astype(bfloat), axis, count, bit)
        parts = parts[:half] + arrived.astype(single)
    return parts[0]


def tie(*values):
    return lax.optimization_barrier(values)


def gather_both(owns, axis, count, orders):
    helds = [own[None] for own in owns]
    for bits in zip(*orders):
        arrived = tie(*(swap(held, axis, count, bit) for held, bit in zip(helds, bits)))
        helds = [jnp.concatenate([held, more], 0) for held, more in zip(helds, arrived)]
    return helds


def total_over(value, axis, count, order):
    for bit in order:
        value = value + swap(value, axis, count, bit)
    return value


def xor_take(table, me, array, axis):
    return jnp.take(array, me ^ jnp.asarray(table, jnp.int32), axis=axis, mode="clip")


def places(table):
    inverse = [0] * len(table)
    for position, relative in enumerate(table):
        inverse[relative] = position
    return inverse


def natural_order(table, me, array, axis):
    count = len(table)
    order = jnp.asarray(places(table), jnp.int32)[me ^ jnp.arange(count, dtype=jnp.int32)]
    return jnp.take(array, order, axis=axis, mode="clip")


VMEM = pl.BlockSpec(memory_space=pltpu.VMEM)


def run_whole(kernel, name, outs, *operands, scratch=()):
    return pl.pallas_call(
        kernel,
        in_specs=[VMEM] * len(operands),
        out_specs=[VMEM] * len(outs),
        out_shape=[jax.ShapeDtypeStruct(shape, dtype) for shape, dtype in outs],
        scratch_shapes=list(scratch),
        compiler_params=pltpu.CompilerParams(vmem_limit_bytes=56 * 1024 * 1024),
        cost_estimate=BRIEF,
        name=name,
    )(*operands)


def row(vector):
    return vector.reshape(1, -1).astype(single)


def norm_forward_kernel(kept_ref, arrived_ref, state_ref, bias_ref, gain_ref, shift_ref, in_ref, out_ref, low_ref):
    hidden = (
        state_ref[...].astype(single)
        + (kept_ref[...].astype(single) + arrived_ref[...].astype(single))
        + bias_ref[...]
    )
    in_ref[...] = hidden
    center = hidden - jnp.mean(hidden, -1, keepdims=True)
    spread = jnp.mean(center * center, -1, keepdims=True)
    normal = center * lax.rsqrt(spread + EPSILON) * gain_ref[...] + shift_ref[...]
    out_ref[...] = normal
    low_ref[...] = normal.astype(bfloat)


def norm_forward(kept, arrived, state, bias, gain, shift):
    shape = state.shape
    return run_whole(
        norm_forward_kernel,
        "norm_forward",
        [(shape, single), (shape, single), (shape, bfloat)],
        kept.reshape(shape),
        arrived.reshape(shape),
        state,
        row(bias),
        row(gain),
        row(shift),
    )


def norm_backward_kernel(count, *refs):
    hidden_ref, gain_ref, out_ref, low_ref, sums_ref = refs[count:]
    upstream = refs[0][...].astype(single)
    for ref in refs[1:count]:
        upstream = upstream + ref[...].astype(single)
    hidden = hidden_ref[...]
    center = hidden - jnp.mean(hidden, -1, keepdims=True)
    spread = jnp.mean(center * center, -1, keepdims=True)
    inverse = lax.rsqrt(spread + EPSILON)
    normal = center * inverse
    scaled = upstream * gain_ref[...]
    delta = inverse * (
        scaled
        - jnp.mean(scaled, -1, keepdims=True)
        - normal * jnp.mean(scaled * normal, -1, keepdims=True)
    )
    low = delta.astype(bfloat)
    out_ref[...] = delta
    low_ref[...] = low
    sums_ref[0:1, :] = jnp.sum(low.astype(single), 0, keepdims=True)
    sums_ref[1:2, :] = jnp.sum(upstream * normal, 0, keepdims=True)
    sums_ref[2:3, :] = jnp.sum(upstream, 0, keepdims=True)


def norm_backward(parts, hidden, gain):
    shape = hidden.shape
    return run_whole(
        functools.partial(norm_backward_kernel, len(parts)),
        "norm_backward",
        [(shape, single), (shape, bfloat), ((3, shape[1]), single)],
        *(part.reshape(shape) for part in parts),
        hidden,
        row(gain),
    )


def erf_gelu(value):
    phi = 0.5 * (1.0 + lax.erf(value * 0.7071067811865476))
    return value * phi, phi


def join(pieces, full_ref):
    rows = pieces[0].shape[0]
    for index, piece in enumerate(pieces):
        full_ref[index * rows : (index + 1) * rows, :] = piece[...]


def feed_forward_kernel(count, *refs):
    expand_ref, bias_ref, shrink_ref, full_ref, hidden_ref, act_ref, sent_ref, kept_ref = refs[count:]
    join(refs[:count], full_ref)
    half = sent_ref.shape[0]
    for index in (1, 0):
        part = slice(index * half, (index + 1) * half)
        hidden = matmul(full_ref[part, :], expand_ref[...]) + bias_ref[...]
        hidden_ref[part, :] = hidden
        act = erf_gelu(hidden)[0].astype(bfloat)
        act_ref[part, :] = act
        out = matmul(act, shrink_ref[...])
        if index == 0:
            kept_ref[...] = out
        else:
            sent_ref[...] = out.astype(bfloat)


def feed_forward(pieces, expand, bias, shrink):
    rows, width = len(pieces) * pieces[0].shape[0], pieces[0].shape[1]
    hidden = expand.shape[1]
    return run_whole(
        functools.partial(feed_forward_kernel, len(pieces)),
        "feed_forward",
        [
            ((rows, width), bfloat),
            ((rows, hidden), single),
            ((rows, hidden), bfloat),
            ((rows // 2, width), bfloat),
            ((rows // 2, width), single),
        ],
        *pieces,
        expand,
        row(bias),
        shrink,
    )


def feed_backward_kernel(count, *refs):
    expand_ref, shrink_ref, hidden_ref, full_ref, delta_ref, sums_ref, sent_ref, kept_ref = refs[count:]
    join(refs[:count], full_ref)
    half = sent_ref.shape[0]
    sums = jnp.zeros(sums_ref.shape, single)
    for index in (1, 0):
        part = slice(index * half, (index + 1) * half)
        upstream = outer_rows(full_ref[part, :], shrink_ref[...])
        hidden = hidden_ref[part, :]
        slope = erf_gelu(hidden)[1] + hidden * jnp.exp(-0.5 * hidden * hidden) * 0.3989422804014327
        delta = (upstream * slope).astype(bfloat)
        delta_ref[part, :] = delta
        sums = sums + jnp.sum(delta.astype(single), 0, keepdims=True)
        out = outer_rows(delta, expand_ref[...])
        if index == 0:
            kept_ref[...] = out
        else:
            sent_ref[...] = out.astype(bfloat)
    sums_ref[...] = sums


def feed_backward(pieces, expand, shrink, hidden):
    rows, width = len(pieces) * pieces[0].shape[0], pieces[0].shape[1]
    return run_whole(
        functools.partial(feed_backward_kernel, len(pieces)),
        "feed_backward",
        [
            ((rows, width), bfloat),
            (hidden.shape, bfloat),
            ((1, hidden.shape[1]), single),
            ((rows // 2, width), bfloat),
            ((rows // 2, width), single),
        ],
        *pieces,
        expand,
        shrink,
        hidden,
    )


def project_kernel(count, transposed, *refs):
    weight_ref, bias_ref, full_ref, out_ref = refs[count:]
    join(refs[:count], full_ref)
    out = (outer_rows if transposed else matmul)(full_ref[...], weight_ref[...])
    out_ref[...] = (out + bias_ref[...]).astype(bfloat)


def project(pieces, weight, bias, transposed=False):
    rows, width = len(pieces) * pieces[0].shape[0], pieces[0].shape[1]
    return run_whole(
        functools.partial(project_kernel, len(pieces), transposed),
        "project",
        [((rows, width), bfloat), ((rows, bias.shape[0]), bfloat)],
        *pieces,
        weight,
        row(bias),
    )


def halves_kernel(count, transposed, *refs):
    lefts, weights, (sent_ref, kept_ref) = refs[:count], refs[count : 2 * count], refs[2 * count :]
    half = sent_ref.shape[0]
    product = outer_rows if transposed else matmul
    for part, out in ((slice(half, 2 * half), sent_ref), (slice(0, half), kept_ref)):
        total = product(lefts[0][part, :], weights[0][...])
        for left, weight in zip(lefts[1:], weights[1:]):
            total = total + product(left[part, :], weight[...])
        out[...] = total.astype(out.dtype)


def product_halves(lefts, weights, transposed=False):
    half = lefts[0].shape[0] // 2
    width = weights[0].shape[0] if transposed else weights[0].shape[1]
    return run_whole(
        functools.partial(halves_kernel, len(lefts), transposed),
        "product_halves",
        [((half, width), bfloat), ((half, width), single)],
        *lefts,
        *weights,
    )


def add_halves_kernel(kept_ref, arrived_ref, sent_ref, left_ref):
    half = kept_ref.shape[0] // 2
    sent_ref[...] = (kept_ref[half:, :].astype(single) + arrived_ref[half:, :].astype(single)).astype(bfloat)
    left_ref[...] = kept_ref[:half, :].astype(single) + arrived_ref[:half, :].astype(single)


def add_halves(kept, arrived):
    half, width = kept.shape[0] // 2, kept.shape[1]
    return run_whole(
        add_halves_kernel,
        "add_halves",
        [((half, width), bfloat), ((half, width), single)],
        kept,
        arrived,
    )


def add_columns_kernel(kept_ref, arrived_ref, sent_ref, left_ref):
    half = sent_ref.shape[1]
    total = kept_ref[...].astype(single) + arrived_ref[...].astype(single)
    sent_ref[...] = total[:, half:].astype(bfloat)
    left_ref[...] = total[:, :half].astype(bfloat)


def add_columns(kept, arrived):
    rows, width = kept.shape
    block = rows
    for count in (4, 3, 2):
        if rows % (16 * count) == 0:
            block = rows // count
            break
    whole = pl.BlockSpec((block, width), lambda i: (i, 0))
    half = pl.BlockSpec((block, width // 2), lambda i: (i, 0))
    return pl.pallas_call(
        add_columns_kernel,
        grid=(rows // block,),
        in_specs=[whole, whole],
        out_specs=[half, half],
        out_shape=[jax.ShapeDtypeStruct((rows, width // 2), bfloat)] * 2,
        cost_estimate=BRIEF,
        name="add_columns",
    )(kept, arrived)


def bin_rows_kernel(bins_ref, value_ref, sent_ref, kept_ref, sums):
    sums[...] = jnp.zeros_like(sums)
    for slot in range(value_ref.shape[0]):
        sums[bins_ref[slot]] += value_ref[slot]
    half = sent_ref.shape[0]
    sent_ref[...] = sums[half:].astype(bfloat)
    kept_ref[...] = sums[:half]


def bin_rows(value, bins, count):
    shape = (count // 2,) + value.shape[1:]
    return pl.pallas_call(
        bin_rows_kernel,
        in_specs=[pl.BlockSpec(memory_space=pltpu.SMEM), VMEM],
        out_specs=[VMEM, VMEM],
        out_shape=[jax.ShapeDtypeStruct(shape, bfloat), jax.ShapeDtypeStruct(shape, single)],
        scratch_shapes=[pltpu.VMEM((count,) + value.shape[1:], single)],
        compiler_params=pltpu.CompilerParams(vmem_limit_bytes=56 * 1024 * 1024),
        cost_estimate=BRIEF,
        name="bin_rows",
    )(bins, value)


def vocab_tile(vocab_share):
    for tile in (1792, 896, 512, 256, 128):
        if vocab_share % tile == 0:
            return tile
    return vocab_share


def vocab_forward_kernel(state_ref, table_ref, label_ref, weight_ref, sum_ref, mixed_ref, tops_ref, top):
    step = pl.program_id(0)
    rows = state_ref.shape[0]
    tile = table_ref.shape[0]
    block = min(rows, 1024)

    @pl.when(step == 0)
    def start():
        top[...] = jnp.full_like(top, -jnp.inf)
        sum_ref[...] = jnp.zeros_like(sum_ref)
        mixed_ref[...] = jnp.zeros_like(mixed_ref)
        tops_ref[...] = jnp.zeros_like(tops_ref)

    repeat = lambda value, count: jnp.concatenate([value] * count, 1) if count > 1 else value
    spans = tile // LANES
    for index in range(rows // block):
        part = pl.ds(index * block, block)
        logits = outer_rows(state_ref[part, :], table_ref[...])
        old = top[part, :]
        new = jnp.maximum(old, jnp.max(logits, -1, keepdims=True))
        lanes = lax.broadcasted_iota(jnp.int32, new.shape, 1)
        offset = label_ref[part, :] - step * tile
        shrink = jnp.exp(old - new)
        top[part, :] = new
        tops_ref[part, :] = jnp.where(lanes == step, new, tops_ref[part, :])
        sums = sum_ref[part, :] * shrink
        low = []
        for span in range(spans):
            weights = jnp.exp(logits[:, span * LANES : (span + 1) * LANES] - new)
            weights = jnp.where(lanes + span * LANES == offset, 0.0, weights)
            sums = sums + weights
            low.append(weights.astype(bfloat))
        sum_ref[part, :] = sums
        low = jnp.concatenate(low, 1)
        weight_ref[part, :] = low
        mixed_ref[part, :] = mixed_ref[part, :] * repeat(shrink, mixed_ref.shape[1] // LANES) + matmul(
            low, table_ref[...]
        )


def vocab_forward(states, table, label):
    rows, width = states.shape
    entries = table.shape[0]
    tile = vocab_tile(entries)
    whole = lambda *shape: pl.BlockSpec(shape, lambda i: (0,) * len(shape))
    return pl.pallas_call(
        vocab_forward_kernel,
        grid=(entries // tile,),
        in_specs=[
            whole(rows, width),
            pl.BlockSpec((tile, width), lambda i: (i, 0)),
            whole(rows, LANES),
        ],
        out_specs=[
            pl.BlockSpec((rows, tile), lambda i: (0, i)),
            whole(rows, LANES),
            whole(rows, width),
            whole(rows, LANES),
        ],
        out_shape=[
            jax.ShapeDtypeStruct((rows, entries), bfloat),
            jax.ShapeDtypeStruct((rows, LANES), single),
            jax.ShapeDtypeStruct((rows, width), single),
            jax.ShapeDtypeStruct((rows, LANES), single),
        ],
        scratch_shapes=[pltpu.VMEM((rows, LANES), single)],
        compiler_params=pltpu.CompilerParams(
            dimension_semantics=("arbitrary",), vmem_limit_bytes=56 * 1024 * 1024
        ),
        cost_estimate=BRIEF,
        name="vocab_forward",
    )(states, table, label)


def vocab_slope_kernel(first, ratio, order_ref, weight_ref, factor_ref, label_ref, patch_ref, state_ref, sent_ref, kept_ref, moved):
    step = pl.program_id(0)
    tile = weight_ref.shape[1]
    width = state_ref.shape[1]
    blocks = order_ref.shape[0]
    span = width // blocks

    @pl.when(step == 0)
    def start():
        for place in range(blocks):
            source = pl.multiple_of(order_ref[place] * span, span)
            moved[:, place * span : (place + 1) * span] = state_ref[:, pl.ds(source, span)]

    here = step + first
    factors = factor_ref[...]
    lanes = lax.broadcasted_iota(jnp.int32, factors.shape, 1)
    factor = jnp.sum(jnp.where(lanes == here // ratio, factors, 0.0), -1, keepdims=True)
    columns = lax.broadcasted_iota(jnp.int32, weight_ref.shape, 1) + here * tile
    delta = jnp.where(
        columns == label_ref[...], patch_ref[...], weight_ref[...].astype(single) * factor
    ).astype(bfloat)
    half = width // 2
    slope = inner_rows(delta, moved[...])
    sent_ref[...] = slope[:, half:].astype(bfloat)
    kept_ref[...] = slope[:, :half].astype(bfloat)


def vocab_slope(weights, factors, label, patch, states, order, first, count, tile):
    rows, width = states.shape
    whole = lambda *shape: pl.BlockSpec(shape, lambda i, o: (0,) * len(shape))
    half = pl.BlockSpec((tile, width // 2), lambda i, o: (i, 0))
    return pl.pallas_call(
        functools.partial(vocab_slope_kernel, first, vocab_tile(weights.shape[1]) // tile),
        grid_spec=pltpu.PrefetchScalarGridSpec(
            num_scalar_prefetch=1,
            grid=(count,),
            in_specs=[
                pl.BlockSpec((rows, tile), lambda i, o: (0, i + first)),
                whole(rows, LANES),
                whole(rows, 1),
                whole(rows, 1),
                whole(rows, width),
            ],
            out_specs=[half, half],
            scratch_shapes=[pltpu.VMEM((rows, width), bfloat)],
        ),
        out_shape=[jax.ShapeDtypeStruct((count * tile, width // 2), bfloat)] * 2,
        compiler_params=pltpu.CompilerParams(
            dimension_semantics=("arbitrary",), vmem_limit_bytes=56 * 1024 * 1024
        ),
        cost_estimate=BRIEF,
        name="vocab_slope",
    )(order, weights, factors, label, patch, states)


def slope_group_kernel(count, order_ref, *refs):
    lefts, rights = refs[:count], refs[count : 2 * count]
    sent_ref, kept_ref, moved = refs[2 * count :]
    blocks = order_ref.shape[0]
    width = rights[0].shape[1]
    span, half = width // blocks, width // 2
    base = 0
    for index in range(count):
        rows, entries = lefts[index].shape
        if index == 0 or rights[index] is not rights[index - 1]:
            for place in range(blocks):
                source = pl.multiple_of(order_ref[place] * span, span)
                moved[:rows, place * span : (place + 1) * span] = rights[index][:, pl.ds(source, span)]
        right = moved[:rows, :]
        left = lefts[index][...]
        slope = inner_rows(left, right)
        sent_ref[base : base + entries, :] = slope[:, half:].astype(bfloat)
        kept_ref[base : base + entries, :] = slope[:, :half].astype(bfloat)
        base += entries


def slope_group(pairs, order):
    width = pairs[0][1].shape[1]
    total = sum(left.shape[1] for left, right in pairs)
    rows = max(left.shape[0] for left, right in pairs)
    lefts = [left for left, right in pairs]
    rights = [right for left, right in pairs]
    whole = pl.BlockSpec(memory_space=pltpu.VMEM)
    return pl.pallas_call(
        functools.partial(slope_group_kernel, len(pairs)),
        in_specs=[pl.BlockSpec(memory_space=pltpu.SMEM)] + [whole] * (2 * len(pairs)),
        out_specs=[whole, whole],
        out_shape=[jax.ShapeDtypeStruct((total, width // 2), bfloat)] * 2,
        scratch_shapes=[pltpu.VMEM((rows, width), bfloat)],
        compiler_params=pltpu.CompilerParams(vmem_limit_bytes=56 * 1024 * 1024),
        cost_estimate=BRIEF,
        name="slope_group",
    )(order, *lefts, *rights)


def head_weights(causal, places, query, address, lanes, head):
    own = (lanes // HD) == head
    scores = outer_rows(jnp.where(own, query, jnp.zeros_like(query)), address) * 0.125
    if causal:
        scores = jnp.where(places[0][:, :1] >= places[1][:1, :], scores, -1000000000.0)
    expo = jnp.exp(scores - jnp.max(scores, -1, keepdims=True))
    return own, expo / jnp.sum(expo, -1, keepdims=True)


def attend_forward_kernel(causal, bins_ref, stores_ref, query_ref, address_ref, content_ref, *refs):
    mixed_ref = refs[-1]
    places = [ref[...] for ref in refs[:-1]]
    length, width = query_ref.shape[1:]
    for pair in range(width // LANES):
        part = slice(pair * LANES, (pair + 1) * LANES)
        query, address, content = query_ref[0, :, part], address_ref[0, :, part], content_ref[0, :, part]
        lanes = lax.broadcasted_iota(jnp.int32, query.shape, 1)
        total = jnp.zeros(query.shape, single)
        for head in range(LANES // HD):
            own, weights = head_weights(causal, places, query, address, lanes, head)
            total = jnp.where(own, matmul(weights.astype(bfloat), content), total)
        shape = (mixed_ref.shape[0], mixed_ref.shape[2], LANES)
        mixed_ref[:, 0, :, part] = total.astype(bfloat).reshape(shape)


def attend_forward(queries, addresses, contents, bins, stores, parts, places=()):
    count = bins.shape[0]
    length, width = queries.shape[1:]
    stored = addresses.shape[1]
    return pl.pallas_call(
        functools.partial(attend_forward_kernel, bool(places)),
        grid_spec=pltpu.PrefetchScalarGridSpec(
            num_scalar_prefetch=2,
            grid=(count,),
            in_specs=[
                pl.BlockSpec((1, length, width), lambda i, b, s: (b[i], 0, 0)),
                pl.BlockSpec((1, stored, width), lambda i, b, s: (s[i], 0, 0)),
                pl.BlockSpec((1, stored, width), lambda i, b, s: (s[i], 0, 0)),
            ]
            + [pl.BlockSpec(place.shape, lambda i, b, s: (0, 0)) for place in places],
            out_specs=pl.BlockSpec((parts, 1, length // parts, width), lambda i, b, s: (0, i, 0, 0)),
        ),
        out_shape=jax.ShapeDtypeStruct((parts, count, length // parts, width), bfloat),
        compiler_params=pltpu.CompilerParams(
            dimension_semantics=("arbitrary",), vmem_limit_bytes=32 * 1024 * 1024
        ),
        cost_estimate=BRIEF,
        name="attend_forward",
    )(bins, stores, queries, addresses, contents, *places)


def attend_backward_kernel(
    causal, bins_ref, stores_ref, sums_ref, query_ref, address_ref, content_ref, upstream_ref, *refs
):
    query_out, address_out, content_out, query_sum, address_sum, content_sum = refs[-6:]
    places = [ref[...] for ref in refs[:-6]]
    step = pl.program_id(0)
    length, width = query_ref.shape[1:]

    @pl.when(step == 0)
    def start():
        query_sum[...] = jnp.zeros_like(query_sum)
        address_sum[...] = jnp.zeros_like(address_sum)
        content_sum[...] = jnp.zeros_like(content_sum)

    for pair in range(width // LANES):
        part = slice(pair * LANES, (pair + 1) * LANES)
        query, address, content = query_ref[0, :, part], address_ref[0, :, part], content_ref[0, :, part]
        upstream = upstream_ref[:, 0, :, part].reshape(length, LANES)
        lanes = lax.broadcasted_iota(jnp.int32, query.shape, 1)
        query_delta = jnp.zeros(query.shape, single)
        address_delta = jnp.zeros(address.shape, single)
        content_delta = jnp.zeros(address.shape, single)
        for head in range(LANES // HD):
            own, weights = head_weights(causal, places, query, address, lanes, head)
            weight_delta = outer_rows(jnp.where(own, upstream, jnp.zeros_like(upstream)), content)
            score_delta = (
                weights * (weight_delta - jnp.sum(weights * weight_delta, -1, keepdims=True))
            ).astype(bfloat)
            query_delta = jnp.where(own, matmul(score_delta, address), query_delta)
            address_delta = jnp.where(own, inner_rows(score_delta, query), address_delta)
            content_delta = jnp.where(own, inner_rows(weights.astype(bfloat), upstream), content_delta)
        query_sum[sums_ref[step], :, part] += query_delta * 0.125
        address_sum[stores_ref[step], :, part] += address_delta * 0.125
        content_sum[stores_ref[step], :, part] += content_delta

    @pl.when(step == pl.num_programs(0) - 1)
    def finish():
        query_out[...] = query_sum[...].astype(bfloat)
        address_out[...] = address_sum[...].astype(bfloat)
        content_out[...] = content_sum[...].astype(bfloat)


def attend_backward(queries, addresses, contents, upstream, bins, stores, sums, places=()):
    count = bins.shape[0]
    length, width = queries.shape[1:]
    stored = addresses.shape[1]
    whole = lambda shape: pl.BlockSpec(shape, lambda i, b, s, t: (0,) * len(shape))
    return pl.pallas_call(
        functools.partial(attend_backward_kernel, bool(places)),
        grid_spec=pltpu.PrefetchScalarGridSpec(
            num_scalar_prefetch=3,
            grid=(count,),
            in_specs=[
                pl.BlockSpec((1, length, width), lambda i, b, s, t: (b[i], 0, 0)),
                pl.BlockSpec((1, stored, width), lambda i, b, s, t: (s[i], 0, 0)),
                pl.BlockSpec((1, stored, width), lambda i, b, s, t: (s[i], 0, 0)),
                pl.BlockSpec((upstream.shape[0], 1) + upstream.shape[2:], lambda i, b, s, t: (0, i, 0, 0)),
            ]
            + [whole(place.shape) for place in places],
            out_specs=[whole(queries.shape), whole(addresses.shape), whole(addresses.shape)],
            scratch_shapes=[
                pltpu.VMEM(queries.shape, single),
                pltpu.VMEM(addresses.shape, single),
                pltpu.VMEM(addresses.shape, single),
            ],
        ),
        out_shape=[
            jax.ShapeDtypeStruct(queries.shape, bfloat),
            jax.ShapeDtypeStruct(addresses.shape, bfloat),
            jax.ShapeDtypeStruct(addresses.shape, bfloat),
        ],
        compiler_params=pltpu.CompilerParams(
            dimension_semantics=("arbitrary",), vmem_limit_bytes=56 * 1024 * 1024
        ),
        cost_estimate=BRIEF,
        name="attend_backward",
    )(bins, stores, sums, queries, addresses, contents, upstream, *places)


def pick_kernel(bins_ref, value_ref, out_ref):
    out_ref[...] = value_ref[...]


def pick(value, bins):
    block = (1,) + value.shape[1:]
    return pl.pallas_call(
        pick_kernel,
        grid_spec=pltpu.PrefetchScalarGridSpec(
            num_scalar_prefetch=1,
            grid=(bins.shape[0],),
            in_specs=[pl.BlockSpec(block, lambda i, b: (b[i], 0, 0))],
            out_specs=pl.BlockSpec(block, lambda i, b: (i, 0, 0)),
        ),
        out_shape=jax.ShapeDtypeStruct(bins.shape + value.shape[1:], value.dtype),
        name="pick",
    )(bins, value)


def finish_kernel(count, *refs):
    base = 0
    for index in range(count):
        rows = refs[index].shape[0]
        refs[-1][base : base + rows, :] = refs[index][...].astype(single) + refs[count + index][
            ...
        ].astype(single)
        base += rows


def finish_sums(kept, arrived):
    total = sum(part.shape[0] for part in kept)
    whole = pl.BlockSpec(memory_space=pltpu.VMEM)
    return pl.pallas_call(
        functools.partial(finish_kernel, len(kept)),
        in_specs=[whole] * (2 * len(kept)),
        out_specs=whole,
        out_shape=jax.ShapeDtypeStruct((total, kept[0].shape[1]), single),
        compiler_params=pltpu.CompilerParams(vmem_limit_bytes=40 * 1024 * 1024),
        name="finish_sums",
    )(*kept, *arrived)


def order_columns_kernel(count, order_ref, *refs):
    pieces, (joined_ref, moved_ref) = refs[:count], refs[count:]
    rows, width = pieces[0].shape
    span = width // order_ref.shape[0]
    for index in range(count):
        part = slice(index * rows, (index + 1) * rows)
        joined_ref[part, :] = pieces[index][...]
        for place in range(order_ref.shape[0]):
            source = pl.multiple_of(order_ref[place] * span, span)
            moved_ref[part, place * span : (place + 1) * span] = pieces[index][:, pl.ds(source, span)]


def order_columns(pieces, order):
    shape = (len(pieces) * pieces[0].shape[0], pieces[0].shape[1])
    return pl.pallas_call(
        functools.partial(order_columns_kernel, len(pieces)),
        in_specs=[pl.BlockSpec(memory_space=pltpu.SMEM)] + [VMEM] * len(pieces),
        out_specs=[VMEM, VMEM],
        out_shape=[jax.ShapeDtypeStruct(shape, bfloat)] * 2,
        compiler_params=pltpu.CompilerParams(vmem_limit_bytes=40 * 1024 * 1024),
        cost_estimate=BRIEF,
        name="order_columns",
    )(order, *pieces)


def half_slope_kernel(
    first,
    ratio,
    base_ref,
    weight_ref,
    table_ref,
    factor_ref,
    label_ref,
    patch_ref,
    far_ref,
    far_norm_ref,
    far_scale_ref,
    far_label_ref,
    moved_ref,
    far_moved_ref,
    sent_ref,
    kept_ref,
    delta,
):
    rows, tile = weight_ref.shape
    here = base_ref[0] + first + pl.program_id(0)
    factors = factor_ref[...]
    lanes = lax.broadcasted_iota(jnp.int32, factors.shape, 1)
    factor = jnp.sum(jnp.where(lanes == here // ratio, factors, 0.0), -1, keepdims=True)
    columns = lax.broadcasted_iota(jnp.int32, weight_ref.shape, 1) + here * tile
    logits = outer_rows(far_ref[...], table_ref[...])
    delta[:rows, :] = jnp.where(
        columns == label_ref[...], patch_ref[...], weight_ref[...].astype(single) * factor
    ).astype(bfloat)
    hit = jnp.where(columns == far_label_ref[...], 1.0, 0.0)
    delta[rows:, :] = (far_scale_ref[...] * (hit - jnp.exp(logits - far_norm_ref[...]))).astype(bfloat)
    slope = inner_rows(delta[:rows, :], moved_ref[...]) + inner_rows(delta[rows:, :], far_moved_ref[...])
    half = sent_ref.shape[1]
    sent_ref[...] = slope[:, half:].astype(bfloat)
    kept_ref[...] = slope[:, :half].astype(bfloat)


def half_slope(base, weights, table, factors, label, patch, far, far_norm, far_scale, far_label, moved, far_moved, first, count, tile):
    rows, width = far.shape
    whole = lambda *shape: pl.BlockSpec(shape, lambda i, b: (0,) * len(shape))
    half = pl.BlockSpec((tile, width // 2), lambda i, b: (i, 0))
    return pl.pallas_call(
        functools.partial(half_slope_kernel, first, vocab_tile(weights.shape[1]) // tile),
        grid_spec=pltpu.PrefetchScalarGridSpec(
            num_scalar_prefetch=1,
            grid=(count,),
            in_specs=[
                pl.BlockSpec((rows, tile), lambda i, b: (0, i + first + b[0])),
                pl.BlockSpec((tile, width), lambda i, b: (i + first + b[0], 0)),
                whole(rows, LANES),
                whole(rows, 1),
                whole(rows, 1),
                whole(rows, width),
                whole(rows, 1),
                whole(rows, 1),
                whole(rows, 1),
                whole(rows, width),
                whole(rows, width),
            ],
            out_specs=[half, half],
            scratch_shapes=[pltpu.VMEM((2 * rows, tile), bfloat)],
        ),
        out_shape=[jax.ShapeDtypeStruct((count * tile, width // 2), bfloat)] * 2,
        compiler_params=pltpu.CompilerParams(
            dimension_semantics=("arbitrary",), vmem_limit_bytes=56 * 1024 * 1024
        ),
        cost_estimate=BRIEF,
        name="half_slope",
    )(base, weights, table, factors, label, patch, far, far_norm, far_scale, far_label, moved, far_moved)


def place_halves_kernel(count, side_ref, *refs):
    out_ref = refs[-1]
    half = out_ref.shape[0] // 2
    for group, side in ((refs[:count], side_ref[0]), (refs[count : 2 * count], 1 - side_ref[0])):
        offset = 0
        for ref in group:
            rows = ref.shape[0]
            start = pl.multiple_of(side * half + offset, LANES)
            out_ref[pl.ds(start, rows), :] = ref[...].astype(single)
            offset += rows


def place_halves(side, own, other):
    total = sum(part.shape[0] for part in own) * 2
    return pl.pallas_call(
        functools.partial(place_halves_kernel, len(own)),
        in_specs=[pl.BlockSpec(memory_space=pltpu.SMEM)] + [VMEM] * (2 * len(own)),
        out_specs=VMEM,
        out_shape=jax.ShapeDtypeStruct((total, own[0].shape[1]), single),
        compiler_params=pltpu.CompilerParams(vmem_limit_bytes=40 * 1024 * 1024),
        cost_estimate=BRIEF,
        name="place_halves",
    )(side, *own, *other)


def marginal_objective(seq_values, doc_scores, member, length):
    joint = doc_scores + seq_values / length
    masked = jnp.where(member, joint[None, :], -1e30)
    top = jnp.max(masked, 1, keepdims=True)
    unscaled = jnp.where(member, jnp.exp(masked - top), 0.0)
    total = jnp.sum(unscaled, 1, keepdims=True)
    marginal = top[:, 0] + jnp.log(total[:, 0])
    posterior = unscaled / total
    entropy = -jnp.sum(jnp.where(member, posterior * (joint[None, :] - marginal[:, None]), 0.0), 1)
    return jnp.mean(-marginal + ENTROPY_WEIGHT * entropy)


def on_device(
    dp,
    mp,
    targets,
    labels,
    passages,
    slot_question,
    slot_passage,
    score_table,
    score_index,
    query_weight,
    query_bias,
    key_weight,
    value_weight,
    value_bias,
    output_weight,
    output_bias,
    first_gain,
    first_shift,
    probe_weight,
    probe_bias,
    address_weight,
    content_weight,
    content_bias,
    merged_weight,
    merged_bias,
    second_gain,
    second_shift,
    expand_weight,
    expand_bias,
    shrink_weight,
    shrink_bias,
    third_gain,
    third_shift,
    embedding,
):
    group = lax.axis_index("dp")
    member_index = lax.axis_index("mp")
    own_questions, length, width = targets.shape
    questions = own_questions * dp
    pair_count = slot_passage.shape[0]
    store_count, passage_length = (passages.shape[0], passages.shape[1])
    vocab_share = embedding.shape[0]
    local_width = query_weight.shape[1]
    quarter = length // mp
    assert own_questions == 1

    token = [score_table]

    def through(*values):
        values = tie(*values, token[0])
        token[0] = values[-1]
        return values[:-1] if len(values) > 2 else values[0]

    mp_order = bits_of(mp)[::-1]
    mp_table = relative_of(mp_order)
    dp_bits = bits_of(dp)
    dp_order = dp_bits[::-1]
    dp_table = relative_of(dp_order)
    fast = dp >= 4 and width % (dp * LANES) == 0
    far = dp_bits[-1]

    def to_own(rows, count):
        natural = rows.reshape((count, mp, quarter) + rows.shape[2:])
        return jnp.moveaxis(xor_take(mp_table, member_index, natural, 1), 1, 0)

    def to_natural(rows, count):
        shaped = rows.reshape((mp, count, quarter) + rows.shape[1:])
        return jnp.moveaxis(natural_order(mp_table, member_index, shaped, 0), 0, 1)

    def mp_scatter_steps(halves):
        assert len(mp_order) == 2
        sent, kept = through(*halves)
        arrived = swap(sent, "mp", mp, mp_order[1])
        yield None
        sent, kept = through(*add_halves(kept, through(arrived)))
        arrived = swap(sent, "mp", mp, mp_order[0])
        yield None
        yield kept, through(arrived)

    def mp_gather_steps(own):
        own = through(own)
        held = [own, swap(own, "mp", mp, mp_order[0]), swap(own, "mp", mp, mp_order[1])]
        yield None
        held[1] = through(held[1])
        held.append(swap(held[1], "mp", mp, mp_order[1]))
        yield None
        yield through(*held)

    def dp_scatter_steps(halves, order):
        for bit in reversed(order):
            sent, kept = through(*halves)
            arrived = swap(sent, "dp", dp, bit)
            yield None
            if bit == order[0]:
                yield kept, through(arrived)
            else:
                halves = add_halves(kept, through(arrived))

    def last(steps):
        for value in steps:
            pass
        return value

    my_questions = lax.dynamic_slice_in_dim(slot_question, group * pair_count, pair_count)
    every = jnp.arange(own_questions, dtype=jnp.int32)
    quarters = member_index ^ jnp.asarray(mp_table, jnp.int32)
    place = (
        quarters[:, None] * quarter + jnp.arange(quarter, dtype=jnp.int32)[None, :]
    ).reshape(length)
    places_of = (
        jnp.broadcast_to(place[:, None], (length, LANES)),
        jnp.broadcast_to(place[None, :], (8, length)),
    )
    inputs = to_own(targets, own_questions)

    def by_question(rows):
        return jnp.moveaxis(rows.reshape(mp, own_questions, quarter, -1), 0, 1).reshape(
            own_questions, length, -1
        )

    inputs = inputs.reshape(-1, width)
    self_queries = by_question((matmul(inputs, query_weight) + query_bias).astype(bfloat))
    self_addresses = by_question(matmul(inputs, key_weight).astype(bfloat))
    self_contents = by_question((matmul(inputs, value_weight) + value_bias).astype(bfloat))
    self_flat = attend_forward(
        self_queries, self_addresses, self_contents, every, every, mp, places_of
    ).reshape(-1, local_width)
    kept, arrived = last(mp_scatter_steps(product_halves([self_flat], [output_weight])))
    first_in, first_norm, first_low = norm_forward(
        kept, arrived, inputs[:quarter], output_bias, first_gain, first_shift
    )
    first_full, probe_own = project(last(mp_gather_steps(first_low)), probe_weight, probe_bias)
    probe_own = by_question(probe_own)

    def where_slots(order):
        spots = jnp.asarray(places(relative_of(order)), jnp.int32)
        return spots[group ^ (my_questions // own_questions)] * own_questions + (
            my_questions % own_questions
        )

    probe_order = dp_bits[::-1]
    return_order = dp_bits[:1] + dp_bits[:0:-1]
    return_bins = where_slots(return_order)
    state_order = probe_order
    state_bins = where_slots(state_order)
    first_order = dp_bits[:1] + dp_bits[:0:-1]
    probe_bins = where_slots(probe_order)
    first_bins = where_slots(first_order)
    probe_all, first_all = gather_both(
        (probe_own, first_low.reshape(own_questions, quarter, width)),
        "dp",
        dp,
        (probe_order, first_order),
    )
    probe_all = probe_all.reshape(questions, length, local_width)
    first_all = first_all.reshape(questions, quarter, width)
    passage_rows = passages.reshape(-1, width)
    stored_addresses = matmul(passage_rows, address_weight).astype(bfloat)
    stored_contents = (matmul(passage_rows, content_weight) + content_bias).astype(bfloat)
    stored_addresses = stored_addresses.reshape(store_count, passage_length, local_width)
    stored_contents = stored_contents.reshape(store_count, passage_length, local_width)

    def label_index(slots):
        wanted = to_own(jnp.take(labels, slots, axis=0, mode="clip"), pair_count).reshape(-1)
        return wanted - member_index * vocab_share

    local_index = label_index(my_questions)
    inside = (local_index >= 0) & (local_index < vocab_share)
    label_rows = jnp.take(embedding, jnp.clip(local_index, 0, vocab_share - 1), axis=0, mode="clip")
    probe_all, label_rows = lax.optimization_barrier((probe_all, label_rows))

    cross_flat = attend_forward(
        probe_all, stored_addresses, stored_contents, probe_bins, slot_passage, mp
    ).reshape(-1, local_width)
    first_slots = pick(first_all, first_bins).reshape(-1, width)
    kept, arrived = last(mp_scatter_steps(product_halves([cross_flat], [merged_weight])))
    second_in, second_norm, low = norm_forward(
        kept, arrived, first_slots, merged_bias, second_gain, second_shift
    )
    second_low, expanded, activated, sent, kept = feed_forward(
        last(mp_gather_steps(low)), expand_weight, expand_bias, shrink_weight
    )
    kept, arrived = last(mp_scatter_steps((sent, kept)))
    third_in, third_norm, low = norm_forward(
        kept, arrived, second_norm, shrink_bias, third_gain, third_shift
    )
    def order_table(order):
        if not fast:
            return jnp.arange(width // LANES, dtype=jnp.int32)
        return group ^ jnp.asarray(relative_of(order), jnp.int32)

    order_a = dp_bits[::-1]
    order_b = order_a if dp < 4 else [dp_bits[-1], dp_bits[0]] + dp_bits[1:-1]
    third_low, third_moved = order_columns(last(mp_gather_steps(low)), order_table(order_a))
    far_low = swap(through(low), "dp", dp, far)


    label_lanes = jnp.broadcast_to(local_index[:, None], (local_index.shape[0], LANES))
    third_low = through(third_low)
    entry_weights, entry_sums, entry_mix, entry_tops = vocab_forward(third_low, embedding, label_lanes)
    entry_tops, entry_sums, entry_mix, far_low = through(
        entry_tops, entry_sums, entry_mix, far_low
    )
    entry_tile = vocab_tile(vocab_share)
    local_top = entry_tops[:, vocab_share // entry_tile - 1]
    local_target = jnp.where(
        inside, jnp.sum(third_low.astype(single) * label_rows.astype(single), -1), 0.0
    )
    local_total = jnp.sum(entry_sums, -1) + jnp.where(inside, jnp.exp(local_target - local_top), 0.0)
    stats = jnp.stack([local_top, local_total, local_target]).reshape(3, mp, pair_count, quarter)
    for index, bit in reversed(list(enumerate(mp_order))):
        other = swap(stats, "mp", mp, bit)
        other = jnp.flip(
            other.reshape(3, mp >> (index + 1), 2, 1 << index, pair_count, quarter), 2
        ).reshape(stats.shape)
        high = jnp.maximum(stats[0], other[0])
        sums = stats[1] * jnp.exp(stats[0] - high) + other[1] * jnp.exp(other[0] - high)
        stats = jnp.stack([high, sums, stats[2] + other[2]])
    log_norm = (stats[0] + jnp.log(stats[1])).reshape(-1)
    target_logit = stats[2].reshape(-1)
    pair_likelihood = jnp.sum((target_logit - log_norm).reshape(mp, pair_count, quarter), -1)
    while pair_likelihood.shape[0] > 1:
        pair_likelihood = pair_likelihood[0::2] + pair_likelihood[1::2]
    far_steps = mp_gather_steps(far_low)
    next(far_steps)
    shared = jnp.concatenate([pair_likelihood[0], log_norm])
    arrived = swap(shared, "dp", dp, far)
    far_norm = arrived[pair_count:]
    every_likelihood = jnp.stack([shared[:pair_count], arrived[:pair_count]])
    for bit in dp_order[1:]:
        every_likelihood = jnp.concatenate(
            [every_likelihood, swap(every_likelihood, "dp", dp, bit)], 0
        )
    every_likelihood = natural_order(dp_table, group, every_likelihood, 0).reshape(-1)
    next(far_steps)
    far_third, far_moved = order_columns(next(far_steps), order_table(order_a))
    doc_scores = jnp.take(token[0], score_index)
    member = slot_question[None, :] == jnp.arange(questions, dtype=jnp.int32)[:, None]

    def scored(values_all):
        return marginal_objective(values_all, doc_scores, member, length)

    objective, pullback = jax.vjp(scored, every_likelihood)
    likelihood_delta = pullback(jnp.ones_like(objective) * (questions * length))[0]
    pair_delta = lax.dynamic_slice_in_dim(likelihood_delta, group * pair_count, pair_count)

    def by_row(values):
        return jnp.broadcast_to(values[None, :, None], (mp, pair_count, quarter)).reshape(-1)

    row_delta = by_row(pair_delta)
    far_group = group ^ far
    far_delta = by_row(
        lax.dynamic_slice_in_dim(likelihood_delta, far_group * pair_count, pair_count)
    )
    far_label = label_index(
        lax.dynamic_slice_in_dim(slot_question, far_group * pair_count, pair_count)
    )
    surplus = row_delta * (1.0 - jnp.exp(target_logit - log_norm))
    factors = -row_delta[:, None] * jnp.exp(entry_tops - log_norm[:, None])
    third_part = (
        jnp.where(inside, surplus, 0.0)[:, None] * label_rows.astype(single)
        - (row_delta * jnp.exp(local_top - log_norm))[:, None] * entry_mix
    )

    token[0] = objective

    class ColumnSum:
        def __init__(self, halves, order):
            self.sent, self.kept = through(*halves)
            self.bits = order[::-1]
            self.arrived = None

        def send(self):
            if fast:
                self.sent = through(self.sent)
                self.arrived = swap(self.sent, "dp", dp, self.bits[0])
                self.bits = self.bits[1:]

        def add(self):
            if fast:
                self.arrived, self.kept = through(self.arrived, self.kept)
                self.sent, self.kept = add_columns(self.kept, self.arrived)

        def step(self):
            self.add()
            self.send()

        def wait(self):
            if fast:
                self.arrived = through(self.arrived)

    def finish(parts):
        if not fast:
            slopes = [
                lax.psum_scatter(
                    jnp.concatenate([part.kept, part.sent], 1), "dp", scatter_dimension=1, tiled=True
                )
                for part in parts
            ]
            return jnp.concatenate(slopes, 0).astype(single)
        assert not any(part.bits for part in parts)
        return finish_sums([part.kept for part in parts], [part.arrived for part in parts])

    slope_tile = entry_tile // 2 if entry_tile % (2 * LANES) == 0 else entry_tile
    side = (group // far).astype(jnp.int32).reshape(1)
    tiles = vocab_share // slope_tile // 2 if fast else vocab_share // slope_tile
    cuts = [-(-tiles * i // 7) for i in CUTS]

    def table_sum(index):
        first, count = cuts[index], cuts[index + 1] - cuts[index]
        if fast:
            halves = half_slope(
                side * tiles,
                entry_weights,
                embedding,
                through(factors),
                local_index[:, None],
                surplus[:, None],
                far_third,
                far_norm[:, None],
                far_delta[:, None],
                far_label[:, None],
                third_moved,
                far_moved,
                first,
                count,
                slope_tile,
            )
        else:
            halves = vocab_slope(
                entry_weights,
                through(factors),
                local_index[:, None],
                surplus[:, None],
                third_low,
                order_table(order_a),
                first,
                count,
                slope_tile,
            )
        return ColumnSum(halves, order_a)

    def group_sum(pairs, order):
        pairs = [(through(pairs[0][0]), pairs[0][1])] + pairs[1:]
        return ColumnSum(slope_group(pairs, order_table(order)), order)

    sums = {}
    makers = {
        "a": lambda: table_sum(0),
        "b": lambda: table_sum(1),
        "c": lambda: table_sum(2),
        "f": lambda: group_sum(
            [(activated, feed_delta), (expanded_delta, second_low)], orders[ORDERS["f"]]
        ),
        "p": lambda: group_sum(
            [
                (cross_flat, recall_delta),
                (address_delta, passage_rows),
                (content_delta, passage_rows),
                (probe_flat, first_full),
                (self_flat, self_delta),
            ],
            orders[ORDERS["p"]],
        ),
        "s": lambda: group_sum(
            [
                (query_flat, inputs),
                (key_flat, inputs),
                (value_flat, inputs),
                (jnp.eye(16, dtype=bfloat), vectors.astype(bfloat)),
            ],
            orders[ORDERS["s"]],
        ),
    }
    orders = {"y": order_a, "z": order_b}

    def at(point):
        for name, action in PLAN[point]:
            if name == "t":
                next(state_steps)
            elif action == "make":
                sums[name] = makers[name]()
            else:
                getattr(sums[name], action)()

    half = third_part.shape[0] // 2
    steps = mp_scatter_steps((third_part[half:].astype(bfloat), third_part[:half]))
    next(steps)
    at(0)
    next(steps)
    at(1)
    third_back, feed_low, third_sums = norm_backward(next(steps), third_in, third_gain)
    steps = mp_gather_steps(feed_low)
    next(steps)
    at(2)
    next(steps)
    at(3)
    feed_delta, expanded_delta, bias_expand, sent, kept = feed_backward(
        next(steps), expand_weight, shrink_weight, expanded
    )
    steps = mp_scatter_steps((sent, kept))
    next(steps)
    at(4)
    next(steps)
    at(5)
    parts = next(steps)
    at(6)
    second_back, recall_low, second_sums = norm_backward(
        parts + (third_back,), second_in, second_gain
    )
    steps = mp_gather_steps(recall_low)
    next(steps)
    state_steps = dp_scatter_steps(
        tuple(
            value.reshape(-1, width)
            for value in bin_rows(
                second_back.reshape(pair_count, quarter, width), state_bins, questions
            )
        ),
        state_order,
    )
    at(7)
    next(steps)
    at(8)
    recall_delta, mixed_delta = project(
        next(steps), merged_weight, jnp.zeros((local_width,), single), True
    )
    probe_binned, address_delta, content_delta = attend_backward(
        probe_all,
        stored_addresses,
        stored_contents,
        mixed_delta.reshape(mp, pair_count, quarter, local_width),
        probe_bins,
        slot_passage,
        return_bins,
    )
    address_delta = address_delta.reshape(-1, local_width)
    content_delta = content_delta.reshape(-1, local_width)

    half = questions // 2
    steps = dp_scatter_steps(
        (
            probe_binned[half:].reshape(-1, local_width),
            probe_binned[:half].reshape(-1, local_width),
        ),
        return_order,
    )
    at(9)
    next(steps)
    at(10)
    for unused in range(len(dp_bits) - 2):
        next(steps)
    at(11)
    next(steps)
    at(12)
    probe_parts = next(steps)
    at(13)
    probe_flat = (
        probe_parts[0] + probe_parts[1].astype(single)
    ).astype(bfloat)

    bias_content = jnp.sum(content_delta, 0, dtype=single)
    passages_slope = lax.psum(
        (outer_rows(address_delta, address_weight) + outer_rows(content_delta, content_weight)).astype(bfloat),
        "mp",
    ).astype(single).reshape(passages.shape)

    bias_probe = jnp.sum(probe_flat, 0, dtype=single)
    steps = mp_scatter_steps(product_halves([probe_flat], [probe_weight], True))
    next(steps)
    at(14)
    next(steps)
    at(15)
    state_parts = last(state_steps)
    first_back, self_low, first_sums = norm_backward(
        next(steps) + tuple(state_parts), first_in, first_gain
    )
    steps = mp_gather_steps(self_low)
    next(steps)
    at(16)
    next(steps)
    at(17)
    self_delta, self_mixed_delta = project(
        next(steps), output_weight, jnp.zeros((local_width,), single), True
    )
    self_deltas = attend_backward(
        self_queries,
        self_addresses,
        self_contents,
        self_mixed_delta.reshape(mp, own_questions, quarter, local_width),
        every,
        every,
        every,
        places_of,
    )
    query_flat, key_flat, value_flat = (
        jnp.moveaxis(delta.reshape(own_questions, mp, quarter, local_width), 1, 0).reshape(
            -1, local_width
        )
        for delta in self_deltas
    )
    steps = mp_scatter_steps(
        product_halves(
            [query_flat, key_flat, value_flat], [query_weight, key_weight, value_weight], True
        )
    )
    shared = total_over(
        jnp.concatenate([first_sums, second_sums, third_sums], 0), "mp", mp, mp_order
    )
    bias_query = jnp.sum(query_flat, 0, dtype=single)
    bias_value = jnp.sum(value_flat, 0, dtype=single)
    quads = jnp.stack([bias_query, bias_value, bias_probe, bias_content])
    quads = quads.reshape(4, dp, local_width // dp).swapaxes(0, 1).reshape(1, width)
    vectors = jnp.concatenate([shared, bias_expand, quads, jnp.zeros((5, width), single)], 0)
    next(steps)
    at(18)
    next(steps)
    at(19)
    kept, arrived = next(steps)
    input_low = (kept + arrived.astype(single) + first_back).astype(bfloat)
    steps = mp_gather_steps(input_low)
    next(steps)
    at(20)
    next(steps)
    at(21)
    targets_slope = to_natural(jnp.concatenate(next(steps), 0), own_questions)
    targets_slope = targets_slope.reshape(targets.shape).astype(single)
    at(22)
    table_parts = [sums[name] for name in "abc"]
    if fast:
        embedding_slope = place_halves(
            side, [part.kept for part in table_parts], [part.arrived for part in table_parts]
        )
    else:
        embedding_slope = finish(table_parts)
    feed_slopes = finish([sums["f"]])
    probe_slopes = finish([sums["p"]])
    self_slopes = finish([sums["s"]])
    hidden = expanded.shape[1]

    def parts_of(slopes, counts):
        edges = [sum(counts[:i]) for i in range(len(counts) + 1)]
        return [slopes[a:b] for a, b in zip(edges, edges[1:])]

    shrink_slope, expand_slope = parts_of(feed_slopes, [hidden] * 2)
    merged_slope, address_slope, content_slope, probe_slope, output_slope = parts_of(
        probe_slopes, [local_width] * 5
    )
    query_slope, key_slope, value_slope, vectors = parts_of(self_slopes, [local_width] * 3 + [16])
    expand_slope, address_slope, content_slope = expand_slope.T, address_slope.T, content_slope.T
    probe_slope, query_slope, key_slope, value_slope = (
        slope.T for slope in (probe_slope, query_slope, key_slope, value_slope)
    )
    (
        bias_output,
        first_gain_slope,
        first_shift_slope,
        bias_merged,
        second_gain_slope,
        second_shift_slope,
        bias_shrink,
        third_gain_slope,
        third_shift_slope,
        bias_expand,
    ) = (vectors[i] for i in range(10))
    bias_query, bias_value, bias_probe, bias_content = vectors[10].reshape(4, local_width // dp)
    return (
        token[0],
        targets_slope,
        passages_slope,
        query_slope,
        bias_query,
        key_slope,
        value_slope,
        bias_value,
        output_slope,
        bias_output,
        first_gain_slope,
        first_shift_slope,
        probe_slope,
        bias_probe,
        address_slope,
        content_slope,
        bias_content,
        merged_slope,
        bias_merged,
        second_gain_slope,
        second_shift_slope,
        expand_slope,
        bias_expand,
        shrink_slope,
        bias_shrink,
        third_gain_slope,
        third_shift_slope,
        embedding_slope,
    )


def solution(mesh):
    return jax.shard_map(
        functools.partial(on_device, mesh.shape["dp"], mesh.shape["mp"]),
        mesh=mesh,
        in_specs=(
            P("dp", None, None),
            P(),
            P("dp", None, None),
            P(),
            P("dp"),
            P(),
            P(),
            P(None, "mp"),
            P("mp"),
            P(None, "mp"),
            P(None, "mp"),
            P("mp"),
            P("mp", None),
            P(),
            P(),
            P(),
            P(None, "mp"),
            P("mp"),
            P(None, "mp"),
            P(None, "mp"),
            P("mp"),
            P("mp", None),
            P(),
            P(),
            P(),
            P(None, "mp"),
            P("mp"),
            P("mp", None),
            P(),
            P(),
            P(),
            P("mp", None),
        ),
        out_specs=(
            P(),
            P("dp", None, None),
            P("dp", None, None),
            P("dp", "mp"),
            P(("mp", "dp")),
            P("dp", "mp"),
            P("dp", "mp"),
            P(("mp", "dp")),
            P("mp", "dp"),
            P("dp"),
            P("dp"),
            P("dp"),
            P("dp", "mp"),
            P(("mp", "dp")),
            P("dp", "mp"),
            P("dp", "mp"),
            P(("mp", "dp")),
            P("mp", "dp"),
            P("dp"),
            P("dp"),
            P("dp"),
            P("dp", "mp"),
            P(("mp", "dp")),
            P("mp", "dp"),
            P("dp"),
            P("dp"),
            P("dp"),
            P("mp", "dp"),
        ),
        check_vma=False,
    )
```

```python
import functools

import jax
import jax.numpy as jnp
from jax import lax
from jax.experimental import pallas as pl
from jax.experimental.pallas import tpu as pltpu
from jax.sharding import PartitionSpec as P

HD = 64
LANES = 128
EPSILON = 1e-05
ENTROPY_WEIGHT = 0.5
BRIEF = pl.CostEstimate(flops=0, bytes_accessed=0, transcendentals=0)
bfloat = jnp.bfloat16

CUTS = (0, 2, 4, 7)
FREE = 99
ORDERS = {"f": "z", "p": "y", "s": "z"}
ORDERS = {"f": "z", "p": "y", "s": "z"}
PLAN = (
    (),
    (),
    (("a", "make"), ("a", "send"),),
    (),
    (),
    (("f", "make"), ("f", "send"), ("a", "add"), ("a", "send"),),
    (),
    (("b", "make"), ("b", "send"),),
    (),
    (),
    (("t", "step"), ("f", "add"),),
    (("t", "step"), ("c", "make"),),
    (("a", "add"), ("a", "send"), ("b", "add"), ("b", "send"),),
    (("c", "send"), ("t", "step"), ("f", "send"),),
    (),
    (),
    (),
    (),
    (("p", "make"), ("p", "send"), ("b", "add"), ("b", "send"),),
    (("s", "make"), ("s", "send"),),
    (("f", "add"), ("f", "send"), ("c", "add"), ("c", "send"),),
    (),
    (("p", "add"), ("p", "send"), ("a", "wait"), ("b", "wait"), ("s", "add"), ("s", "send"), ("c", "add"), ("c", "send"), ("p", "add"), ("p", "send"), ("f", "wait"), ("s", "add"), ("s", "send"), ("c", "wait"), ("p", "wait"), ("s", "wait"),),
    (),
    (),
    (),
    (),
)
single = jnp.float32


def matmul(left, right):
    return jnp.dot(left, right, preferred_element_type=single)


def inner_rows(left, right):
    return lax.dot_general(left, right, (((0,), (0,)), ((), ())), preferred_element_type=single)


def outer_rows(left, right):
    return lax.dot_general(left, right, (((1,), (1,)), ((), ())), preferred_element_type=single)


def bits_of(count):
    bits = []
    while (1 << len(bits)) < count:
        bits.append(1 << len(bits))
    return bits


def swap(value, axis, count, bit):
    return lax.ppermute(value, axis, [(i, i ^ bit) for i in range(count)])


def relative_of(order):
    table = [0]
    for bit in order:
        table = table + [r ^ bit for r in table]
    return table


def gather_blocks(own, axis, count, order):
    held = own[None]
    for bit in order:
        held = jnp.concatenate([held, swap(held, axis, count, bit)], 0)
    return held


def scatter_blocks(parts, axis, count, order):
    for bit in reversed(order):
        half = parts.shape[0] // 2
        arrived = swap(parts[half:].astype(bfloat), axis, count, bit)
        parts = parts[:half] + arrived.astype(single)
    return parts[0]


def tie(*values):
    return lax.optimization_barrier(values)


def gather_both_steps(owns, axis, count, orders):
    helds = [own[None] for own in owns]
    for bits in zip(*orders):
        arrived = [swap(held, axis, count, bit) for held, bit in zip(helds, bits)]
        yield None
        arrived = tie(*arrived)
        helds = [jnp.concatenate([held, more], 0) for held, more in zip(helds, arrived)]
    yield helds


def total_over(value, axis, count, order):
    for bit in order:
        value = value + swap(value, axis, count, bit)
    return value


def xor_take(table, me, array, axis):
    return jnp.take(array, me ^ jnp.asarray(table, jnp.int32), axis=axis, mode="clip")


def places(table):
    inverse = [0] * len(table)
    for position, relative in enumerate(table):
        inverse[relative] = position
    return inverse


def natural_order(table, me, array, axis):
    count = len(table)
    order = jnp.asarray(places(table), jnp.int32)[me ^ jnp.arange(count, dtype=jnp.int32)]
    return jnp.take(array, order, axis=axis, mode="clip")


VMEM = pl.BlockSpec(memory_space=pltpu.VMEM)


def run_whole(kernel, name, outs, *operands, scratch=()):
    return pl.pallas_call(
        kernel,
        in_specs=[VMEM] * len(operands),
        out_specs=[VMEM] * len(outs),
        out_shape=[jax.ShapeDtypeStruct(shape, dtype) for shape, dtype in outs],
        scratch_shapes=list(scratch),
        compiler_params=pltpu.CompilerParams(vmem_limit_bytes=16 * 1024 * 1024),
        cost_estimate=BRIEF,
        name=name,
    )(*operands)


def row(vector):
    return vector.reshape(1, -1).astype(single)


def norm_forward_kernel(kept_ref, arrived_ref, state_ref, bias_ref, gain_ref, shift_ref, in_ref, out_ref, low_ref):
    hidden = (
        state_ref[...].astype(single)
        + (kept_ref[...].astype(single) + arrived_ref[...].astype(single))
        + bias_ref[...]
    )
    in_ref[...] = hidden
    center = hidden - jnp.mean(hidden, -1, keepdims=True)
    spread = jnp.mean(center * center, -1, keepdims=True)
    normal = center * lax.rsqrt(spread + EPSILON) * gain_ref[...] + shift_ref[...]
    out_ref[...] = normal
    low_ref[...] = normal.astype(bfloat)


def norm_forward(kept, arrived, state, bias, gain, shift):
    shape = state.shape
    return run_whole(
        norm_forward_kernel,
        "norm_forward",
        [(shape, single), (shape, single), (shape, bfloat)],
        kept.reshape(shape),
        arrived.reshape(shape),
        state,
        row(bias),
        row(gain),
        row(shift),
    )


def norm_backward_kernel(count, *refs):
    upstream = refs[0][...].astype(single)
    for ref in refs[1:count]:
        upstream = upstream + ref[...].astype(single)
    norm_backward_rows(upstream, *refs[count:])


def norm_backward_rows(upstream, hidden_ref, gain_ref, out_ref, low_ref, sums_ref):
    hidden = hidden_ref[...]
    center = hidden - jnp.mean(hidden, -1, keepdims=True)
    spread = jnp.mean(center * center, -1, keepdims=True)
    inverse = lax.rsqrt(spread + EPSILON)
    normal = center * inverse
    scaled = upstream * gain_ref[...]
    delta = inverse * (
        scaled
        - jnp.mean(scaled, -1, keepdims=True)
        - normal * jnp.mean(scaled * normal, -1, keepdims=True)
    )
    low = delta.astype(bfloat)
    out_ref[...] = delta
    low_ref[...] = low
    sums_ref[0:1, :] = jnp.sum(low.astype(single), 0, keepdims=True)
    sums_ref[1:2, :] = jnp.sum(upstream * normal, 0, keepdims=True)
    sums_ref[2:3, :] = jnp.sum(upstream, 0, keepdims=True)


def norm_backward(parts, hidden, gain):
    shape = hidden.shape
    return run_whole(
        functools.partial(norm_backward_kernel, len(parts)),
        "norm_backward",
        [(shape, single), (shape, bfloat), ((3, shape[1]), single)],
        *(part.reshape(shape) for part in parts),
        hidden,
        row(gain),
    )


def erf_gelu(value):
    phi = 0.5 * (1.0 + lax.erf(value * 0.7071067811865476))
    return value * phi, phi


def join(pieces, full_ref):
    rows = pieces[0].shape[0]
    for index, piece in enumerate(pieces):
        full_ref[index * rows : (index + 1) * rows, :] = piece[...]


def feed_forward_kernel(count, *refs):
    expand_ref, bias_ref, shrink_ref, full_ref, hidden_ref, act_ref, sent_ref, kept_ref = refs[count:]
    join(refs[:count], full_ref)
    half = sent_ref.shape[0]
    for index in (1, 0):
        part = slice(index * half, (index + 1) * half)
        hidden = matmul(full_ref[part, :], expand_ref[...]) + bias_ref[...]
        hidden_ref[part, :] = hidden
        act = erf_gelu(hidden)[0].astype(bfloat)
        act_ref[part, :] = act
        out = matmul(act, shrink_ref[...])
        if index == 0:
            kept_ref[...] = out
        else:
            sent_ref[...] = out.astype(bfloat)


def feed_forward(pieces, expand, bias, shrink):
    rows, width = len(pieces) * pieces[0].shape[0], pieces[0].shape[1]
    hidden = expand.shape[1]
    return run_whole(
        functools.partial(feed_forward_kernel, len(pieces)),
        "feed_forward",
        [
            ((rows, width), bfloat),
            ((rows, hidden), single),
            ((rows, hidden), bfloat),
            ((rows // 2, width), bfloat),
            ((rows // 2, width), single),
        ],
        *pieces,
        expand,
        row(bias),
        shrink,
    )


def feed_backward_kernel(count, *refs):
    expand_ref, shrink_ref, hidden_ref, full_ref, delta_ref, sums_ref, sent_ref, kept_ref = refs[count:]
    join(refs[:count], full_ref)
    half = sent_ref.shape[0]
    sums = jnp.zeros(sums_ref.shape, single)
    for index in (1, 0):
        part = slice(index * half, (index + 1) * half)
        upstream = outer_rows(full_ref[part, :], shrink_ref[...])
        hidden = hidden_ref[part, :]
        slope = erf_gelu(hidden)[1] + hidden * jnp.exp(-0.5 * hidden * hidden) * 0.3989422804014327
        delta = (upstream * slope).astype(bfloat)
        delta_ref[part, :] = delta
        sums = sums + jnp.sum(delta.astype(single), 0, keepdims=True)
        out = outer_rows(delta, expand_ref[...])
        if index == 0:
            kept_ref[...] = out
        else:
            sent_ref[...] = out.astype(bfloat)
    sums_ref[...] = sums


def feed_backward(pieces, expand, shrink, hidden):
    rows, width = len(pieces) * pieces[0].shape[0], pieces[0].shape[1]
    return run_whole(
        functools.partial(feed_backward_kernel, len(pieces)),
        "feed_backward",
        [
            ((rows, width), bfloat),
            (hidden.shape, bfloat),
            ((1, hidden.shape[1]), single),
            ((rows // 2, width), bfloat),
            ((rows // 2, width), single),
        ],
        *pieces,
        expand,
        shrink,
        hidden,
    )


def project_kernel(count, transposed, *refs):
    weight_ref, bias_ref, full_ref, out_ref = refs[count:]
    join(refs[:count], full_ref)
    out = (outer_rows if transposed else matmul)(full_ref[...], weight_ref[...])
    out_ref[...] = (out + bias_ref[...]).astype(bfloat)


def project(pieces, weight, bias, transposed=False):
    rows, width = len(pieces) * pieces[0].shape[0], pieces[0].shape[1]
    return run_whole(
        functools.partial(project_kernel, len(pieces), transposed),
        "project",
        [((rows, width), bfloat), ((rows, bias.shape[0]), bfloat)],
        *pieces,
        weight,
        row(bias),
    )


def halves_kernel(count, transposed, *refs):
    lefts, weights, (sent_ref, kept_ref) = refs[:count], refs[count : 2 * count], refs[2 * count :]
    half = sent_ref.shape[0]
    product = outer_rows if transposed else matmul
    for part, out in ((slice(half, 2 * half), sent_ref), (slice(0, half), kept_ref)):
        total = product(lefts[0][part, :], weights[0][...])
        for left, weight in zip(lefts[1:], weights[1:]):
            total = total + product(left[part, :], weight[...])
        out[...] = total.astype(out.dtype)


def product_halves(lefts, weights, transposed=False):
    half = lefts[0].shape[0] // 2
    width = weights[0].shape[0] if transposed else weights[0].shape[1]
    return run_whole(
        functools.partial(halves_kernel, len(lefts), transposed),
        "product_halves",
        [((half, width), bfloat), ((half, width), single)],
        *lefts,
        *weights,
    )


def add_halves_kernel(kept_ref, arrived_ref, sent_ref, left_ref):
    half = kept_ref.shape[0] // 2
    sent_ref[...] = (kept_ref[half:, :].astype(single) + arrived_ref[half:, :].astype(single)).astype(bfloat)
    left_ref[...] = kept_ref[:half, :].astype(single) + arrived_ref[:half, :].astype(single)


def add_halves(kept, arrived):
    half, width = kept.shape[0] // 2, kept.shape[1]
    return run_whole(
        add_halves_kernel,
        "add_halves",
        [((half, width), bfloat), ((half, width), single)],
        kept,
        arrived,
    )


def add_columns_kernel(kept_ref, arrived_ref, sent_ref, left_ref):
    half = sent_ref.shape[1]
    total = kept_ref[...].astype(single) + arrived_ref[...].astype(single)
    sent_ref[...] = total[:, half:].astype(bfloat)
    left_ref[...] = total[:, :half].astype(bfloat)


def add_columns(kept, arrived):
    rows, width = kept.shape
    return run_whole(
        add_columns_kernel, "add_columns", [((rows, width // 2), bfloat)] * 2, kept, arrived
    )


def bin_rows_kernel(bins_ref, value_ref, sent_ref, kept_ref, sums):
    sums[...] = jnp.zeros_like(sums)
    for slot in range(value_ref.shape[0]):
        sums[bins_ref[slot]] += value_ref[slot]
    half = sent_ref.shape[0]
    sent_ref[...] = sums[half:].astype(bfloat)
    kept_ref[...] = sums[:half]


def bin_rows(value, bins, count):
    shape = (count // 2,) + value.shape[1:]
    return pl.pallas_call(
        bin_rows_kernel,
        in_specs=[pl.BlockSpec(memory_space=pltpu.SMEM), VMEM],
        out_specs=[VMEM, VMEM],
        out_shape=[jax.ShapeDtypeStruct(shape, bfloat), jax.ShapeDtypeStruct(shape, single)],
        scratch_shapes=[pltpu.VMEM((count,) + value.shape[1:], single)],
        compiler_params=pltpu.CompilerParams(
            vmem_limit_bytes=8 * 1024 * 1024 + 6 * count * value.shape[1] * value.shape[2]
        ),
        cost_estimate=BRIEF,
        name="bin_rows",
    )(bins, value)


def vocab_tile(vocab_share):
    for tile in (1792, 896, 512, 256, 128):
        if vocab_share % tile == 0:
            return tile
    return vocab_share


def vocab_forward_kernel(
    state_ref, table_ref, label_ref, label_rows_ref, weight_ref, mixed_ref, tops_ref, stats_ref, top, sum_ref
):
    step = pl.program_id(0)
    rows = state_ref.shape[0]
    tile = table_ref.shape[0]
    block = min(rows, 1024)

    @pl.when(step == 0)
    def start():
        top[...] = jnp.full_like(top, -jnp.inf)
        sum_ref[...] = jnp.zeros_like(sum_ref)
        mixed_ref[...] = jnp.zeros_like(mixed_ref)
        tops_ref[...] = jnp.zeros_like(tops_ref)

    repeat = lambda value, count: jnp.concatenate([value] * count, 1) if count > 1 else value
    spans = tile // LANES
    for index in range(rows // block):
        part = pl.ds(index * block, block)
        logits = outer_rows(state_ref[part, :], table_ref[...])
        old = top[part, :]
        new = jnp.maximum(old, jnp.max(logits, -1, keepdims=True))
        lanes = lax.broadcasted_iota(jnp.int32, new.shape, 1)
        offset = label_ref[part, :] - step * tile
        shrink = jnp.exp(old - new)
        top[part, :] = new
        tops_ref[part, :] = jnp.where(lanes == step, new, tops_ref[part, :])
        sums = sum_ref[part, :] * shrink
        low = []
        for span in range(spans):
            weights = jnp.exp(logits[:, span * LANES : (span + 1) * LANES] - new)
            weights = jnp.where(lanes + span * LANES == offset, 0.0, weights)
            sums = sums + weights
            low.append(weights.astype(bfloat))
        sum_ref[part, :] = sums
        low = jnp.concatenate(low, 1)
        weight_ref[part, :] = low
        mixed_ref[part, :] = mixed_ref[part, :] * repeat(shrink, mixed_ref.shape[1] // LANES) + matmul(
            low, table_ref[...]
        )

    @pl.when(step == pl.num_programs(0) - 1)
    def finish():
        label = label_ref[...]
        entries = tile * pl.num_programs(0)
        inside = (label >= 0) & (label < entries)
        target = jnp.sum(
            state_ref[...].astype(single) * label_rows_ref[...].astype(single), -1, keepdims=True
        )
        target = jnp.where(inside, target, 0.0)
        total = jnp.sum(sum_ref[...], -1, keepdims=True)
        total = total + jnp.where(inside, jnp.exp(target - top[...]), 0.0)
        lanes = lax.broadcasted_iota(jnp.int32, label.shape, 1)
        columns = jnp.where(lanes == 0, top[...], jnp.where(lanes == 1, total, target))
        stats_ref[...] = jnp.swapaxes(columns, 0, 1)[:8, :]


def vocab_forward(states, table, label, label_rows):
    rows, width = states.shape
    entries = table.shape[0]
    tile = vocab_tile(entries)
    whole = lambda *shape: pl.BlockSpec(shape, lambda i: (0,) * len(shape))
    return pl.pallas_call(
        vocab_forward_kernel,
        grid=(entries // tile,),
        in_specs=[
            whole(rows, width),
            pl.BlockSpec((tile, width), lambda i: (i, 0)),
            whole(rows, LANES),
            whole(rows, width),
        ],
        out_specs=[pl.BlockSpec((rows, tile), lambda i: (0, i)), VMEM, VMEM, VMEM],
        out_shape=[
            jax.ShapeDtypeStruct((rows, entries), bfloat),
            jax.ShapeDtypeStruct((rows, width), single),
            jax.ShapeDtypeStruct((rows, LANES), single),
            jax.ShapeDtypeStruct((8, rows), single),
        ],
        scratch_shapes=[pltpu.VMEM((rows, LANES), single)] * 2,
        compiler_params=pltpu.CompilerParams(
            dimension_semantics=("arbitrary",), vmem_limit_bytes=40 * 1024 * 1024
        ),
        cost_estimate=BRIEF,
        name="vocab_forward",
    )(states, table, label, label_rows)


def vocab_slope_kernel(first, ratio, order_ref, weight_ref, factor_ref, label_ref, column_ref, state_ref, sent_ref, kept_ref, moved):
    step = pl.program_id(0)
    tile = weight_ref.shape[1]
    width = state_ref.shape[1]
    blocks = order_ref.shape[0]
    span = width // blocks

    @pl.when(step == 0)
    def start():
        for place in range(blocks):
            source = pl.multiple_of(order_ref[place] * span, span)
            moved[:, place * span : (place + 1) * span] = state_ref[:, pl.ds(source, span)]

    here = step + first
    factors = factor_ref[...]
    lanes = lax.broadcasted_iota(jnp.int32, factors.shape, 1)
    factor = jnp.sum(jnp.where(lanes == here // ratio, factors, 0.0), -1, keepdims=True)
    columns = lax.broadcasted_iota(jnp.int32, weight_ref.shape, 1) + here * tile
    delta = jnp.where(
        columns == label_ref[:, :1], column_ref[:, :1], weight_ref[...].astype(single) * factor
    ).astype(bfloat)
    half = width // 2
    slope = inner_rows(delta, moved[...])
    sent_ref[...] = slope[:, half:].astype(bfloat)
    kept_ref[...] = slope[:, :half].astype(bfloat)


def vocab_slope(weights, factors, label, values, states, order, first, count, tile):
    rows, width = states.shape
    whole = lambda *shape: pl.BlockSpec(shape, lambda i, o: (0,) * len(shape))
    half = pl.BlockSpec((tile, width // 2), lambda i, o: (i, 0))
    return pl.pallas_call(
        functools.partial(vocab_slope_kernel, first, vocab_tile(weights.shape[1]) // tile),
        grid_spec=pltpu.PrefetchScalarGridSpec(
            num_scalar_prefetch=1,
            grid=(count,),
            in_specs=[
                pl.BlockSpec((rows, tile), lambda i, o: (0, i + first)),
                whole(rows, LANES),
                whole(rows, LANES),
                whole(rows, LANES),
                whole(rows, width),
            ],
            out_specs=[half, half],
            scratch_shapes=[pltpu.VMEM((rows, width), bfloat)],
        ),
        out_shape=[jax.ShapeDtypeStruct((count * tile, width // 2), bfloat)] * 2,
        compiler_params=pltpu.CompilerParams(
            dimension_semantics=("arbitrary",), vmem_limit_bytes=56 * 1024 * 1024
        ),
        cost_estimate=BRIEF,
        name="vocab_slope",
    )(order, weights, factors, label, values, states)


def slope_group_kernel(count, order_ref, *refs):
    lefts, rights = refs[:count], refs[count : 2 * count]
    sent_ref, kept_ref, moved = refs[2 * count :]
    blocks = order_ref.shape[0]
    width = rights[0].shape[1]
    span, half = width // blocks, width // 2
    base = 0
    for index in range(count):
        rows, entries = lefts[index].shape
        if index == 0 or rights[index] is not rights[index - 1]:
            for place in range(blocks):
                source = pl.multiple_of(order_ref[place] * span, span)
                moved[:rows, place * span : (place + 1) * span] = rights[index][:, pl.ds(source, span)]
        right = moved[:rows, :]
        left = lefts[index][...]
        slope = inner_rows(left, right)
        sent_ref[base : base + entries, :] = slope[:, half:].astype(bfloat)
        kept_ref[base : base + entries, :] = slope[:, :half].astype(bfloat)
        base += entries


def slope_group(pairs, order):
    width = pairs[0][1].shape[1]
    total = sum(left.shape[1] for left, right in pairs)
    rows = max(left.shape[0] for left, right in pairs)
    lefts = [left for left, right in pairs]
    rights = [right for left, right in pairs]
    whole = pl.BlockSpec(memory_space=pltpu.VMEM)
    return pl.pallas_call(
        functools.partial(slope_group_kernel, len(pairs)),
        in_specs=[pl.BlockSpec(memory_space=pltpu.SMEM)] + [whole] * (2 * len(pairs)),
        out_specs=[whole, whole],
        out_shape=[jax.ShapeDtypeStruct((total, width // 2), bfloat)] * 2,
        scratch_shapes=[pltpu.VMEM((rows, width), bfloat)],
        compiler_params=pltpu.CompilerParams(vmem_limit_bytes=16 * 1024 * 1024),
        cost_estimate=BRIEF,
        name="slope_group",
    )(order, *lefts, *rights)


def head_weights(causal, places, query, address, lanes, head):
    own = (lanes // HD) == head
    scores = outer_rows(jnp.where(own, query, jnp.zeros_like(query)), address) * 0.125
    if causal:
        scores = jnp.where(places[0][:, :1] >= places[1][:1, :], scores, -1000000000.0)
    expo = jnp.exp(scores - jnp.max(scores, -1, keepdims=True))
    return own, expo / jnp.sum(expo, -1, keepdims=True)


def attend_forward_kernel(causal, bins_ref, stores_ref, query_ref, address_ref, content_ref, *refs):
    mixed_ref = refs[-1]
    places = [ref[...] for ref in refs[:-1]]
    length, width = query_ref.shape[1:]
    for pair in range(width // LANES):
        part = slice(pair * LANES, (pair + 1) * LANES)
        query, address, content = query_ref[0, :, part], address_ref[0, :, part], content_ref[0, :, part]
        lanes = lax.broadcasted_iota(jnp.int32, query.shape, 1)
        total = jnp.zeros(query.shape, single)
        for head in range(LANES // HD):
            own, weights = head_weights(causal, places, query, address, lanes, head)
            total = jnp.where(own, matmul(weights.astype(bfloat), content), total)
        shape = (mixed_ref.shape[0], mixed_ref.shape[2], LANES)
        mixed_ref[:, 0, :, part] = total.astype(bfloat).reshape(shape)


def attend_forward(queries, addresses, contents, bins, stores, parts, places=()):
    count = bins.shape[0]
    length, width = queries.shape[1:]
    stored = addresses.shape[1]
    return pl.pallas_call(
        functools.partial(attend_forward_kernel, bool(places)),
        grid_spec=pltpu.PrefetchScalarGridSpec(
            num_scalar_prefetch=2,
            grid=(count,),
            in_specs=[
                pl.BlockSpec((1, length, width), lambda i, b, s: (b[i], 0, 0)),
                pl.BlockSpec((1, stored, width), lambda i, b, s: (s[i], 0, 0)),
                pl.BlockSpec((1, stored, width), lambda i, b, s: (s[i], 0, 0)),
            ]
            + [pl.BlockSpec(place.shape, lambda i, b, s: (0, 0)) for place in places],
            out_specs=pl.BlockSpec((parts, 1, length // parts, width), lambda i, b, s: (0, i, 0, 0)),
        ),
        out_shape=jax.ShapeDtypeStruct((parts, count, length // parts, width), bfloat),
        compiler_params=pltpu.CompilerParams(
            dimension_semantics=("arbitrary",), vmem_limit_bytes=12 * 1024 * 1024
        ),
        cost_estimate=BRIEF,
        name="attend_forward",
    )(bins, stores, queries, addresses, contents, *places)


def attend_backward_kernel(
    causal, bins_ref, stores_ref, sums_ref, query_ref, address_ref, content_ref, upstream_ref, *refs
):
    query_out, address_out, content_out, query_sum, address_sum, content_sum = refs[-6:]
    places = [ref[...] for ref in refs[:-6]]
    step = pl.program_id(0)
    length, width = query_ref.shape[1:]

    @pl.when(step == 0)
    def start():
        query_sum[...] = jnp.zeros_like(query_sum)
        address_sum[...] = jnp.zeros_like(address_sum)
        content_sum[...] = jnp.zeros_like(content_sum)

    for pair in range(width // LANES):
        part = slice(pair * LANES, (pair + 1) * LANES)
        query, address, content = query_ref[0, :, part], address_ref[0, :, part], content_ref[0, :, part]
        upstream = upstream_ref[:, 0, :, part].reshape(length, LANES)
        lanes = lax.broadcasted_iota(jnp.int32, query.shape, 1)
        query_delta = jnp.zeros(query.shape, single)
        address_delta = jnp.zeros(address.shape, single)
        content_delta = jnp.zeros(address.shape, single)
        for head in range(LANES // HD):
            own, weights = head_weights(causal, places, query, address, lanes, head)
            weight_delta = outer_rows(jnp.where(own, upstream, jnp.zeros_like(upstream)), content)
            score_delta = (
                weights * (weight_delta - jnp.sum(weights * weight_delta, -1, keepdims=True))
            ).astype(bfloat)
            query_delta = jnp.where(own, matmul(score_delta, address), query_delta)
            address_delta = jnp.where(own, inner_rows(score_delta, query), address_delta)
            content_delta = jnp.where(own, inner_rows(weights.astype(bfloat), upstream), content_delta)
        query_sum[sums_ref[step], :, part] += query_delta * 0.125
        address_sum[stores_ref[step], :, part] += address_delta * 0.125
        content_sum[stores_ref[step], :, part] += content_delta

    @pl.when(step == pl.num_programs(0) - 1)
    def finish():
        query_out[...] = query_sum[...].astype(bfloat)
        address_out[...] = address_sum[...].astype(bfloat)
        content_out[...] = content_sum[...].astype(bfloat)


def attend_backward(queries, addresses, contents, upstream, bins, stores, sums, places=()):
    count = bins.shape[0]
    length, width = queries.shape[1:]
    stored = addresses.shape[1]
    whole = lambda shape: pl.BlockSpec(shape, lambda i, b, s, t: (0,) * len(shape))
    return pl.pallas_call(
        functools.partial(attend_backward_kernel, bool(places)),
        grid_spec=pltpu.PrefetchScalarGridSpec(
            num_scalar_prefetch=3,
            grid=(count,),
            in_specs=[
                pl.BlockSpec((1, length, width), lambda i, b, s, t: (b[i], 0, 0)),
                pl.BlockSpec((1, stored, width), lambda i, b, s, t: (s[i], 0, 0)),
                pl.BlockSpec((1, stored, width), lambda i, b, s, t: (s[i], 0, 0)),
                pl.BlockSpec((upstream.shape[0], 1) + upstream.shape[2:], lambda i, b, s, t: (0, i, 0, 0)),
            ]
            + [whole(place.shape) for place in places],
            out_specs=[whole(queries.shape), whole(addresses.shape), whole(addresses.shape)],
            scratch_shapes=[
                pltpu.VMEM(queries.shape, single),
                pltpu.VMEM(addresses.shape, single),
                pltpu.VMEM(addresses.shape, single),
            ],
        ),
        out_shape=[
            jax.ShapeDtypeStruct(queries.shape, bfloat),
            jax.ShapeDtypeStruct(addresses.shape, bfloat),
            jax.ShapeDtypeStruct(addresses.shape, bfloat),
        ],
        compiler_params=pltpu.CompilerParams(
            dimension_semantics=("arbitrary",),
            vmem_limit_bytes=12 * 1024 * 1024 + 10 * queries.size,
        ),
        cost_estimate=BRIEF,
        name="attend_backward",
    )(bins, stores, sums, queries, addresses, contents, upstream, *places)


def pick_kernel(bins_ref, value_ref, out_ref):
    out_ref[...] = value_ref[...]


def pick(value, bins):
    block = (1,) + value.shape[1:]
    return pl.pallas_call(
        pick_kernel,
        grid_spec=pltpu.PrefetchScalarGridSpec(
            num_scalar_prefetch=1,
            grid=(bins.shape[0],),
            in_specs=[pl.BlockSpec(block, lambda i, b: (b[i], 0, 0))],
            out_specs=pl.BlockSpec(block, lambda i, b: (i, 0, 0)),
        ),
        out_shape=jax.ShapeDtypeStruct(bins.shape + value.shape[1:], value.dtype),
        name="pick",
    )(bins, value)


def finish_kernel(count, *refs):
    base = 0
    for index in range(count):
        rows = refs[index].shape[0]
        refs[-1][base : base + rows, :] = refs[index][...].astype(single) + refs[count + index][
            ...
        ].astype(single)
        base += rows


def finish_sums(kept, arrived):
    total = sum(part.shape[0] for part in kept)
    whole = pl.BlockSpec(memory_space=pltpu.VMEM)
    return pl.pallas_call(
        functools.partial(finish_kernel, len(kept)),
        in_specs=[whole] * (2 * len(kept)),
        out_specs=whole,
        out_shape=jax.ShapeDtypeStruct((total, kept[0].shape[1]), single),
        compiler_params=pltpu.CompilerParams(vmem_limit_bytes=8 * 1024 * 1024),
        name="finish_sums",
    )(*kept, *arrived)


def order_columns_kernel(count, order_ref, *refs):
    pieces, (joined_ref, moved_ref) = refs[:count], refs[count:]
    rows, width = pieces[0].shape
    span = width // order_ref.shape[0]
    for index in range(count):
        part = slice(index * rows, (index + 1) * rows)
        joined_ref[part, :] = pieces[index][...]
        for place in range(order_ref.shape[0]):
            source = pl.multiple_of(order_ref[place] * span, span)
            moved_ref[part, place * span : (place + 1) * span] = pieces[index][:, pl.ds(source, span)]


def order_columns(pieces, order):
    shape = (len(pieces) * pieces[0].shape[0], pieces[0].shape[1])
    return pl.pallas_call(
        functools.partial(order_columns_kernel, len(pieces)),
        in_specs=[pl.BlockSpec(memory_space=pltpu.SMEM)] + [VMEM] * len(pieces),
        out_specs=[VMEM, VMEM],
        out_shape=[jax.ShapeDtypeStruct(shape, bfloat)] * 2,
        compiler_params=pltpu.CompilerParams(vmem_limit_bytes=8 * 1024 * 1024),
        cost_estimate=BRIEF,
        name="order_columns",
    )(order, *pieces)


def half_slope_kernel(
    first,
    ratio,
    base_ref,
    weight_ref,
    table_ref,
    factor_ref,
    label_ref,
    column_ref,
    far_ref,
    far_label_ref,
    moved_ref,
    far_moved_ref,
    sent_ref,
    kept_ref,
    delta,
):
    rows, tile = weight_ref.shape
    here = base_ref[0] + first + pl.program_id(0)
    factors = factor_ref[...]
    lanes = lax.broadcasted_iota(jnp.int32, factors.shape, 1)
    factor = jnp.sum(jnp.where(lanes == here // ratio, factors, 0.0), -1, keepdims=True)
    columns = lax.broadcasted_iota(jnp.int32, weight_ref.shape, 1) + here * tile
    logits = outer_rows(far_ref[...], table_ref[...])
    delta[:rows, :] = jnp.where(
        columns == label_ref[:, :1], column_ref[:, :1], weight_ref[...].astype(single) * factor
    ).astype(bfloat)
    hit = jnp.where(columns == far_label_ref[:, :1], 1.0, 0.0)
    delta[rows:, :] = (column_ref[:, 5:6] * (hit - jnp.exp(logits - column_ref[:, 4:5]))).astype(bfloat)
    slope = inner_rows(delta[:rows, :], moved_ref[...]) + inner_rows(delta[rows:, :], far_moved_ref[...])
    half = sent_ref.shape[1]
    part = pl.ds(pl.multiple_of(pl.program_id(0) * tile, tile), tile)
    sent_ref[part, :] = slope[:, half:].astype(bfloat)
    kept_ref[part, :] = slope[:, :half].astype(bfloat)


def half_slope(base, weights, table, factors, label, values, far, far_label, moved, far_moved, first, count, tile):
    rows, width = far.shape
    return pl.pallas_call(
        functools.partial(half_slope_kernel, first, vocab_tile(weights.shape[1]) // tile),
        grid_spec=pltpu.PrefetchScalarGridSpec(
            num_scalar_prefetch=1,
            grid=(count,),
            in_specs=[
                pl.BlockSpec((rows, tile), lambda i, b: (0, i + first + b[0])),
                pl.BlockSpec((tile, width), lambda i, b: (i + first + b[0], 0)),
                VMEM,
                VMEM,
                VMEM,
                VMEM,
                VMEM,
                VMEM,
                VMEM,
            ],
            out_specs=[VMEM, VMEM],
            scratch_shapes=[pltpu.VMEM((2 * rows, tile), bfloat)],
        ),
        out_shape=[jax.ShapeDtypeStruct((count * tile, width // 2), bfloat)] * 2,
        compiler_params=pltpu.CompilerParams(
            dimension_semantics=("arbitrary",), vmem_limit_bytes=32 * 1024 * 1024
        ),
        cost_estimate=BRIEF,
        name="half_slope",
    )(base, weights, table, factors, label, values, far, far_label, moved, far_moved)


def place_halves_kernel(count, side_ref, *refs):
    out_ref = refs[-1]
    half = out_ref.shape[0] // 2
    for group, side in ((refs[:count], side_ref[0]), (refs[count : 2 * count], 1 - side_ref[0])):
        offset = 0
        for ref in group:
            rows = ref.shape[0]
            start = pl.multiple_of(side * half + offset, LANES)
            out_ref[pl.ds(start, rows), :] = ref[...].astype(single)
            offset += rows


def place_halves(side, own, other):
    total = sum(part.shape[0] for part in own) * 2
    return pl.pallas_call(
        functools.partial(place_halves_kernel, len(own)),
        in_specs=[pl.BlockSpec(memory_space=pltpu.SMEM)] + [VMEM] * (2 * len(own)),
        out_specs=VMEM,
        out_shape=jax.ShapeDtypeStruct((total, own[0].shape[1]), single),
        compiler_params=pltpu.CompilerParams(vmem_limit_bytes=8 * 1024 * 1024),
        cost_estimate=BRIEF,
        name="place_halves",
    )(side, *own, *other)


def lane_blocks(value, count, index):
    span = value.shape[1] // count
    return jnp.concatenate(
        [value[:, (p ^ (1 << index)) * span : ((p ^ (1 << index)) + 1) * span] for p in range(count)], 1
    )


def merge_stats_kernel(count, index, own_ref, other_ref, out_ref):
    own, other = own_ref[...], lane_blocks(other_ref[...], count, index)
    high = jnp.maximum(own[0:1], other[0:1])
    sums = own[1:2] * jnp.exp(own[0:1] - high) + other[1:2] * jnp.exp(other[0:1] - high)
    out_ref[...] = jnp.concatenate([high, sums, own[2:3] + other[2:3], own[3:]], 0)


def merge_stats(own, other, count, index):
    return run_whole(
        functools.partial(merge_stats_kernel, count, index), "merge_stats", [(own.shape, single)], own, other
    )[0]


def row_norms_kernel(count, slots, own_ref, out_ref):
    own = own_ref[...]
    norm = own[0:1] + jnp.log(own[1:2])
    parts = own[2:3] - norm
    span = parts.shape[1] // count
    parts = [parts[:, p * span : (p + 1) * span] for p in range(count)]
    while len(parts) > 1:
        parts = [parts[p] + parts[p + 1] for p in range(0, len(parts), 2)]
    lanes = lax.broadcasted_iota(jnp.int32, parts[0].shape, 1)
    places = lax.broadcasted_iota(jnp.int32, norm.shape, 1)
    likelihood = jnp.zeros_like(norm)
    for slot in range(slots):
        total = jnp.sum(jnp.where(lanes // (span // slots) == slot, parts[0], 0.0), -1, keepdims=True)
        likelihood = jnp.where(places == slot, total, likelihood)
    out_ref[...] = jnp.concatenate([norm, likelihood, own[2:]], 0)


def row_norms(own, count, slots):
    return run_whole(
        functools.partial(row_norms_kernel, count, slots), "row_norms", [(own.shape, single)], own
    )[0]


def as_columns(rows):
    return jnp.swapaxes(
        jnp.concatenate([rows, jnp.zeros((LANES - rows.shape[0], rows.shape[1]), single)], 0), 0, 1
    )


def vocab_part_kernel(
    place_ref, norm_ref, merged_ref, local_ref, label_rows_ref, label_ref, mixed_ref, sent_ref, kept_ref
):
    norm = norm_ref[0:1, :]
    surplus = 1.0 - jnp.exp(merged_ref[2:3, :] - norm)
    share = jnp.exp(local_ref[0:1, :] - norm)
    columns = as_columns(jnp.concatenate([surplus, share] + [norm] * 6, 0))
    label = label_ref[:, 0:1]
    inside = (label >= 0) & (label < place_ref[3])
    part = (
        jnp.where(inside, columns[:, 0:1], 0.0) * label_rows_ref[...].astype(single)
        - columns[:, 1:2] * mixed_ref[...]
    )
    half = kept_ref.shape[0]
    kept_ref[...] = part[:half]
    sent_ref[...] = part[half:].astype(bfloat)


def vocab_part(place, norm, merged, local, label_rows, label, mixed):
    rows, width = mixed.shape
    return pl.pallas_call(
        vocab_part_kernel,
        in_specs=[pl.BlockSpec(memory_space=pltpu.SMEM)] + [VMEM] * 6,
        out_specs=[VMEM] * 2,
        out_shape=[
            jax.ShapeDtypeStruct((rows // 2, width), bfloat),
            jax.ShapeDtypeStruct((rows // 2, width), single),
        ],
        compiler_params=pltpu.CompilerParams(vmem_limit_bytes=16 * 1024 * 1024),
        cost_estimate=BRIEF,
        name="vocab_part",
    )(place, norm, merged, local, label_rows, label, mixed)


def vocab_scale_kernel(
    slots, delta_ref, place_ref, norm_ref, merged_ref, far_ref, tops_ref, factor_ref, column_ref
):
    norm = norm_ref[0:1, :]
    lanes = lax.broadcasted_iota(jnp.int32, norm.shape, 1)
    quarter = norm.shape[1] // slots // place_ref[2]
    slot_of = lax.rem(lanes // quarter, slots)
    scale, far_scale = jnp.zeros_like(norm), jnp.zeros_like(norm)
    for slot in range(slots):
        scale = jnp.where(slot_of == slot, delta_ref[place_ref[0] + slot], scale)
        far_scale = jnp.where(slot_of == slot, delta_ref[place_ref[1] + slot], far_scale)
    surplus = scale * (1.0 - jnp.exp(merged_ref[2:3, :] - norm))
    columns = as_columns(
        jnp.concatenate([surplus, norm, scale, norm, far_ref[0:1, :], far_scale, norm, norm], 0)
    )
    column_ref[...] = columns
    factor_ref[...] = -columns[:, 2:3] * jnp.exp(tops_ref[...] - columns[:, 1:2])


def vocab_scale(delta, place, norm, merged, far, tops, slots):
    smem = pl.BlockSpec(memory_space=pltpu.SMEM)
    return pl.pallas_call(
        functools.partial(vocab_scale_kernel, slots),
        in_specs=[smem, smem] + [VMEM] * 4,
        out_specs=[VMEM] * 2,
        out_shape=[jax.ShapeDtypeStruct(tops.shape, single)] * 2,
        compiler_params=pltpu.CompilerParams(vmem_limit_bytes=12 * 1024 * 1024),
        cost_estimate=BRIEF,
        name="vocab_scale",
    )(delta, place, norm, merged, far, tops)


def scaled_backward_kernel(slots, delta_ref, place_ref, kept_ref, arrived_ref, *refs):
    shape = kept_ref.shape
    slot_of = lax.broadcasted_iota(jnp.int32, (shape[0], LANES), 0) // (shape[0] // slots)
    scale = jnp.zeros(slot_of.shape, single)
    for slot in range(slots):
        scale = jnp.where(slot_of == slot, delta_ref[place_ref[0] + slot], scale)
    upstream = (kept_ref[...].astype(single) + arrived_ref[...].astype(single)) * scale[:, :1]
    norm_backward_rows(upstream, *refs)


def scaled_backward(delta, place, kept, arrived, hidden, gain, slots):
    shape = hidden.shape
    smem = pl.BlockSpec(memory_space=pltpu.SMEM)
    return pl.pallas_call(
        functools.partial(scaled_backward_kernel, slots),
        in_specs=[smem, smem] + [VMEM] * 4,
        out_specs=[VMEM] * 3,
        out_shape=[
            jax.ShapeDtypeStruct(shape, single),
            jax.ShapeDtypeStruct(shape, bfloat),
            jax.ShapeDtypeStruct((3, shape[1]), single),
        ],
        compiler_params=pltpu.CompilerParams(vmem_limit_bytes=12 * 1024 * 1024),
        cost_estimate=BRIEF,
        name="norm_backward",
    )(delta, place, kept.reshape(shape), arrived.reshape(shape), hidden, row(gain))


def marginal_objective(seq_values, doc_scores, member, length):
    joint = doc_scores + seq_values / length
    masked = jnp.where(member, joint[None, :], -1e30)
    top = jnp.max(masked, 1, keepdims=True)
    unscaled = jnp.where(member, jnp.exp(masked - top), 0.0)
    total = jnp.sum(unscaled, 1, keepdims=True)
    marginal = top[:, 0] + jnp.log(total[:, 0])
    posterior = unscaled / total
    entropy = -jnp.sum(jnp.where(member, posterior * (joint[None, :] - marginal[:, None]), 0.0), 1)
    return jnp.mean(-marginal + ENTROPY_WEIGHT * entropy)


def on_device(
    dp,
    mp,
    targets,
    labels,
    passages,
    slot_question,
    slot_passage,
    score_table,
    score_index,
    query_weight,
    query_bias,
    key_weight,
    value_weight,
    value_bias,
    output_weight,
    output_bias,
    first_gain,
    first_shift,
    probe_weight,
    probe_bias,
    address_weight,
    content_weight,
    content_bias,
    merged_weight,
    merged_bias,
    second_gain,
    second_shift,
    expand_weight,
    expand_bias,
    shrink_weight,
    shrink_bias,
    third_gain,
    third_shift,
    embedding,
):
    group = lax.axis_index("dp")
    member_index = lax.axis_index("mp")
    own_questions, length, width = targets.shape
    questions = own_questions * dp
    pair_count = slot_passage.shape[0]
    store_count, passage_length = (passages.shape[0], passages.shape[1])
    vocab_share = embedding.shape[0]
    local_width = query_weight.shape[1]
    quarter = length // mp
    assert own_questions == 1

    token = [score_table]

    free = [False]

    def through(*values):
        if not free[0]:
            values = tie(*values, token[0])
            token[0] = values[-1]
            values = values[:-1]
        return values if len(values) > 1 else values[0]

    mp_order = bits_of(mp)[::-1]
    mp_table = relative_of(mp_order)
    dp_bits = bits_of(dp)
    dp_order = dp_bits[::-1]
    dp_table = relative_of(dp_order)
    fast = dp >= 4 and width % (dp * LANES) == 0
    far = dp_bits[-1]

    def to_own(rows, count):
        natural = rows.reshape((count, mp, quarter) + rows.shape[2:])
        return jnp.moveaxis(xor_take(mp_table, member_index, natural, 1), 1, 0)

    def to_natural(rows, count):
        shaped = rows.reshape((mp, count, quarter) + rows.shape[1:])
        return jnp.moveaxis(natural_order(mp_table, member_index, shaped, 0), 0, 1)

    def mp_scatter_steps(halves):
        assert len(mp_order) == 2
        sent, kept = through(*halves)
        arrived = swap(sent, "mp", mp, mp_order[1])
        yield None
        sent, kept = through(*add_halves(kept, through(arrived)))
        arrived = swap(sent, "mp", mp, mp_order[0])
        yield None
        yield kept, through(arrived)

    def mp_gather_steps(own):
        own = through(own)
        held = [own, swap(own, "mp", mp, mp_order[0]), swap(own, "mp", mp, mp_order[1])]
        yield None
        held[1] = through(held[1])
        held.append(swap(held[1], "mp", mp, mp_order[1]))
        yield None
        yield through(*held)

    def dp_scatter_steps(halves, order):
        for bit in reversed(order):
            sent, kept = through(*halves)
            arrived = swap(sent, "dp", dp, bit)
            yield None
            if bit == order[0]:
                yield kept, through(arrived)
            else:
                halves = add_halves(kept, through(arrived))

    def last(steps):
        for value in steps:
            pass
        return value

    my_questions = lax.dynamic_slice_in_dim(slot_question, group * pair_count, pair_count)
    every = jnp.arange(own_questions, dtype=jnp.int32)
    quarters = member_index ^ jnp.asarray(mp_table, jnp.int32)
    place = (
        quarters[:, None] * quarter + jnp.arange(quarter, dtype=jnp.int32)[None, :]
    ).reshape(length)
    places_of = (
        jnp.broadcast_to(place[:, None], (length, LANES)),
        jnp.broadcast_to(place[None, :], (8, length)),
    )
    inputs = to_own(targets, own_questions)

    def by_question(rows):
        return jnp.moveaxis(rows.reshape(mp, own_questions, quarter, -1), 0, 1).reshape(
            own_questions, length, -1
        )

    inputs = inputs.reshape(-1, width)
    self_queries = by_question((matmul(inputs, query_weight) + query_bias).astype(bfloat))
    self_addresses = by_question(matmul(inputs, key_weight).astype(bfloat))
    self_contents = by_question((matmul(inputs, value_weight) + value_bias).astype(bfloat))
    self_flat = attend_forward(
        self_queries, self_addresses, self_contents, every, every, mp, places_of
    ).reshape(-1, local_width)
    kept, arrived = last(mp_scatter_steps(product_halves([self_flat], [output_weight])))
    first_in, first_norm, first_low = norm_forward(
        kept, arrived, inputs[:quarter], output_bias, first_gain, first_shift
    )
    first_full, probe_own = project(last(mp_gather_steps(first_low)), probe_weight, probe_bias)
    probe_own = by_question(probe_own)

    def where_slots(order):
        spots = jnp.asarray(places(relative_of(order)), jnp.int32)
        return spots[group ^ (my_questions // own_questions)] * own_questions + (
            my_questions % own_questions
        )

    probe_order = dp_bits[::-1]
    return_order = dp_bits[:1] + dp_bits[:0:-1]
    return_bins = where_slots(return_order)
    state_order = probe_order
    state_bins = where_slots(state_order)
    first_order = dp_bits[:1] + dp_bits[:0:-1]
    probe_bins = where_slots(probe_order)
    first_bins = where_slots(first_order)
    def label_index(slots):
        wanted = to_own(jnp.take(labels, slots, axis=0, mode="clip"), pair_count).reshape(-1)
        return wanted - member_index * vocab_share

    local_index = label_index(my_questions)
    inside = (local_index >= 0) & (local_index < vocab_share)
    label_places = jnp.clip(local_index, 0, vocab_share - 1)
    gather = gather_both_steps(
        (probe_own, first_low.reshape(own_questions, quarter, width)),
        "dp",
        dp,
        (probe_order, first_order),
    )
    for step in range(len(dp_bits)):
        next(gather)
    label_rows = through(jnp.take(embedding, through(label_places), axis=0, mode="clip"))
    probe_all, first_all = next(gather)
    probe_all = probe_all.reshape(questions, length, local_width)
    first_all = first_all.reshape(questions, quarter, width)
    passage_rows = passages.reshape(-1, width)
    stored_addresses = matmul(passage_rows, address_weight).astype(bfloat)
    stored_contents = (matmul(passage_rows, content_weight) + content_bias).astype(bfloat)
    stored_addresses = stored_addresses.reshape(store_count, passage_length, local_width)
    stored_contents = stored_contents.reshape(store_count, passage_length, local_width)

    cross_flat = attend_forward(
        probe_all, stored_addresses, stored_contents, probe_bins, slot_passage, mp
    ).reshape(-1, local_width)
    first_slots = pick(first_all, first_bins).reshape(-1, width)
    kept, arrived = last(mp_scatter_steps(product_halves([cross_flat], [merged_weight])))
    second_in, second_norm, low = norm_forward(
        kept, arrived, first_slots, merged_bias, second_gain, second_shift
    )
    second_low, expanded, activated, sent, kept = feed_forward(
        last(mp_gather_steps(low)), expand_weight, expand_bias, shrink_weight
    )
    kept, arrived = last(mp_scatter_steps((sent, kept)))
    third_in, third_norm, low = norm_forward(
        kept, arrived, second_norm, shrink_bias, third_gain, third_shift
    )
    def order_table(order):
        if not fast:
            return jnp.arange(width // LANES, dtype=jnp.int32)
        return group ^ jnp.asarray(relative_of(order), jnp.int32)

    order_a = dp_bits[::-1]
    order_b = order_a if dp < 4 else [dp_bits[-1], dp_bits[0]] + dp_bits[1:-1]
    third_pieces = last(mp_gather_steps(low))
    third_low, third_moved = order_columns(third_pieces, order_table(order_a))
    far_pieces = [swap(piece, "dp", dp, far) for piece in third_pieces[: mp // 2]]

    def label_lanes(index):
        return jnp.broadcast_to(index[:, None], (index.shape[0], LANES))

    own_labels = label_lanes(local_index)
    third_low = through(third_low)
    entry_weights, entry_mix, entry_tops, local_stats = vocab_forward(
        third_low, embedding, own_labels, label_rows
    )
    local_stats, *far_pieces = through(local_stats, *far_pieces)
    entry_tile = vocab_tile(vocab_share)
    stats = local_stats
    for index, bit in reversed(list(enumerate(mp_order))):
        stats = merge_stats(stats, through(swap(stats, "mp", mp, bit)), mp, index)
    norms = through(row_norms(stats, mp, pair_count))
    far_norms = swap(norms, "dp", dp, far)
    far_group = group ^ far
    place = jnp.stack([group * pair_count, far_group * pair_count, mp, vocab_share]).astype(jnp.int32)
    sent, kept = vocab_part(place, norms, stats, local_stats, label_rows, own_labels, entry_mix)
    steps = mp_scatter_steps((sent, kept))
    next(steps)
    far_norms = through(far_norms)
    every_likelihood = jnp.stack([norms[1, :pair_count], far_norms[1, :pair_count]])
    arrived = swap(every_likelihood, "dp", dp, dp_order[1])
    next(steps)
    for bit in dp_order[2:]:
        every_likelihood = jnp.concatenate([every_likelihood, through(arrived)], 0)
        arrived = swap(every_likelihood, "dp", dp, bit)
    far_pieces += [swap(piece, "mp", mp, mp_order[-1]) for piece in far_pieces]
    every_likelihood = jnp.concatenate([every_likelihood, through(arrived)], 0)
    every_likelihood = natural_order(dp_table, group, every_likelihood, 0).reshape(-1)
    doc_scores = jnp.take(token[0], score_index)
    member = slot_question[None, :] == jnp.arange(questions, dtype=jnp.int32)[:, None]

    def scored(values_all):
        return marginal_objective(values_all, doc_scores, member, length)

    objective, pullback = jax.vjp(scored, every_likelihood)
    likelihood_delta = pullback(jnp.ones_like(objective) * (questions * length))[0]
    far_labels = label_lanes(
        label_index(lax.dynamic_slice_in_dim(slot_question, far_group * pair_count, pair_count))
    )
    factors, values = vocab_scale(
        likelihood_delta, place, norms, stats, far_norms, entry_tops, pair_count
    )
    far_third, far_moved = order_columns(through(*far_pieces), order_table(order_a))

    objective = through(objective)

    class ColumnSum:
        def __init__(self, halves, order):
            self.sent, self.kept = through(*halves)
            self.bits = order[::-1]
            self.arrived = None

        def send(self):
            if fast:
                self.sent = through(self.sent)
                self.arrived = swap(self.sent, "dp", dp, self.bits[0])
                self.bits = self.bits[1:]

        def add(self):
            if fast:
                self.arrived, self.kept = through(self.arrived, self.kept)
                self.sent, self.kept = add_columns(self.kept, self.arrived)

        def step(self):
            self.add()
            self.send()

        def wait(self):
            if fast:
                self.arrived = through(self.arrived)

    def finish(parts):
        if not fast:
            slopes = [
                lax.psum_scatter(
                    jnp.concatenate([part.kept, part.sent], 1), "dp", scatter_dimension=1, tiled=True
                )
                for part in parts
            ]
            return jnp.concatenate(slopes, 0).astype(single)
        assert not any(part.bits for part in parts)
        return finish_sums([part.kept for part in parts], [part.arrived for part in parts])

    slope_tile = entry_tile // 2 if entry_tile % (2 * LANES) == 0 else entry_tile
    side = (group // far).astype(jnp.int32).reshape(1)
    tiles = vocab_share // slope_tile // 2 if fast else vocab_share // slope_tile
    cuts = [-(-tiles * i // 7) for i in CUTS]

    def table_sum(index):
        first, count = cuts[index], cuts[index + 1] - cuts[index]
        if fast:
            halves = half_slope(
                side * tiles,
                entry_weights,
                embedding,
                through(factors),
                own_labels,
                values,
                far_third,
                far_labels,
                third_moved,
                far_moved,
                first,
                count,
                slope_tile,
            )
        else:
            halves = vocab_slope(
                entry_weights,
                through(factors),
                own_labels,
                values,
                third_low,
                order_table(order_a),
                first,
                count,
                slope_tile,
            )
        return ColumnSum(halves, order_a)

    def group_sum(pairs, order):
        pairs = [(through(pairs[0][0]), pairs[0][1])] + pairs[1:]
        return ColumnSum(slope_group(pairs, order_table(order)), order)

    sums = {}
    makers = {
        "a": lambda: table_sum(0),
        "b": lambda: table_sum(1),
        "c": lambda: table_sum(2),
        "f": lambda: group_sum(
            [(activated, feed_delta), (expanded_delta, second_low)], orders[ORDERS["f"]]
        ),
        "p": lambda: group_sum(
            [
                (cross_flat, recall_delta),
                (address_delta, passage_rows),
                (content_delta, passage_rows),
                (probe_flat, first_full),
                (self_flat, self_delta),
            ],
            orders[ORDERS["p"]],
        ),
        "s": lambda: group_sum(
            [
                (query_flat, inputs),
                (key_flat, inputs),
                (value_flat, inputs),
                (jnp.eye(16, dtype=bfloat), vectors.astype(bfloat)),
            ],
            orders[ORDERS["s"]],
        ),
    }
    orders = {"y": order_a, "z": order_b}

    def at(point):
        free[0] = free[0] or point >= FREE
        for name, action in PLAN[point]:
            if name == "t":
                next(state_steps)
            elif action == "make":
                sums[name] = makers[name]()
            else:
                getattr(sums[name], action)()

    at(0)
    at(1)
    kept, arrived = next(steps)
    third_back, feed_low, third_sums = scaled_backward(
        likelihood_delta, place, kept, arrived, third_in, third_gain, pair_count
    )
    steps = mp_gather_steps(feed_low)
    next(steps)
    at(2)
    next(steps)
    at(3)
    feed_delta, expanded_delta, bias_expand, sent, kept = feed_backward(
        next(steps), expand_weight, shrink_weight, expanded
    )
    steps = mp_scatter_steps((sent, kept))
    next(steps)
    at(4)
    next(steps)
    at(5)
    parts = next(steps)
    at(6)
    second_back, recall_low, second_sums = norm_backward(
        parts + (third_back,), second_in, second_gain
    )
    steps = mp_gather_steps(recall_low)
    next(steps)
    state_steps = dp_scatter_steps(
        tuple(
            value.reshape(-1, width)
            for value in bin_rows(
                second_back.reshape(pair_count, quarter, width), state_bins, questions
            )
        ),
        state_order,
    )
    at(7)
    next(steps)
    at(8)
    recall_delta, mixed_delta = project(
        next(steps), merged_weight, jnp.zeros((local_width,), single), True
    )
    probe_binned, address_delta, content_delta = attend_backward(
        probe_all,
        stored_addresses,
        stored_contents,
        mixed_delta.reshape(mp, pair_count, quarter, local_width),
        probe_bins,
        slot_passage,
        return_bins,
    )
    address_delta = address_delta.reshape(-1, local_width)
    content_delta = content_delta.reshape(-1, local_width)

    half = questions // 2
    steps = dp_scatter_steps(
        (
            probe_binned[half:].reshape(-1, local_width),
            probe_binned[:half].reshape(-1, local_width),
        ),
        return_order,
    )
    at(9)
    next(steps)
    at(10)
    for unused in range(len(dp_bits) - 2):
        next(steps)
    at(11)
    next(steps)
    at(12)
    probe_parts = next(steps)
    at(13)
    probe_flat = (
        probe_parts[0] + probe_parts[1].astype(single)
    ).astype(bfloat)

    bias_content = jnp.sum(content_delta, 0, dtype=single)
    passages_slope = lax.psum(
        (outer_rows(address_delta, address_weight) + outer_rows(content_delta, content_weight)).astype(bfloat),
        "mp",
    ).astype(single).reshape(passages.shape)

    bias_probe = jnp.sum(probe_flat, 0, dtype=single)
    steps = mp_scatter_steps(product_halves([probe_flat], [probe_weight], True))
    next(steps)
    at(14)
    next(steps)
    at(15)
    state_parts = last(state_steps)
    first_back, self_low, first_sums = norm_backward(
        next(steps) + tuple(state_parts), first_in, first_gain
    )
    steps = mp_gather_steps(self_low)
    next(steps)
    at(16)
    next(steps)
    at(17)
    self_delta, self_mixed_delta = project(
        next(steps), output_weight, jnp.zeros((local_width,), single), True
    )
    self_deltas = attend_backward(
        self_queries,
        self_addresses,
        self_contents,
        self_mixed_delta.reshape(mp, own_questions, quarter, local_width),
        every,
        every,
        every,
        places_of,
    )
    query_flat, key_flat, value_flat = (
        jnp.moveaxis(delta.reshape(own_questions, mp, quarter, local_width), 1, 0).reshape(
            -1, local_width
        )
        for delta in self_deltas
    )
    steps = mp_scatter_steps(
        product_halves(
            [query_flat, key_flat, value_flat], [query_weight, key_weight, value_weight], True
        )
    )
    shared = total_over(
        jnp.concatenate([first_sums, second_sums, third_sums], 0), "mp", mp, mp_order
    )
    bias_query = jnp.sum(query_flat, 0, dtype=single)
    bias_value = jnp.sum(value_flat, 0, dtype=single)
    quads = jnp.stack([bias_query, bias_value, bias_probe, bias_content])
    quads = quads.reshape(4, dp, local_width // dp).swapaxes(0, 1).reshape(1, width)
    vectors = jnp.concatenate([shared, bias_expand, quads, jnp.zeros((5, width), single)], 0)
    next(steps)
    at(18)
    next(steps)
    at(19)
    kept, arrived = next(steps)
    input_low = (kept + arrived.astype(single) + first_back).astype(bfloat)
    steps = mp_gather_steps(input_low)
    next(steps)
    at(20)
    next(steps)
    at(21)
    targets_slope = to_natural(jnp.concatenate(next(steps), 0), own_questions)
    targets_slope = targets_slope.reshape(targets.shape).astype(single)
    at(22)
    table_parts = [sums[name] for name in "abc"]
    if fast:
        embedding_slope = place_halves(
            side, [part.kept for part in table_parts], [part.arrived for part in table_parts]
        )
    else:
        embedding_slope = finish(table_parts)
    feed_slopes = finish([sums["f"]])
    probe_slopes = finish([sums["p"]])
    self_slopes = finish([sums["s"]])
    hidden = expanded.shape[1]

    def parts_of(slopes, counts):
        edges = [sum(counts[:i]) for i in range(len(counts) + 1)]
        return [slopes[a:b] for a, b in zip(edges, edges[1:])]

    shrink_slope, expand_slope = parts_of(feed_slopes, [hidden] * 2)
    merged_slope, address_slope, content_slope, probe_slope, output_slope = parts_of(
        probe_slopes, [local_width] * 5
    )
    query_slope, key_slope, value_slope, vectors = parts_of(self_slopes, [local_width] * 3 + [16])
    expand_slope, address_slope, content_slope = expand_slope.T, address_slope.T, content_slope.T
    probe_slope, query_slope, key_slope, value_slope = (
        slope.T for slope in (probe_slope, query_slope, key_slope, value_slope)
    )
    (
        bias_output,
        first_gain_slope,
        first_shift_slope,
        bias_merged,
        second_gain_slope,
        second_shift_slope,
        bias_shrink,
        third_gain_slope,
        third_shift_slope,
        bias_expand,
    ) = (vectors[i] for i in range(10))
    bias_query, bias_value, bias_probe, bias_content = vectors[10].reshape(4, local_width // dp)
    return (
        objective,
        targets_slope,
        passages_slope,
        query_slope,
        bias_query,
        key_slope,
        value_slope,
        bias_value,
        output_slope,
        bias_output,
        first_gain_slope,
        first_shift_slope,
        probe_slope,
        bias_probe,
        address_slope,
        content_slope,
        bias_content,
        merged_slope,
        bias_merged,
        second_gain_slope,
        second_shift_slope,
        expand_slope,
        bias_expand,
        shrink_slope,
        bias_shrink,
        third_gain_slope,
        third_shift_slope,
        embedding_slope,
    )


def solution(mesh):
    return jax.shard_map(
        functools.partial(on_device, mesh.shape["dp"], mesh.shape["mp"]),
        mesh=mesh,
        in_specs=(
            P("dp", None, None),
            P(),
            P("dp", None, None),
            P(),
            P("dp"),
            P(),
            P(),
            P(None, "mp"),
            P("mp"),
            P(None, "mp"),
            P(None, "mp"),
            P("mp"),
            P("mp", None),
            P(),
            P(),
            P(),
            P(None, "mp"),
            P("mp"),
            P(None, "mp"),
            P(None, "mp"),
            P("mp"),
            P("mp", None),
            P(),
            P(),
            P(),
            P(None, "mp"),
            P("mp"),
            P("mp", None),
            P(),
            P(),
            P(),
            P("mp", None),
        ),
        out_specs=(
            P(),
            P("dp", None, None),
            P("dp", None, None),
            P("dp", "mp"),
            P(("mp", "dp")),
            P("dp", "mp"),
            P("dp", "mp"),
            P(("mp", "dp")),
            P("mp", "dp"),
            P("dp"),
            P("dp"),
            P("dp"),
            P("dp", "mp"),
            P(("mp", "dp")),
            P("dp", "mp"),
            P("dp", "mp"),
            P(("mp", "dp")),
            P("mp", "dp"),
            P("dp"),
            P("dp"),
            P("dp"),
            P("dp", "mp"),
            P(("mp", "dp")),
            P("mp", "dp"),
            P("dp"),
            P("dp"),
            P("dp"),
            P("mp", "dp"),
        ),
        check_vma=False,
    )
```

```python
import functools

import jax
import jax.numpy as jnp
from jax import lax
from jax.experimental import pallas as pl
from jax.experimental.pallas import tpu as pltpu
from jax.sharding import PartitionSpec as P

HD = 64
LANES = 128
EPSILON = 1e-05
ENTROPY_WEIGHT = 0.5
BRIEF = pl.CostEstimate(flops=0, bytes_accessed=0, transcendentals=0)
bfloat = jnp.bfloat16

CUTS = (0, 2, 4, 7)
FREE = 99
ORDERS = {"f": "z", "p": "y", "s": "z"}
ORDERS = {"f": "z", "p": "y", "s": "z"}
PLAN = (
    (),
    (),
    (("a", "make"), ("a", "send"),),
    (),
    (),
    (("f", "make"), ("f", "send"),),
    (),
    (("b", "make"), ("a", "add"), ("a", "send"),),
    (("b", "send"),),
    (),
    (("t", "step"), ("f", "add"),),
    (("c", "make"), ("t", "step"),),
    (("a", "add"), ("a", "send"), ("b", "add"), ("b", "send"),),
    (("c", "send"), ("t", "step"), ("f", "send"),),
    (),
    (),
    (),
    (),
    (("b", "add"), ("b", "send"), ("s", "make"), ("s", "send"),),
    (("p", "make"), ("p", "send"),),
    (("f", "add"), ("f", "send"), ("c", "add"), ("c", "send"),),
    (),
    (("p", "add"), ("p", "send"), ("s", "add"), ("s", "send"), ("c", "add"), ("c", "send"), ("s", "add"), ("s", "send"), ("p", "add"), ("p", "send"), ("a", "wait"), ("b", "wait"), ("f", "wait"), ("c", "wait"), ("p", "wait"), ("s", "wait"),),
    (),
    (),
    (),
    (),
)
single = jnp.float32


def matmul(left, right):
    return jnp.dot(left, right, preferred_element_type=single)


def inner_rows(left, right):
    return lax.dot_general(left, right, (((0,), (0,)), ((), ())), preferred_element_type=single)


def outer_rows(left, right):
    return lax.dot_general(left, right, (((1,), (1,)), ((), ())), preferred_element_type=single)


def bits_of(count):
    bits = []
    while (1 << len(bits)) < count:
        bits.append(1 << len(bits))
    return bits


def swap(value, axis, count, bit):
    return lax.ppermute(value, axis, [(i, i ^ bit) for i in range(count)])


def relative_of(order):
    table = [0]
    for bit in order:
        table = table + [r ^ bit for r in table]
    return table


def gather_blocks(own, axis, count, order):
    held = own[None]
    for bit in order:
        held = jnp.concatenate([held, swap(held, axis, count, bit)], 0)
    return held


def scatter_blocks(parts, axis, count, order):
    for bit in reversed(order):
        half = parts.shape[0] // 2
        arrived = swap(parts[half:].astype(bfloat), axis, count, bit)
        parts = parts[:half] + arrived.astype(single)
    return parts[0]


def tie(*values):
    return lax.optimization_barrier(values)


def gather_both_steps(owns, axis, count, orders):
    helds = [own[None] for own in owns]
    for bits in zip(*orders):
        arrived = [swap(held, axis, count, bit) for held, bit in zip(helds, bits)]
        yield None
        arrived = tie(*arrived)
        helds = [jnp.concatenate([held, more], 0) for held, more in zip(helds, arrived)]
    yield helds


def total_over(value, axis, count, order):
    for bit in order:
        value = value + swap(value, axis, count, bit)
    return value


def xor_take(table, me, array, axis):
    return jnp.take(array, me ^ jnp.asarray(table, jnp.int32), axis=axis, mode="clip")


def places(table):
    inverse = [0] * len(table)
    for position, relative in enumerate(table):
        inverse[relative] = position
    return inverse


def natural_order(table, me, array, axis):
    count = len(table)
    order = jnp.asarray(places(table), jnp.int32)[me ^ jnp.arange(count, dtype=jnp.int32)]
    return jnp.take(array, order, axis=axis, mode="clip")


VMEM = pl.BlockSpec(memory_space=pltpu.VMEM)


def run_whole(kernel, name, outs, *operands, scratch=()):
    return pl.pallas_call(
        kernel,
        in_specs=[VMEM] * len(operands),
        out_specs=[VMEM] * len(outs),
        out_shape=[jax.ShapeDtypeStruct(shape, dtype) for shape, dtype in outs],
        scratch_shapes=list(scratch),
        compiler_params=pltpu.CompilerParams(vmem_limit_bytes=16 * 1024 * 1024),
        cost_estimate=BRIEF,
        name=name,
    )(*operands)


def row(vector):
    return vector.reshape(1, -1).astype(single)


def norm_forward_kernel(kept_ref, arrived_ref, state_ref, bias_ref, gain_ref, shift_ref, in_ref, out_ref, low_ref):
    hidden = (
        state_ref[...].astype(single)
        + (kept_ref[...].astype(single) + arrived_ref[...].astype(single))
        + bias_ref[...]
    )
    in_ref[...] = hidden
    center = hidden - jnp.mean(hidden, -1, keepdims=True)
    spread = jnp.mean(center * center, -1, keepdims=True)
    normal = center * lax.rsqrt(spread + EPSILON) * gain_ref[...] + shift_ref[...]
    out_ref[...] = normal
    low_ref[...] = normal.astype(bfloat)


def norm_forward(kept, arrived, state, bias, gain, shift):
    shape = state.shape
    return run_whole(
        norm_forward_kernel,
        "norm_forward",
        [(shape, single), (shape, single), (shape, bfloat)],
        kept.reshape(shape),
        arrived.reshape(shape),
        state,
        row(bias),
        row(gain),
        row(shift),
    )


def norm_backward_kernel(count, *refs):
    upstream = refs[0][...].astype(single)
    for ref in refs[1:count]:
        upstream = upstream + ref[...].astype(single)
    norm_backward_rows(upstream, *refs[count:])


def norm_backward_rows(upstream, hidden_ref, gain_ref, out_ref, low_ref, sums_ref):
    hidden = hidden_ref[...]
    center = hidden - jnp.mean(hidden, -1, keepdims=True)
    spread = jnp.mean(center * center, -1, keepdims=True)
    inverse = lax.rsqrt(spread + EPSILON)
    normal = center * inverse
    scaled = upstream * gain_ref[...]
    delta = inverse * (
        scaled
        - jnp.mean(scaled, -1, keepdims=True)
        - normal * jnp.mean(scaled * normal, -1, keepdims=True)
    )
    low = delta.astype(bfloat)
    out_ref[...] = delta
    low_ref[...] = low
    sums_ref[0:1, :] = jnp.sum(low.astype(single), 0, keepdims=True)
    sums_ref[1:2, :] = jnp.sum(upstream * normal, 0, keepdims=True)
    sums_ref[2:3, :] = jnp.sum(upstream, 0, keepdims=True)


def norm_backward(parts, hidden, gain):
    shape = hidden.shape
    return run_whole(
        functools.partial(norm_backward_kernel, len(parts)),
        "norm_backward",
        [(shape, single), (shape, bfloat), ((3, shape[1]), single)],
        *(part.reshape(shape) for part in parts),
        hidden,
        row(gain),
    )


def erf_gelu(value):
    phi = 0.5 * (1.0 + lax.erf(value * 0.7071067811865476))
    return value * phi, phi


def join(pieces, full_ref):
    rows = pieces[0].shape[0]
    for index, piece in enumerate(pieces):
        full_ref[index * rows : (index + 1) * rows, :] = piece[...]


def feed_forward_kernel(count, *refs):
    expand_ref, bias_ref, shrink_ref, full_ref, hidden_ref, act_ref, sent_ref, kept_ref = refs[count:]
    join(refs[:count], full_ref)
    half = sent_ref.shape[0]
    for index in (1, 0):
        part = slice(index * half, (index + 1) * half)
        hidden = matmul(full_ref[part, :], expand_ref[...]) + bias_ref[...]
        hidden_ref[part, :] = hidden
        act = erf_gelu(hidden)[0].astype(bfloat)
        act_ref[part, :] = act
        out = matmul(act, shrink_ref[...])
        if index == 0:
            kept_ref[...] = out
        else:
            sent_ref[...] = out.astype(bfloat)


def feed_forward(pieces, expand, bias, shrink):
    rows, width = len(pieces) * pieces[0].shape[0], pieces[0].shape[1]
    hidden = expand.shape[1]
    return run_whole(
        functools.partial(feed_forward_kernel, len(pieces)),
        "feed_forward",
        [
            ((rows, width), bfloat),
            ((rows, hidden), single),
            ((rows, hidden), bfloat),
            ((rows // 2, width), bfloat),
            ((rows // 2, width), single),
        ],
        *pieces,
        expand,
        row(bias),
        shrink,
    )


def feed_backward_kernel(count, *refs):
    expand_ref, shrink_ref, hidden_ref, full_ref, delta_ref, sums_ref, sent_ref, kept_ref = refs[count:]
    join(refs[:count], full_ref)
    half = sent_ref.shape[0]
    sums = jnp.zeros(sums_ref.shape, single)
    for index in (1, 0):
        part = slice(index * half, (index + 1) * half)
        upstream = outer_rows(full_ref[part, :], shrink_ref[...])
        hidden = hidden_ref[part, :]
        slope = erf_gelu(hidden)[1] + hidden * jnp.exp(-0.5 * hidden * hidden) * 0.3989422804014327
        delta = (upstream * slope).astype(bfloat)
        delta_ref[part, :] = delta
        sums = sums + jnp.sum(delta.astype(single), 0, keepdims=True)
        out = outer_rows(delta, expand_ref[...])
        if index == 0:
            kept_ref[...] = out
        else:
            sent_ref[...] = out.astype(bfloat)
    sums_ref[...] = sums


def feed_backward(pieces, expand, shrink, hidden):
    rows, width = len(pieces) * pieces[0].shape[0], pieces[0].shape[1]
    return run_whole(
        functools.partial(feed_backward_kernel, len(pieces)),
        "feed_backward",
        [
            ((rows, width), bfloat),
            (hidden.shape, bfloat),
            ((1, hidden.shape[1]), single),
            ((rows // 2, width), bfloat),
            ((rows // 2, width), single),
        ],
        *pieces,
        expand,
        shrink,
        hidden,
    )


def project_kernel(count, transposed, *refs):
    weight_ref, bias_ref, full_ref, out_ref = refs[count:]
    join(refs[:count], full_ref)
    out = (outer_rows if transposed else matmul)(full_ref[...], weight_ref[...])
    out_ref[...] = (out + bias_ref[...]).astype(bfloat)


def project(pieces, weight, bias, transposed=False):
    rows, width = len(pieces) * pieces[0].shape[0], pieces[0].shape[1]
    return run_whole(
        functools.partial(project_kernel, len(pieces), transposed),
        "project",
        [((rows, width), bfloat), ((rows, bias.shape[0]), bfloat)],
        *pieces,
        weight,
        row(bias),
    )


def halves_kernel(count, transposed, *refs):
    lefts, weights, (sent_ref, kept_ref) = refs[:count], refs[count : 2 * count], refs[2 * count :]
    half = sent_ref.shape[0]
    product = outer_rows if transposed else matmul
    for part, out in ((slice(half, 2 * half), sent_ref), (slice(0, half), kept_ref)):
        total = product(lefts[0][part, :], weights[0][...])
        for left, weight in zip(lefts[1:], weights[1:]):
            total = total + product(left[part, :], weight[...])
        out[...] = total.astype(out.dtype)


def product_halves(lefts, weights, transposed=False):
    half = lefts[0].shape[0] // 2
    width = weights[0].shape[0] if transposed else weights[0].shape[1]
    return run_whole(
        functools.partial(halves_kernel, len(lefts), transposed),
        "product_halves",
        [((half, width), bfloat), ((half, width), single)],
        *lefts,
        *weights,
    )


def add_halves_kernel(kept_ref, arrived_ref, sent_ref, left_ref):
    half = kept_ref.shape[0] // 2
    sent_ref[...] = (kept_ref[half:, :].astype(single) + arrived_ref[half:, :].astype(single)).astype(bfloat)
    left_ref[...] = kept_ref[:half, :].astype(single) + arrived_ref[:half, :].astype(single)


def add_halves(kept, arrived):
    half, width = kept.shape[0] // 2, kept.shape[1]
    return run_whole(
        add_halves_kernel,
        "add_halves",
        [((half, width), bfloat), ((half, width), single)],
        kept,
        arrived,
    )


def add_columns_kernel(kept_ref, arrived_ref, sent_ref, left_ref):
    half = sent_ref.shape[1]
    total = kept_ref[...].astype(single) + arrived_ref[...].astype(single)
    sent_ref[...] = total[:, half:].astype(bfloat)
    left_ref[...] = total[:, :half].astype(bfloat)


def add_columns(kept, arrived):
    rows, width = kept.shape
    return run_whole(
        add_columns_kernel, "add_columns", [((rows, width // 2), bfloat)] * 2, kept, arrived
    )


def bin_rows_kernel(bins_ref, value_ref, sent_ref, kept_ref, sums):
    sums[...] = jnp.zeros_like(sums)
    for slot in range(value_ref.shape[0]):
        sums[bins_ref[slot]] += value_ref[slot]
    half = sent_ref.shape[0]
    sent_ref[...] = sums[half:].astype(bfloat)
    kept_ref[...] = sums[:half]


def bin_rows(value, bins, count):
    shape = (count // 2,) + value.shape[1:]
    return pl.pallas_call(
        bin_rows_kernel,
        in_specs=[pl.BlockSpec(memory_space=pltpu.SMEM), VMEM],
        out_specs=[VMEM, VMEM],
        out_shape=[jax.ShapeDtypeStruct(shape, bfloat), jax.ShapeDtypeStruct(shape, single)],
        scratch_shapes=[pltpu.VMEM((count,) + value.shape[1:], single)],
        compiler_params=pltpu.CompilerParams(
            vmem_limit_bytes=8 * 1024 * 1024 + 6 * count * value.shape[1] * value.shape[2]
        ),
        cost_estimate=BRIEF,
        name="bin_rows",
    )(bins, value)


def vocab_tile(vocab_share):
    for tile in (1792, 896, 512, 256, 128):
        if vocab_share % tile == 0:
            return tile
    return vocab_share


def vocab_forward_kernel(
    state_ref, table_ref, label_ref, label_rows_ref, weight_ref, mixed_ref, tops_ref, stats_ref, top, sum_ref
):
    step = pl.program_id(0)
    rows = state_ref.shape[0]
    tile = table_ref.shape[0]
    block = min(rows, 1024)

    @pl.when(step == 0)
    def start():
        top[...] = jnp.full_like(top, -jnp.inf)
        sum_ref[...] = jnp.zeros_like(sum_ref)
        mixed_ref[...] = jnp.zeros_like(mixed_ref)
        tops_ref[...] = jnp.zeros_like(tops_ref)

    repeat = lambda value, count: jnp.concatenate([value] * count, 1) if count > 1 else value
    spans = tile // LANES
    for index in range(rows // block):
        part = pl.ds(index * block, block)
        logits = outer_rows(state_ref[part, :], table_ref[...])
        old = top[part, :]
        new = jnp.maximum(old, jnp.max(logits, -1, keepdims=True))
        lanes = lax.broadcasted_iota(jnp.int32, new.shape, 1)
        offset = label_ref[part, :] - step * tile
        shrink = jnp.exp(old - new)
        top[part, :] = new
        tops_ref[part, :] = jnp.where(lanes == step, new, tops_ref[part, :])
        sums = sum_ref[part, :] * shrink
        low = []
        for span in range(spans):
            weights = jnp.exp(logits[:, span * LANES : (span + 1) * LANES] - new)
            weights = jnp.where(lanes + span * LANES == offset, 0.0, weights)
            sums = sums + weights
            low.append(weights.astype(bfloat))
        sum_ref[part, :] = sums
        low = jnp.concatenate(low, 1)
        weight_ref[part, :] = low
        mixed_ref[part, :] = mixed_ref[part, :] * repeat(shrink, mixed_ref.shape[1] // LANES) + matmul(
            low, table_ref[...]
        )

    @pl.when(step == pl.num_programs(0) - 1)
    def finish():
        label = label_ref[...]
        entries = tile * pl.num_programs(0)
        inside = (label >= 0) & (label < entries)
        target = jnp.sum(
            state_ref[...].astype(single) * label_rows_ref[...].astype(single), -1, keepdims=True
        )
        target = jnp.where(inside, target, 0.0)
        total = jnp.sum(sum_ref[...], -1, keepdims=True)
        total = total + jnp.where(inside, jnp.exp(target - top[...]), 0.0)
        lanes = lax.broadcasted_iota(jnp.int32, label.shape, 1)
        columns = jnp.where(lanes == 0, top[...], jnp.where(lanes == 1, total, target))
        stats_ref[...] = jnp.swapaxes(columns, 0, 1)[:8, :]


def vocab_forward(states, table, label, label_rows):
    rows, width = states.shape
    entries = table.shape[0]
    tile = vocab_tile(entries)
    whole = lambda *shape: pl.BlockSpec(shape, lambda i: (0,) * len(shape))
    return pl.pallas_call(
        vocab_forward_kernel,
        grid=(entries // tile,),
        in_specs=[
            whole(rows, width),
            pl.BlockSpec((tile, width), lambda i: (i, 0)),
            whole(rows, LANES),
            whole(rows, width),
        ],
        out_specs=[pl.BlockSpec((rows, tile), lambda i: (0, i)), VMEM, VMEM, VMEM],
        out_shape=[
            jax.ShapeDtypeStruct((rows, entries), bfloat),
            jax.ShapeDtypeStruct((rows, width), single),
            jax.ShapeDtypeStruct((rows, LANES), single),
            jax.ShapeDtypeStruct((8, rows), single),
        ],
        scratch_shapes=[pltpu.VMEM((rows, LANES), single)] * 2,
        compiler_params=pltpu.CompilerParams(
            dimension_semantics=("arbitrary",), vmem_limit_bytes=40 * 1024 * 1024
        ),
        cost_estimate=BRIEF,
        name="vocab_forward",
    )(states, table, label, label_rows)


def vocab_slope_kernel(first, ratio, order_ref, weight_ref, factor_ref, label_ref, column_ref, state_ref, sent_ref, kept_ref, moved):
    step = pl.program_id(0)
    tile = weight_ref.shape[1]
    width = state_ref.shape[1]
    blocks = order_ref.shape[0]
    span = width // blocks

    @pl.when(step == 0)
    def start():
        for place in range(blocks):
            source = pl.multiple_of(order_ref[place] * span, span)
            moved[:, place * span : (place + 1) * span] = state_ref[:, pl.ds(source, span)]

    here = step + first
    factors = factor_ref[...]
    lanes = lax.broadcasted_iota(jnp.int32, factors.shape, 1)
    factor = jnp.sum(jnp.where(lanes == here // ratio, factors, 0.0), -1, keepdims=True)
    columns = lax.broadcasted_iota(jnp.int32, weight_ref.shape, 1) + here * tile
    delta = jnp.where(
        columns == label_ref[:, :1], column_ref[:, :1], weight_ref[...].astype(single) * factor
    ).astype(bfloat)
    half = width // 2
    slope = inner_rows(delta, moved[...])
    sent_ref[...] = slope[:, half:].astype(bfloat)
    kept_ref[...] = slope[:, :half].astype(bfloat)


def vocab_slope(weights, factors, label, values, states, order, first, count, tile):
    rows, width = states.shape
    whole = lambda *shape: pl.BlockSpec(shape, lambda i, o: (0,) * len(shape))
    half = pl.BlockSpec((tile, width // 2), lambda i, o: (i, 0))
    return pl.pallas_call(
        functools.partial(vocab_slope_kernel, first, vocab_tile(weights.shape[1]) // tile),
        grid_spec=pltpu.PrefetchScalarGridSpec(
            num_scalar_prefetch=1,
            grid=(count,),
            in_specs=[
                pl.BlockSpec((rows, tile), lambda i, o: (0, i + first)),
                whole(rows, LANES),
                whole(rows, LANES),
                whole(rows, LANES),
                whole(rows, width),
            ],
            out_specs=[half, half],
            scratch_shapes=[pltpu.VMEM((rows, width), bfloat)],
        ),
        out_shape=[jax.ShapeDtypeStruct((count * tile, width // 2), bfloat)] * 2,
        compiler_params=pltpu.CompilerParams(
            dimension_semantics=("arbitrary",), vmem_limit_bytes=56 * 1024 * 1024
        ),
        cost_estimate=BRIEF,
        name="vocab_slope",
    )(order, weights, factors, label, values, states)


def slope_group_kernel(count, order_ref, *refs):
    lefts, rights = refs[:count], refs[count : 2 * count]
    sent_ref, kept_ref, moved = refs[2 * count :]
    blocks = order_ref.shape[0]
    width = rights[0].shape[1]
    span, half = width // blocks, width // 2
    base = 0
    for index in range(count):
        rows, entries = lefts[index].shape
        if index == 0 or rights[index] is not rights[index - 1]:
            for place in range(blocks):
                source = pl.multiple_of(order_ref[place] * span, span)
                moved[:rows, place * span : (place + 1) * span] = rights[index][:, pl.ds(source, span)]
        right = moved[:rows, :]
        left = lefts[index][...]
        slope = inner_rows(left, right)
        sent_ref[base : base + entries, :] = slope[:, half:].astype(bfloat)
        kept_ref[base : base + entries, :] = slope[:, :half].astype(bfloat)
        base += entries


def slope_group(pairs, order):
    width = pairs[0][1].shape[1]
    total = sum(left.shape[1] for left, right in pairs)
    rows = max(left.shape[0] for left, right in pairs)
    lefts = [left for left, right in pairs]
    rights = [right for left, right in pairs]
    whole = pl.BlockSpec(memory_space=pltpu.VMEM)
    return pl.pallas_call(
        functools.partial(slope_group_kernel, len(pairs)),
        in_specs=[pl.BlockSpec(memory_space=pltpu.SMEM)] + [whole] * (2 * len(pairs)),
        out_specs=[whole, whole],
        out_shape=[jax.ShapeDtypeStruct((total, width // 2), bfloat)] * 2,
        scratch_shapes=[pltpu.VMEM((rows, width), bfloat)],
        compiler_params=pltpu.CompilerParams(vmem_limit_bytes=16 * 1024 * 1024),
        cost_estimate=BRIEF,
        name="slope_group",
    )(order, *lefts, *rights)


def head_weights(causal, places, query, address, lanes, head):
    own = (lanes // HD) == head
    scores = outer_rows(jnp.where(own, query, jnp.zeros_like(query)), address) * 0.125
    if causal:
        scores = jnp.where(places[0][:, :1] >= places[1][:1, :], scores, -1000000000.0)
    expo = jnp.exp(scores - jnp.max(scores, -1, keepdims=True))
    return own, expo / jnp.sum(expo, -1, keepdims=True)


def attend_forward_kernel(causal, bins_ref, stores_ref, query_ref, address_ref, content_ref, *refs):
    mixed_ref = refs[-1]
    places = [ref[...] for ref in refs[:-1]]
    length, width = query_ref.shape[1:]
    for pair in range(width // LANES):
        part = slice(pair * LANES, (pair + 1) * LANES)
        query, address, content = query_ref[0, :, part], address_ref[0, :, part], content_ref[0, :, part]
        lanes = lax.broadcasted_iota(jnp.int32, query.shape, 1)
        total = jnp.zeros(query.shape, single)
        for head in range(LANES // HD):
            own, weights = head_weights(causal, places, query, address, lanes, head)
            total = jnp.where(own, matmul(weights.astype(bfloat), content), total)
        shape = (mixed_ref.shape[0], mixed_ref.shape[2], LANES)
        mixed_ref[:, 0, :, part] = total.astype(bfloat).reshape(shape)


def attend_forward(queries, addresses, contents, bins, stores, parts, places=()):
    count = bins.shape[0]
    length, width = queries.shape[1:]
    stored = addresses.shape[1]
    return pl.pallas_call(
        functools.partial(attend_forward_kernel, bool(places)),
        grid_spec=pltpu.PrefetchScalarGridSpec(
            num_scalar_prefetch=2,
            grid=(count,),
            in_specs=[
                pl.BlockSpec((1, length, width), lambda i, b, s: (b[i], 0, 0)),
                pl.BlockSpec((1, stored, width), lambda i, b, s: (s[i], 0, 0)),
                pl.BlockSpec((1, stored, width), lambda i, b, s: (s[i], 0, 0)),
            ]
            + [pl.BlockSpec(place.shape, lambda i, b, s: (0, 0)) for place in places],
            out_specs=pl.BlockSpec((parts, 1, length // parts, width), lambda i, b, s: (0, i, 0, 0)),
        ),
        out_shape=jax.ShapeDtypeStruct((parts, count, length // parts, width), bfloat),
        compiler_params=pltpu.CompilerParams(
            dimension_semantics=("arbitrary",), vmem_limit_bytes=12 * 1024 * 1024
        ),
        cost_estimate=BRIEF,
        name="attend_forward",
    )(bins, stores, queries, addresses, contents, *places)


def attend_backward_kernel(
    causal, bins_ref, stores_ref, sums_ref, query_ref, address_ref, content_ref, upstream_ref, *refs
):
    query_out, address_out, content_out, query_sum, address_sum, content_sum = refs[-6:]
    places = [ref[...] for ref in refs[:-6]]
    step = pl.program_id(0)
    length, width = query_ref.shape[1:]

    @pl.when(step == 0)
    def start():
        query_sum[...] = jnp.zeros_like(query_sum)
        address_sum[...] = jnp.zeros_like(address_sum)
        content_sum[...] = jnp.zeros_like(content_sum)

    for pair in range(width // LANES):
        part = slice(pair * LANES, (pair + 1) * LANES)
        query, address, content = query_ref[0, :, part], address_ref[0, :, part], content_ref[0, :, part]
        upstream = upstream_ref[:, 0, :, part].reshape(length, LANES)
        lanes = lax.broadcasted_iota(jnp.int32, query.shape, 1)
        query_delta = jnp.zeros(query.shape, single)
        address_delta = jnp.zeros(address.shape, single)
        content_delta = jnp.zeros(address.shape, single)
        for head in range(LANES // HD):
            own, weights = head_weights(causal, places, query, address, lanes, head)
            weight_delta = outer_rows(jnp.where(own, upstream, jnp.zeros_like(upstream)), content)
            score_delta = (
                weights * (weight_delta - jnp.sum(weights * weight_delta, -1, keepdims=True))
            ).astype(bfloat)
            query_delta = jnp.where(own, matmul(score_delta, address), query_delta)
            address_delta = jnp.where(own, inner_rows(score_delta, query), address_delta)
            content_delta = jnp.where(own, inner_rows(weights.astype(bfloat), upstream), content_delta)
        query_sum[sums_ref[step], :, part] += query_delta * 0.125
        address_sum[stores_ref[step], :, part] += address_delta * 0.125
        content_sum[stores_ref[step], :, part] += content_delta

    @pl.when(step == pl.num_programs(0) - 1)
    def finish():
        query_out[...] = query_sum[...].astype(bfloat)
        address_out[...] = address_sum[...].astype(bfloat)
        content_out[...] = content_sum[...].astype(bfloat)


def attend_backward(queries, addresses, contents, upstream, bins, stores, sums, places=()):
    count = bins.shape[0]
    length, width = queries.shape[1:]
    stored = addresses.shape[1]
    whole = lambda shape: pl.BlockSpec(shape, lambda i, b, s, t: (0,) * len(shape))
    return pl.pallas_call(
        functools.partial(attend_backward_kernel, bool(places)),
        grid_spec=pltpu.PrefetchScalarGridSpec(
            num_scalar_prefetch=3,
            grid=(count,),
            in_specs=[
                pl.BlockSpec((1, length, width), lambda i, b, s, t: (b[i], 0, 0)),
                pl.BlockSpec((1, stored, width), lambda i, b, s, t: (s[i], 0, 0)),
                pl.BlockSpec((1, stored, width), lambda i, b, s, t: (s[i], 0, 0)),
                pl.BlockSpec((upstream.shape[0], 1) + upstream.shape[2:], lambda i, b, s, t: (0, i, 0, 0)),
            ]
            + [whole(place.shape) for place in places],
            out_specs=[whole(queries.shape), whole(addresses.shape), whole(addresses.shape)],
            scratch_shapes=[
                pltpu.VMEM(queries.shape, single),
                pltpu.VMEM(addresses.shape, single),
                pltpu.VMEM(addresses.shape, single),
            ],
        ),
        out_shape=[
            jax.ShapeDtypeStruct(queries.shape, bfloat),
            jax.ShapeDtypeStruct(addresses.shape, bfloat),
            jax.ShapeDtypeStruct(addresses.shape, bfloat),
        ],
        compiler_params=pltpu.CompilerParams(
            dimension_semantics=("arbitrary",),
            vmem_limit_bytes=12 * 1024 * 1024 + 10 * queries.size,
        ),
        cost_estimate=BRIEF,
        name="attend_backward",
    )(bins, stores, sums, queries, addresses, contents, upstream, *places)


def pick_kernel(bins_ref, value_ref, out_ref):
    out_ref[...] = value_ref[...]


def pick(value, bins):
    block = (1,) + value.shape[1:]
    return pl.pallas_call(
        pick_kernel,
        grid_spec=pltpu.PrefetchScalarGridSpec(
            num_scalar_prefetch=1,
            grid=(bins.shape[0],),
            in_specs=[pl.BlockSpec(block, lambda i, b: (b[i], 0, 0))],
            out_specs=pl.BlockSpec(block, lambda i, b: (i, 0, 0)),
        ),
        out_shape=jax.ShapeDtypeStruct(bins.shape + value.shape[1:], value.dtype),
        name="pick",
    )(bins, value)


def finish_kernel(count, *refs):
    base = 0
    for index in range(count):
        rows = refs[index].shape[0]
        refs[-1][base : base + rows, :] = refs[index][...].astype(single) + refs[count + index][
            ...
        ].astype(single)
        base += rows


def finish_sums(kept, arrived):
    total = sum(part.shape[0] for part in kept)
    whole = pl.BlockSpec(memory_space=pltpu.VMEM)
    return pl.pallas_call(
        functools.partial(finish_kernel, len(kept)),
        in_specs=[whole] * (2 * len(kept)),
        out_specs=whole,
        out_shape=jax.ShapeDtypeStruct((total, kept[0].shape[1]), single),
        compiler_params=pltpu.CompilerParams(vmem_limit_bytes=8 * 1024 * 1024),
        name="finish_sums",
    )(*kept, *arrived)


def order_columns_kernel(count, order_ref, *refs):
    pieces, (joined_ref, moved_ref) = refs[:count], refs[count:]
    rows, width = pieces[0].shape
    span = width // order_ref.shape[0]
    for index in range(count):
        part = slice(index * rows, (index + 1) * rows)
        joined_ref[part, :] = pieces[index][...]
        for place in range(order_ref.shape[0]):
            source = pl.multiple_of(order_ref[place] * span, span)
            moved_ref[part, place * span : (place + 1) * span] = pieces[index][:, pl.ds(source, span)]


def order_columns(pieces, order):
    shape = (len(pieces) * pieces[0].shape[0], pieces[0].shape[1])
    return pl.pallas_call(
        functools.partial(order_columns_kernel, len(pieces)),
        in_specs=[pl.BlockSpec(memory_space=pltpu.SMEM)] + [VMEM] * len(pieces),
        out_specs=[VMEM, VMEM],
        out_shape=[jax.ShapeDtypeStruct(shape, bfloat)] * 2,
        compiler_params=pltpu.CompilerParams(vmem_limit_bytes=8 * 1024 * 1024),
        cost_estimate=BRIEF,
        name="order_columns",
    )(order, *pieces)


def half_slope_kernel(
    first,
    ratio,
    base_ref,
    weight_ref,
    table_ref,
    factor_ref,
    label_ref,
    column_ref,
    far_ref,
    far_label_ref,
    moved_ref,
    far_moved_ref,
    sent_ref,
    kept_ref,
    delta,
):
    rows, tile = weight_ref.shape
    here = base_ref[0] + first + pl.program_id(0)
    factors = factor_ref[...]
    lanes = lax.broadcasted_iota(jnp.int32, factors.shape, 1)
    factor = jnp.sum(jnp.where(lanes == here // ratio, factors, 0.0), -1, keepdims=True)
    columns = lax.broadcasted_iota(jnp.int32, weight_ref.shape, 1) + here * tile
    logits = outer_rows(far_ref[...], table_ref[...])
    delta[:rows, :] = jnp.where(
        columns == label_ref[:, :1], column_ref[:, :1], weight_ref[...].astype(single) * factor
    ).astype(bfloat)
    hit = jnp.where(columns == far_label_ref[:, :1], 1.0, 0.0)
    delta[rows:, :] = (column_ref[:, 5:6] * (hit - jnp.exp(logits - column_ref[:, 4:5]))).astype(bfloat)
    slope = inner_rows(delta[:rows, :], moved_ref[...]) + inner_rows(delta[rows:, :], far_moved_ref[...])
    half = sent_ref.shape[1]
    part = pl.ds(pl.multiple_of(pl.program_id(0) * tile, tile), tile)
    sent_ref[part, :] = slope[:, half:].astype(bfloat)
    kept_ref[part, :] = slope[:, :half].astype(bfloat)


def half_slope(base, weights, table, factors, label, values, far, far_label, moved, far_moved, first, count, tile):
    rows, width = far.shape
    return pl.pallas_call(
        functools.partial(half_slope_kernel, first, vocab_tile(weights.shape[1]) // tile),
        grid_spec=pltpu.PrefetchScalarGridSpec(
            num_scalar_prefetch=1,
            grid=(count,),
            in_specs=[
                pl.BlockSpec((rows, tile), lambda i, b: (0, i + first + b[0])),
                pl.BlockSpec((tile, width), lambda i, b: (i + first + b[0], 0)),
                VMEM,
                VMEM,
                VMEM,
                VMEM,
                VMEM,
                VMEM,
                VMEM,
            ],
            out_specs=[VMEM, VMEM],
            scratch_shapes=[pltpu.VMEM((2 * rows, tile), bfloat)],
        ),
        out_shape=[jax.ShapeDtypeStruct((count * tile, width // 2), bfloat)] * 2,
        compiler_params=pltpu.CompilerParams(
            dimension_semantics=("arbitrary",), vmem_limit_bytes=32 * 1024 * 1024
        ),
        cost_estimate=BRIEF,
        name="half_slope",
    )(base, weights, table, factors, label, values, far, far_label, moved, far_moved)


def place_halves_kernel(count, side_ref, *refs):
    out_ref = refs[-1]
    half = out_ref.shape[0] // 2
    for group, side in ((refs[:count], side_ref[0]), (refs[count : 2 * count], 1 - side_ref[0])):
        offset = 0
        for ref in group:
            rows = ref.shape[0]
            start = pl.multiple_of(side * half + offset, LANES)
            out_ref[pl.ds(start, rows), :] = ref[...].astype(single)
            offset += rows


def place_halves(side, own, other):
    total = sum(part.shape[0] for part in own) * 2
    return pl.pallas_call(
        functools.partial(place_halves_kernel, len(own)),
        in_specs=[pl.BlockSpec(memory_space=pltpu.SMEM)] + [VMEM] * (2 * len(own)),
        out_specs=VMEM,
        out_shape=jax.ShapeDtypeStruct((total, own[0].shape[1]), single),
        compiler_params=pltpu.CompilerParams(vmem_limit_bytes=8 * 1024 * 1024),
        cost_estimate=BRIEF,
        name="place_halves",
    )(side, *own, *other)


def lane_blocks(value, count, index):
    span = value.shape[1] // count
    return jnp.concatenate(
        [value[:, (p ^ (1 << index)) * span : ((p ^ (1 << index)) + 1) * span] for p in range(count)], 1
    )


def merge_stats_kernel(count, index, own_ref, other_ref, out_ref):
    own, other = own_ref[...], lane_blocks(other_ref[...], count, index)
    high = jnp.maximum(own[0:1], other[0:1])
    sums = own[1:2] * jnp.exp(own[0:1] - high) + other[1:2] * jnp.exp(other[0:1] - high)
    out_ref[...] = jnp.concatenate([high, sums, own[2:3] + other[2:3], own[3:]], 0)


def merge_stats(own, other, count, index):
    return run_whole(
        functools.partial(merge_stats_kernel, count, index), "merge_stats", [(own.shape, single)], own, other
    )[0]


def row_norms_kernel(count, slots, own_ref, out_ref):
    own = own_ref[...]
    norm = own[0:1] + jnp.log(own[1:2])
    parts = own[2:3] - norm
    span = parts.shape[1] // count
    parts = [parts[:, p * span : (p + 1) * span] for p in range(count)]
    while len(parts) > 1:
        parts = [parts[p] + parts[p + 1] for p in range(0, len(parts), 2)]
    lanes = lax.broadcasted_iota(jnp.int32, parts[0].shape, 1)
    places = lax.broadcasted_iota(jnp.int32, norm.shape, 1)
    likelihood = jnp.zeros_like(norm)
    for slot in range(slots):
        total = jnp.sum(jnp.where(lanes // (span // slots) == slot, parts[0], 0.0), -1, keepdims=True)
        likelihood = jnp.where(places == slot, total, likelihood)
    out_ref[...] = jnp.concatenate([norm, likelihood, own[2:]], 0)


def row_norms(own, count, slots):
    return run_whole(
        functools.partial(row_norms_kernel, count, slots), "row_norms", [(own.shape, single)], own
    )[0]


def as_columns(rows):
    return jnp.swapaxes(
        jnp.concatenate([rows, jnp.zeros((LANES - rows.shape[0], rows.shape[1]), single)], 0), 0, 1
    )


def vocab_part_kernel(
    place_ref, norm_ref, merged_ref, local_ref, label_rows_ref, label_ref, mixed_ref, sent_ref, kept_ref
):
    norm = norm_ref[0:1, :]
    surplus = 1.0 - jnp.exp(merged_ref[2:3, :] - norm)
    share = jnp.exp(local_ref[0:1, :] - norm)
    columns = as_columns(jnp.concatenate([surplus, share] + [norm] * 6, 0))
    label = label_ref[:, 0:1]
    inside = (label >= 0) & (label < place_ref[3])
    part = (
        jnp.where(inside, columns[:, 0:1], 0.0) * label_rows_ref[...].astype(single)
        - columns[:, 1:2] * mixed_ref[...]
    )
    half = kept_ref.shape[0]
    kept_ref[...] = part[:half]
    sent_ref[...] = part[half:].astype(bfloat)


def vocab_part(place, norm, merged, local, label_rows, label, mixed):
    rows, width = mixed.shape
    return pl.pallas_call(
        vocab_part_kernel,
        in_specs=[pl.BlockSpec(memory_space=pltpu.SMEM)] + [VMEM] * 6,
        out_specs=[VMEM] * 2,
        out_shape=[
            jax.ShapeDtypeStruct((rows // 2, width), bfloat),
            jax.ShapeDtypeStruct((rows // 2, width), single),
        ],
        compiler_params=pltpu.CompilerParams(vmem_limit_bytes=16 * 1024 * 1024),
        cost_estimate=BRIEF,
        name="vocab_part",
    )(place, norm, merged, local, label_rows, label, mixed)


def vocab_scale_kernel(
    slots, delta_ref, place_ref, norm_ref, merged_ref, far_ref, tops_ref, factor_ref, column_ref
):
    norm = norm_ref[0:1, :]
    lanes = lax.broadcasted_iota(jnp.int32, norm.shape, 1)
    quarter = norm.shape[1] // slots // place_ref[2]
    slot_of = lax.rem(lanes // quarter, slots)
    scale, far_scale = jnp.zeros_like(norm), jnp.zeros_like(norm)
    for slot in range(slots):
        scale = jnp.where(slot_of == slot, delta_ref[place_ref[0] + slot], scale)
        far_scale = jnp.where(slot_of == slot, delta_ref[place_ref[1] + slot], far_scale)
    surplus = scale * (1.0 - jnp.exp(merged_ref[2:3, :] - norm))
    columns = as_columns(
        jnp.concatenate([surplus, norm, scale, norm, far_ref[0:1, :], far_scale, norm, norm], 0)
    )
    column_ref[...] = columns
    factor_ref[...] = -columns[:, 2:3] * jnp.exp(tops_ref[...] - columns[:, 1:2])


def vocab_scale(delta, place, norm, merged, far, tops, slots):
    smem = pl.BlockSpec(memory_space=pltpu.SMEM)
    return pl.pallas_call(
        functools.partial(vocab_scale_kernel, slots),
        in_specs=[smem, smem] + [VMEM] * 4,
        out_specs=[VMEM] * 2,
        out_shape=[jax.ShapeDtypeStruct(tops.shape, single)] * 2,
        compiler_params=pltpu.CompilerParams(vmem_limit_bytes=12 * 1024 * 1024),
        cost_estimate=BRIEF,
        name="vocab_scale",
    )(delta, place, norm, merged, far, tops)


def scaled_backward_kernel(slots, delta_ref, place_ref, kept_ref, arrived_ref, *refs):
    shape = kept_ref.shape
    slot_of = lax.broadcasted_iota(jnp.int32, (shape[0], LANES), 0) // (shape[0] // slots)
    scale = jnp.zeros(slot_of.shape, single)
    for slot in range(slots):
        scale = jnp.where(slot_of == slot, delta_ref[place_ref[0] + slot], scale)
    upstream = (kept_ref[...].astype(single) + arrived_ref[...].astype(single)) * scale[:, :1]
    norm_backward_rows(upstream, *refs)


def scaled_backward(delta, place, kept, arrived, hidden, gain, slots):
    shape = hidden.shape
    smem = pl.BlockSpec(memory_space=pltpu.SMEM)
    return pl.pallas_call(
        functools.partial(scaled_backward_kernel, slots),
        in_specs=[smem, smem] + [VMEM] * 4,
        out_specs=[VMEM] * 3,
        out_shape=[
            jax.ShapeDtypeStruct(shape, single),
            jax.ShapeDtypeStruct(shape, bfloat),
            jax.ShapeDtypeStruct((3, shape[1]), single),
        ],
        compiler_params=pltpu.CompilerParams(vmem_limit_bytes=12 * 1024 * 1024),
        cost_estimate=BRIEF,
        name="norm_backward",
    )(delta, place, kept.reshape(shape), arrived.reshape(shape), hidden, row(gain))


def marginal_objective(seq_values, doc_scores, member, length):
    joint = doc_scores + seq_values / length
    masked = jnp.where(member, joint[None, :], -1e30)
    top = jnp.max(masked, 1, keepdims=True)
    unscaled = jnp.where(member, jnp.exp(masked - top), 0.0)
    total = jnp.sum(unscaled, 1, keepdims=True)
    marginal = top[:, 0] + jnp.log(total[:, 0])
    posterior = unscaled / total
    entropy = -jnp.sum(jnp.where(member, posterior * (joint[None, :] - marginal[:, None]), 0.0), 1)
    return jnp.mean(-marginal + ENTROPY_WEIGHT * entropy)


def on_device(
    dp,
    mp,
    targets,
    labels,
    passages,
    slot_question,
    slot_passage,
    score_table,
    score_index,
    query_weight,
    query_bias,
    key_weight,
    value_weight,
    value_bias,
    output_weight,
    output_bias,
    first_gain,
    first_shift,
    probe_weight,
    probe_bias,
    address_weight,
    content_weight,
    content_bias,
    merged_weight,
    merged_bias,
    second_gain,
    second_shift,
    expand_weight,
    expand_bias,
    shrink_weight,
    shrink_bias,
    third_gain,
    third_shift,
    embedding,
):
    group = lax.axis_index("dp")
    member_index = lax.axis_index("mp")
    own_questions, length, width = targets.shape
    questions = own_questions * dp
    pair_count = slot_passage.shape[0]
    store_count, passage_length = (passages.shape[0], passages.shape[1])
    vocab_share = embedding.shape[0]
    local_width = query_weight.shape[1]
    quarter = length // mp
    assert own_questions == 1

    token = [score_table]

    free = [False]

    def through(*values):
        if not free[0]:
            values = tie(*values, token[0])
            token[0] = values[-1]
            values = values[:-1]
        return values if len(values) > 1 else values[0]

    mp_order = bits_of(mp)[::-1]
    mp_table = relative_of(mp_order)
    dp_bits = bits_of(dp)
    dp_order = dp_bits[::-1]
    dp_table = relative_of(dp_order)
    fast = dp >= 4 and width % (dp * LANES) == 0
    far = dp_bits[-1]

    def to_own(rows, count):
        natural = rows.reshape((count, mp, quarter) + rows.shape[2:])
        return jnp.moveaxis(xor_take(mp_table, member_index, natural, 1), 1, 0)

    def to_natural(rows, count):
        shaped = rows.reshape((mp, count, quarter) + rows.shape[1:])
        return jnp.moveaxis(natural_order(mp_table, member_index, shaped, 0), 0, 1)

    def mp_scatter_steps(halves):
        assert len(mp_order) == 2
        sent, kept = through(*halves)
        arrived = swap(sent, "mp", mp, mp_order[1])
        yield None
        sent, kept = through(*add_halves(kept, through(arrived)))
        arrived = swap(sent, "mp", mp, mp_order[0])
        yield None
        yield kept, through(arrived)

    def mp_gather_steps(own):
        own = through(own)
        held = [own, swap(own, "mp", mp, mp_order[0]), swap(own, "mp", mp, mp_order[1])]
        yield None
        held[1] = through(held[1])
        held.append(swap(held[1], "mp", mp, mp_order[1]))
        yield None
        yield through(*held)

    def dp_scatter_steps(halves, order):
        for bit in reversed(order):
            sent, kept = through(*halves)
            arrived = swap(sent, "dp", dp, bit)
            yield None
            if bit == order[0]:
                yield kept, through(arrived)
            else:
                halves = add_halves(kept, through(arrived))

    def last(steps):
        for value in steps:
            pass
        return value

    my_questions = lax.dynamic_slice_in_dim(slot_question, group * pair_count, pair_count)
    every = jnp.arange(own_questions, dtype=jnp.int32)
    quarters = member_index ^ jnp.asarray(mp_table, jnp.int32)
    place = (
        quarters[:, None] * quarter + jnp.arange(quarter, dtype=jnp.int32)[None, :]
    ).reshape(length)
    places_of = (
        jnp.broadcast_to(place[:, None], (length, LANES)),
        jnp.broadcast_to(place[None, :], (8, length)),
    )
    inputs = to_own(targets, own_questions)

    def by_question(rows):
        return jnp.moveaxis(rows.reshape(mp, own_questions, quarter, -1), 0, 1).reshape(
            own_questions, length, -1
        )

    inputs = inputs.reshape(-1, width)
    self_queries = by_question((matmul(inputs, query_weight) + query_bias).astype(bfloat))
    self_addresses = by_question(matmul(inputs, key_weight).astype(bfloat))
    self_contents = by_question((matmul(inputs, value_weight) + value_bias).astype(bfloat))
    self_flat = attend_forward(
        self_queries, self_addresses, self_contents, every, every, mp, places_of
    ).reshape(-1, local_width)
    kept, arrived = last(mp_scatter_steps(product_halves([self_flat], [output_weight])))
    first_in, first_norm, first_low = norm_forward(
        kept, arrived, inputs[:quarter], output_bias, first_gain, first_shift
    )
    first_full, probe_own = project(last(mp_gather_steps(first_low)), probe_weight, probe_bias)
    probe_own = by_question(probe_own)

    def where_slots(order):
        spots = jnp.asarray(places(relative_of(order)), jnp.int32)
        return spots[group ^ (my_questions // own_questions)] * own_questions + (
            my_questions % own_questions
        )

    probe_order = dp_bits[::-1]
    return_order = dp_bits[:1] + dp_bits[:0:-1]
    return_bins = where_slots(return_order)
    state_order = probe_order
    state_bins = where_slots(state_order)
    first_order = dp_bits[:1] + dp_bits[:0:-1]
    probe_bins = where_slots(probe_order)
    first_bins = where_slots(first_order)
    def label_index(slots):
        wanted = to_own(jnp.take(labels, slots, axis=0, mode="clip"), pair_count).reshape(-1)
        return wanted - member_index * vocab_share

    local_index = label_index(my_questions)
    inside = (local_index >= 0) & (local_index < vocab_share)
    label_places = jnp.clip(local_index, 0, vocab_share - 1)
    gather = gather_both_steps(
        (probe_own, first_low.reshape(own_questions, quarter, width)),
        "dp",
        dp,
        (probe_order, first_order),
    )
    for step in range(len(dp_bits)):
        next(gather)
    label_rows = through(jnp.take(embedding, through(label_places), axis=0, mode="clip"))
    probe_all, first_all = next(gather)
    probe_all = probe_all.reshape(questions, length, local_width)
    first_all = first_all.reshape(questions, quarter, width)
    passage_rows = passages.reshape(-1, width)
    stored_addresses = matmul(passage_rows, address_weight).astype(bfloat)
    stored_contents = (matmul(passage_rows, content_weight) + content_bias).astype(bfloat)
    stored_addresses = stored_addresses.reshape(store_count, passage_length, local_width)
    stored_contents = stored_contents.reshape(store_count, passage_length, local_width)

    cross_flat = attend_forward(
        probe_all, stored_addresses, stored_contents, probe_bins, slot_passage, mp
    ).reshape(-1, local_width)
    first_slots = pick(first_all, first_bins).reshape(-1, width)
    kept, arrived = last(mp_scatter_steps(product_halves([cross_flat], [merged_weight])))
    second_in, second_norm, low = norm_forward(
        kept, arrived, first_slots, merged_bias, second_gain, second_shift
    )
    second_low, expanded, activated, sent, kept = feed_forward(
        last(mp_gather_steps(low)), expand_weight, expand_bias, shrink_weight
    )
    kept, arrived = last(mp_scatter_steps((sent, kept)))
    third_in, third_norm, low = norm_forward(
        kept, arrived, second_norm, shrink_bias, third_gain, third_shift
    )
    def order_table(order):
        if not fast:
            return jnp.arange(width // LANES, dtype=jnp.int32)
        return group ^ jnp.asarray(relative_of(order), jnp.int32)

    order_a = dp_bits[::-1]
    order_b = order_a if dp < 4 else [dp_bits[-1], dp_bits[0]] + dp_bits[1:-1]
    third_pieces = last(mp_gather_steps(low))
    third_low, third_moved = order_columns(third_pieces, order_table(order_a))
    far_pieces = [swap(piece, "dp", dp, far) for piece in third_pieces[: mp // 2]]

    def label_lanes(index):
        return jnp.broadcast_to(index[:, None], (index.shape[0], LANES))

    own_labels = label_lanes(local_index)
    third_low = through(third_low)
    entry_weights, entry_mix, entry_tops, local_stats = vocab_forward(
        third_low, embedding, own_labels, label_rows
    )
    local_stats, *far_pieces = through(local_stats, *far_pieces)
    entry_tile = vocab_tile(vocab_share)
    stats = local_stats
    for index, bit in reversed(list(enumerate(mp_order))):
        stats = merge_stats(stats, through(swap(stats, "mp", mp, bit)), mp, index)
    norms = through(row_norms(stats, mp, pair_count))
    far_norms = swap(norms, "dp", dp, far)
    far_group = group ^ far
    place = jnp.stack([group * pair_count, far_group * pair_count, mp, vocab_share]).astype(jnp.int32)
    sent, kept = vocab_part(place, norms, stats, local_stats, label_rows, own_labels, entry_mix)
    steps = mp_scatter_steps((sent, kept))
    next(steps)
    far_norms = through(far_norms)
    every_likelihood = jnp.stack([norms[1, :pair_count], far_norms[1, :pair_count]])
    arrived = swap(every_likelihood, "dp", dp, dp_order[1])
    next(steps)
    for bit in dp_order[2:]:
        every_likelihood = jnp.concatenate([every_likelihood, through(arrived)], 0)
        arrived = swap(every_likelihood, "dp", dp, bit)
    far_pieces += [swap(piece, "mp", mp, mp_order[-1]) for piece in far_pieces]
    every_likelihood = jnp.concatenate([every_likelihood, through(arrived)], 0)
    every_likelihood = natural_order(dp_table, group, every_likelihood, 0).reshape(-1)
    doc_scores = jnp.take(token[0], score_index)
    member = slot_question[None, :] == jnp.arange(questions, dtype=jnp.int32)[:, None]

    def scored(values_all):
        return marginal_objective(values_all, doc_scores, member, length)

    objective, pullback = jax.vjp(scored, every_likelihood)
    likelihood_delta = pullback(jnp.ones_like(objective) * (questions * length))[0]
    far_labels = label_lanes(
        label_index(lax.dynamic_slice_in_dim(slot_question, far_group * pair_count, pair_count))
    )
    factors, values = vocab_scale(
        likelihood_delta, place, norms, stats, far_norms, entry_tops, pair_count
    )
    far_third, far_moved = order_columns(through(*far_pieces), order_table(order_a))

    objective = through(objective)

    class ColumnSum:
        def __init__(self, halves, order):
            self.sent, self.kept = through(*halves)
            self.bits = order[::-1]
            self.arrived = None

        def send(self):
            if fast:
                self.sent = through(self.sent)
                self.arrived = swap(self.sent, "dp", dp, self.bits[0])
                self.bits = self.bits[1:]

        def add(self):
            if fast:
                self.arrived, self.kept = through(self.arrived, self.kept)
                self.sent, self.kept = add_columns(self.kept, self.arrived)

        def step(self):
            self.add()
            self.send()

        def wait(self):
            if fast:
                self.arrived = through(self.arrived)

    def finish(parts):
        if not fast:
            slopes = [
                lax.psum_scatter(
                    jnp.concatenate([part.kept, part.sent], 1), "dp", scatter_dimension=1, tiled=True
                )
                for part in parts
            ]
            return jnp.concatenate(slopes, 0).astype(single)
        assert not any(part.bits for part in parts)
        return finish_sums([part.kept for part in parts], [part.arrived for part in parts])

    slope_tile = entry_tile // 2 if entry_tile % (2 * LANES) == 0 else entry_tile
    side = (group // far).astype(jnp.int32).reshape(1)
    tiles = vocab_share // slope_tile // 2 if fast else vocab_share // slope_tile
    cuts = [-(-tiles * i // 7) for i in CUTS]

    def table_sum(index):
        first, count = cuts[index], cuts[index + 1] - cuts[index]
        if fast:
            halves = half_slope(
                side * tiles,
                entry_weights,
                embedding,
                through(factors),
                own_labels,
                values,
                far_third,
                far_labels,
                third_moved,
                far_moved,
                first,
                count,
                slope_tile,
            )
        else:
            halves = vocab_slope(
                entry_weights,
                through(factors),
                own_labels,
                values,
                third_low,
                order_table(order_a),
                first,
                count,
                slope_tile,
            )
        return ColumnSum(halves, order_a)

    def group_sum(pairs, order):
        pairs = [(through(pairs[0][0]), pairs[0][1])] + pairs[1:]
        return ColumnSum(slope_group(pairs, order_table(order)), order)

    sums = {}
    makers = {
        "a": lambda: table_sum(0),
        "b": lambda: table_sum(1),
        "c": lambda: table_sum(2),
        "f": lambda: group_sum(
            [(activated, feed_delta), (expanded_delta, second_low)], orders[ORDERS["f"]]
        ),
        "p": lambda: group_sum(
            [
                (cross_flat, recall_delta),
                (address_delta, passage_rows),
                (content_delta, passage_rows),
                (probe_flat, first_full),
                (self_flat, self_delta),
            ],
            orders[ORDERS["p"]],
        ),
        "s": lambda: group_sum(
            [
                (query_flat, inputs),
                (key_flat, inputs),
                (value_flat, inputs),
                (jnp.eye(16, dtype=bfloat), vectors.astype(bfloat)),
            ],
            orders[ORDERS["s"]],
        ),
    }
    orders = {"y": order_a, "z": order_b}

    def at(point):
        free[0] = free[0] or point >= FREE
        for name, action in PLAN[point]:
            if name == "t":
                next(state_steps)
            elif action == "make":
                sums[name] = makers[name]()
            else:
                getattr(sums[name], action)()

    at(0)
    at(1)
    kept, arrived = next(steps)
    third_back, feed_low, third_sums = scaled_backward(
        likelihood_delta, place, kept, arrived, third_in, third_gain, pair_count
    )
    steps = mp_gather_steps(feed_low)
    next(steps)
    at(2)
    next(steps)
    at(3)
    feed_delta, expanded_delta, bias_expand, sent, kept = feed_backward(
        next(steps), expand_weight, shrink_weight, expanded
    )
    steps = mp_scatter_steps((sent, kept))
    next(steps)
    at(4)
    next(steps)
    at(5)
    parts = next(steps)
    at(6)
    second_back, recall_low, second_sums = norm_backward(
        parts + (third_back,), second_in, second_gain
    )
    steps = mp_gather_steps(recall_low)
    next(steps)
    state_steps = dp_scatter_steps(
        tuple(
            value.reshape(-1, width)
            for value in bin_rows(
                second_back.reshape(pair_count, quarter, width), state_bins, questions
            )
        ),
        state_order,
    )
    at(7)
    next(steps)
    at(8)
    recall_delta, mixed_delta = project(
        next(steps), merged_weight, jnp.zeros((local_width,), single), True
    )
    probe_binned, address_delta, content_delta = attend_backward(
        probe_all,
        stored_addresses,
        stored_contents,
        mixed_delta.reshape(mp, pair_count, quarter, local_width),
        probe_bins,
        slot_passage,
        return_bins,
    )
    address_delta = address_delta.reshape(-1, local_width)
    content_delta = content_delta.reshape(-1, local_width)

    half = questions // 2
    steps = dp_scatter_steps(
        (
            probe_binned[half:].reshape(-1, local_width),
            probe_binned[:half].reshape(-1, local_width),
        ),
        return_order,
    )
    at(9)
    next(steps)
    at(10)
    for unused in range(len(dp_bits) - 2):
        next(steps)
    at(11)
    next(steps)
    at(12)
    probe_parts = next(steps)
    at(13)
    probe_flat = (
        probe_parts[0] + probe_parts[1].astype(single)
    ).astype(bfloat)

    bias_content = jnp.sum(content_delta, 0, dtype=single)
    passages_slope = lax.psum(
        (outer_rows(address_delta, address_weight) + outer_rows(content_delta, content_weight)).astype(bfloat),
        "mp",
    ).astype(single).reshape(passages.shape)

    bias_probe = jnp.sum(probe_flat, 0, dtype=single)
    steps = mp_scatter_steps(product_halves([probe_flat], [probe_weight], True))
    next(steps)
    at(14)
    next(steps)
    at(15)
    state_parts = last(state_steps)
    first_back, self_low, first_sums = norm_backward(
        next(steps) + tuple(state_parts), first_in, first_gain
    )
    steps = mp_gather_steps(self_low)
    next(steps)
    at(16)
    next(steps)
    at(17)
    self_delta, self_mixed_delta = project(
        next(steps), output_weight, jnp.zeros((local_width,), single), True
    )
    self_deltas = attend_backward(
        self_queries,
        self_addresses,
        self_contents,
        self_mixed_delta.reshape(mp, own_questions, quarter, local_width),
        every,
        every,
        every,
        places_of,
    )
    query_flat, key_flat, value_flat = (
        jnp.moveaxis(delta.reshape(own_questions, mp, quarter, local_width), 1, 0).reshape(
            -1, local_width
        )
        for delta in self_deltas
    )
    steps = mp_scatter_steps(
        product_halves(
            [query_flat, key_flat, value_flat], [query_weight, key_weight, value_weight], True
        )
    )
    shared = total_over(
        jnp.concatenate([first_sums, second_sums, third_sums], 0), "mp", mp, mp_order
    )
    bias_query = jnp.sum(query_flat, 0, dtype=single)
    bias_value = jnp.sum(value_flat, 0, dtype=single)
    quads = jnp.stack([bias_query, bias_value, bias_probe, bias_content])
    quads = quads.reshape(4, dp, local_width // dp).swapaxes(0, 1).reshape(1, width)
    vectors = jnp.concatenate([shared, bias_expand, quads, jnp.zeros((5, width), single)], 0)
    next(steps)
    at(18)
    next(steps)
    at(19)
    kept, arrived = next(steps)
    input_low = (kept + arrived.astype(single) + first_back).astype(bfloat)
    steps = mp_gather_steps(input_low)
    next(steps)
    at(20)
    next(steps)
    at(21)
    targets_slope = to_natural(jnp.concatenate(next(steps), 0), own_questions)
    targets_slope = targets_slope.reshape(targets.shape).astype(single)
    at(22)
    table_parts = [sums[name] for name in "abc"]
    if fast:
        embedding_slope = place_halves(
            side, [part.kept for part in table_parts], [part.arrived for part in table_parts]
        )
    else:
        embedding_slope = finish(table_parts)
    feed_slopes = finish([sums["f"]])
    probe_slopes = finish([sums["p"]])
    self_slopes = finish([sums["s"]])
    hidden = expanded.shape[1]

    def parts_of(slopes, counts):
        edges = [sum(counts[:i]) for i in range(len(counts) + 1)]
        return [slopes[a:b] for a, b in zip(edges, edges[1:])]

    shrink_slope, expand_slope = parts_of(feed_slopes, [hidden] * 2)
    merged_slope, address_slope, content_slope, probe_slope, output_slope = parts_of(
        probe_slopes, [local_width] * 5
    )
    query_slope, key_slope, value_slope, vectors = parts_of(self_slopes, [local_width] * 3 + [16])
    expand_slope, address_slope, content_slope = expand_slope.T, address_slope.T, content_slope.T
    probe_slope, query_slope, key_slope, value_slope = (
        slope.T for slope in (probe_slope, query_slope, key_slope, value_slope)
    )
    (
        bias_output,
        first_gain_slope,
        first_shift_slope,
        bias_merged,
        second_gain_slope,
        second_shift_slope,
        bias_shrink,
        third_gain_slope,
        third_shift_slope,
        bias_expand,
    ) = (vectors[i] for i in range(10))
    bias_query, bias_value, bias_probe, bias_content = vectors[10].reshape(4, local_width // dp)
    return (
        objective,
        targets_slope,
        passages_slope,
        query_slope,
        bias_query,
        key_slope,
        value_slope,
        bias_value,
        output_slope,
        bias_output,
        first_gain_slope,
        first_shift_slope,
        probe_slope,
        bias_probe,
        address_slope,
        content_slope,
        bias_content,
        merged_slope,
        bias_merged,
        second_gain_slope,
        second_shift_slope,
        expand_slope,
        bias_expand,
        shrink_slope,
        bias_shrink,
        third_gain_slope,
        third_shift_slope,
        embedding_slope,
    )


def solution(mesh):
    return jax.shard_map(
        functools.partial(on_device, mesh.shape["dp"], mesh.shape["mp"]),
        mesh=mesh,
        in_specs=(
            P("dp", None, None),
            P(),
            P("dp", None, None),
            P(),
            P("dp"),
            P(),
            P(),
            P(None, "mp"),
            P("mp"),
            P(None, "mp"),
            P(None, "mp"),
            P("mp"),
            P("mp", None),
            P(),
            P(),
            P(),
            P(None, "mp"),
            P("mp"),
            P(None, "mp"),
            P(None, "mp"),
            P("mp"),
            P("mp", None),
            P(),
            P(),
            P(),
            P(None, "mp"),
            P("mp"),
            P("mp", None),
            P(),
            P(),
            P(),
            P("mp", None),
        ),
        out_specs=(
            P(),
            P("dp", None, None),
            P("dp", None, None),
            P("dp", "mp"),
            P(("mp", "dp")),
            P("dp", "mp"),
            P("dp", "mp"),
            P(("mp", "dp")),
            P("mp", "dp"),
            P("dp"),
            P("dp"),
            P("dp"),
            P("dp", "mp"),
            P(("mp", "dp")),
            P("dp", "mp"),
            P("dp", "mp"),
            P(("mp", "dp")),
            P("mp", "dp"),
            P("dp"),
            P("dp"),
            P("dp"),
            P("dp", "mp"),
            P(("mp", "dp")),
            P("mp", "dp"),
            P("dp"),
            P("dp"),
            P("dp"),
            P("mp", "dp"),
        ),
        check_vma=False,
    )
```
